32 devices in a mesh: dp: 16 (over z, y, core), blk: 2 (over x).
Axes of the slice: x: 2, y: 2, z: 4, core: 2. Of those that a mesh axis runs over, the one named last changes fastest.
Arguments:
- tokens: bfloat16 [2048, 16, 1, 384], P('blk', 'dp'), may hold values from -6 to 6
- slot_kind: int32 [16, 1], P('dp'), may hold values from 0 to 1, as said below
- frame_lead: int32 [16, 1, 2], P('dp'), may hold values from 0 to 39
- norm1_gain: float32 [2, 384], replicated, may hold values from 0.5 to 1.5
- w_qkv: bfloat16 [2, 384, 1152], replicated, may hold values from -0.3125 to 0.3125
- w_out: bfloat16 [2, 384, 384], replicated, may hold values from -1.75 to 1.75
- norm2_gain: float32 [2, 384], replicated, may hold values from 0.5 to 1.5
- w_fc1: bfloat16 [2, 384, 1536], replicated, may hold values from -0.3125 to 0.3125
- b_fc1: float32 [2, 1536], replicated, may hold values from -3 to 3
- w_fc2: bfloat16 [2, 1536, 384], replicated, may hold values from -0.15625 to 0.15625
- lead_table: float32 [40, 384], replicated, may hold values from -3 to 3
- final_gain: float32 [384], replicated, may hold values from 0.5 to 1.5
- head_w: float32 [384, 3], replicated, may hold values from -0.3125 to 0.3125
- head_b: float32 [3], replicated, may hold values from -1.5 to 1.5
- lead_prior: float32 [40, 3], replicated, may hold values from 0.2 to 0.5
- gate_cot: float32 [3, 2048, 16, 1], P(None, 'blk', 'dp'), may hold values from -6 to 6
Outputs:
- expert_weights: float32 [3, 2048, 16, 1], P(None, 'blk', 'dp')
- lead_average: float32 [40, 3], replicated
- token_grad: bfloat16 [2048, 16, 1, 384], P('blk', 'dp')
- norm1_gain_grad: float32 [2, 384], replicated
- qkv_grad: float32 [2, 384, 1152], replicated
- out_grad: float32 [2, 384, 384], replicated
- norm2_gain_grad: float32 [2, 384], replicated
- fc1_grad: float32 [2, 384, 1536], replicated
- fc1_bias_grad: float32 [2, 1536], replicated
- fc2_grad: float32 [2, 1536, 384], replicated
- lead_table_grad: float32 [40, 384], replicated
- final_gain_grad: float32 [384], replicated
- head_grad: float32 [384, 3], replicated
- head_bias_grad: float32 [3], replicated
The draws below stay inside these ranges and needn't reach their ends.
Inputs may be any that keep to these rules, and one draw needn't show every extreme that they name: `slot_kind`: 1 where a slot holds two coarse frames of 1024 patches (in each band, the first half of the rows belong to the first frame), 0 where it holds one fine frame; exactly 2 slots over all groups are 1. `frame_lead`: the second entry is unused in a slot of one fine frame.
All inputs are finite; a program needn't handle non-finite values.
Results may differ from the reference program's by a relative error of at most 0.013.
Values may be sent and summed in bfloat16 or wider, within the bound.
A program may use at most 192 MiB of HBM per device.

```python
import math
import jax
import jax.numpy as jnp
from jax import lax

D = 384
HEADS = 6
HEAD_DIM = 64
FF = 1536
LEADS = 40
EXPERTS = 3
LAYERS = 2
FINE_LEN = 2048
SLOTS = 1
GROUPS = 16
BAND = 1024
COARSE = 2


def draw_slot_kind(key, part):
    key = jax.random.fold_in(key, 7)
    order = jax.random.permutation(key, GROUPS * SLOTS)
    return (order < COARSE).astype(jnp.int32).reshape(GROUPS, SLOTS)


def set_ends(values, rng, least, largest):
    dims = values.shape
    index_at = [jax.random.randint(jax.random.fold_in(rng, axis), (), 0, dims[axis]) for axis in range(len(dims))]
    values = values.at[tuple(index_at)].set(least)
    longest = dims.index(max(dims))
    index_at[longest] = (index_at[longest] + 1) % dims[longest]
    return values.at[tuple(index_at)].set(largest)


def level_of(own_key, dims, split, smallest, top_value):
    def one(position, parts):
        draws = jax.random.uniform(jax.random.fold_in(jax.random.fold_in(own_key, 6), position), (parts,), jnp.float32, smallest / len(split), top_value / len(split))
        return jnp.repeat(jnp.exp(draws), dims[position] // parts).reshape((-1,) + (1,) * (len(dims) - position - 1))

    loudness = one(*split[0])
    for cut in split[1:]:
        loudness = loudness * one(*cut)
    return loudness


def bell_draw(rng, dims, spread, limit, pieces=(), held_as=jnp.bfloat16):
    factor_of = level_of(rng, dims, pieces, -0.22, 0.18) if pieces else 1.0
    result = jax.random.normal(rng, dims, jnp.float32) * spread * factor_of
    return jnp.minimum(jnp.maximum(result, -limit), limit).astype(held_as)


def setup_inputs(seed: int = 0) -> dict:
    streams_of = jax.random.split(jax.random.key(seed), 17)
    return {
        "tokens": bell_draw(streams_of[0], (FINE_LEN, GROUPS, SLOTS, D), 1.0, 6.0, ((0, 2), (1, 16))),
        "slot_kind": draw_slot_kind(jax.random.fold_in(streams_of[16], 71), 0),
        "frame_lead": set_ends(jax.random.randint(streams_of[2], (GROUPS, SLOTS, 2), 0, LEADS), jax.random.fold_in(streams_of[2], 1), 0, LEADS - 1).astype(jnp.int32),
        "norm1_gain": jnp.clip(jax.random.uniform(streams_of[3], (LAYERS, D), jnp.float32, 0.5, 1.5), 0.5, 1.5),
        "w_qkv": bell_draw(streams_of[4], (LAYERS, D, 3 * D), D ** -0.5, 0.3125),
        "w_out": bell_draw(streams_of[5], (LAYERS, D, D), (max(D // 32, 1)) ** -0.5, 1.75),
        "norm2_gain": jnp.clip(jax.random.uniform(streams_of[6], (LAYERS, D), jnp.float32, 0.5, 1.5), 0.5, 1.5),
        "w_fc1": bell_draw(streams_of[7], (LAYERS, D, FF), D ** -0.5, 0.3125),
        "b_fc1": bell_draw(streams_of[8], (LAYERS, FF), 0.5, 3.0, (), jnp.float32),
        "w_fc2": bell_draw(streams_of[9], (LAYERS, FF, D), FF ** -0.5, 0.15625),
        "lead_table": bell_draw(streams_of[10], (LEADS, D), 0.5, 3.0, (), jnp.float32),
        "final_gain": jnp.clip(jax.random.uniform(streams_of[11], (D,), jnp.float32, 0.5, 1.5), 0.5, 1.5),
        "head_w": bell_draw(streams_of[12], (D, EXPERTS), D ** -0.5, 0.3125, (), jnp.float32),
        "head_b": bell_draw(streams_of[13], (EXPERTS,), 0.3, 1.5, (), jnp.float32),
        "lead_prior": jnp.clip(jnp.exp(jax.random.uniform(streams_of[14], (LEADS, EXPERTS), jnp.float32, math.log(0.2), math.log(0.5))), 0.2, 0.5),
        "gate_cot": bell_draw(streams_of[15], (EXPERTS, FINE_LEN, GROUPS, SLOTS), 1.0, 6.0, ((1, 2), (2, 16)), jnp.float32),
    }


masked_score = -1e+30
norm_eps = 1e-06

@jax.custom_vjp
def low(v):
    return lax.optimization_barrier(v.astype(jnp.bfloat16)).astype(jnp.float32)

@jax.custom_vjp
def low_back(v):
    return v

def low_keep(v):
    return (low(v), None)

def low_pass(kept, grad):
    return (grad,)

def back_keep(v):
    return (v, None)

def back_low(kept, grad):
    return (low(grad),)
low.defvjp(low_keep, low_pass)
low_back.defvjp(back_keep, back_low)

def product(left_side, right_side):
    return jnp.dot(left_side, right_side, precision=lax.Precision.HIGHEST, preferred_element_type=jnp.float32)

def layer_norm(hidden, gain_row):
    centered = hidden - lax.optimization_barrier(jnp.mean(hidden, axis=-1, keepdims=True))
    variance = lax.optimization_barrier(jnp.mean(centered * centered, axis=-1, keepdims=True))
    return centered * lax.rsqrt(variance + norm_eps) * gain_row

def slot_frames(slot_kind_one):
    positions = jnp.arange(FINE_LEN, dtype=jnp.int32)
    upper_half = (positions % BAND >= BAND // 2).astype(jnp.int32)
    return slot_kind_one * upper_half

def lead_onehot(slot_kind_one, lead_pair):
    frame_rows = slot_frames(slot_kind_one)
    lead_rows = jnp.where(frame_rows == 1, lead_pair[1], lead_pair[0])
    return (lead_rows[:, None] == jnp.arange(LEADS, dtype=jnp.int32)[None, :]).astype(jnp.float32)

def slot_forward(params, hidden, slot_kind_one, lead_pair, log_prior):
    norm1_gain, w_qkv, w_out, norm2_gain, w_fc1, b_fc1, w_fc2, lead_table, final_gain, head_w, head_b = params
    frame_rows = slot_frames(slot_kind_one)
    same_frame = frame_rows[:, None] == frame_rows[None, :]
    lead_hot = lead_onehot(slot_kind_one, lead_pair)
    hidden = hidden + product(lead_hot, lead_table)
    score_scale = HEAD_DIM ** (-0.5)
    for layer_idx in range(LAYERS):
        normed = low(layer_norm(hidden, norm1_gain[layer_idx]))
        qkv_rows = low(low_back(product(normed, w_qkv[layer_idx])))
        query_rows = qkv_rows[:, :D].reshape(FINE_LEN, HEADS, HEAD_DIM)
        key_rows = qkv_rows[:, D:2 * D].reshape(FINE_LEN, HEADS, HEAD_DIM)
        value_rows = qkv_rows[:, 2 * D:].reshape(FINE_LEN, HEADS, HEAD_DIM)
        scores = jnp.einsum('qhe,khe->hqk', query_rows, key_rows, precision=lax.Precision.HIGHEST) * score_scale
        scores = low_back(jnp.where(same_frame[None], scores, masked_score))
        highest = lax.optimization_barrier(jnp.max(scores, axis=-1, keepdims=True))
        exp_scores = jnp.exp(scores - highest)
        prob_rows = exp_scores / lax.optimization_barrier(jnp.sum(exp_scores, axis=-1, keepdims=True))
        attended = jnp.einsum('hqk,khe->qhe', low(prob_rows), value_rows, precision=lax.Precision.HIGHEST)
        mixed_rows = low(low_back(attended.reshape(FINE_LEN, D)))
        hidden = hidden + low_back(product(mixed_rows, w_out[layer_idx]))
        normed_mid = low(layer_norm(hidden, norm2_gain[layer_idx]))
        pre_gelu = low_back(product(normed_mid, w_fc1[layer_idx]) + b_fc1[layer_idx])
        gelu_rows = low(jax.nn.gelu(pre_gelu))
        hidden = hidden + low_back(product(gelu_rows, w_fc2[layer_idx]))
    normed_last = layer_norm(hidden, final_gain)
    logits = product(normed_last, head_w) + head_b - product(lead_hot, log_prior)
    logits = logits - lax.optimization_barrier(jnp.max(logits, axis=-1, keepdims=True))
    exp_logits = jnp.exp(logits)
    expert_rows = exp_logits / lax.optimization_barrier(jnp.sum(exp_logits, axis=-1, keepdims=True))
    lead_totals = jnp.einsum('rl,re->le', lead_hot, expert_rows, precision=lax.Precision.HIGHEST)
    lead_counts = lax.optimization_barrier(jnp.sum(lead_hot, axis=0))
    return (expert_rows, (lead_totals, lead_counts))

def reference(tokens, slot_kind, frame_lead, norm1_gain, w_qkv, w_out, norm2_gain, w_fc1, b_fc1, w_fc2, lead_table, final_gain, head_w, head_b, lead_prior, gate_cot):
    params = tuple((array.astype(jnp.float32) for array in (norm1_gain, w_qkv, w_out, norm2_gain, w_fc1, b_fc1, w_fc2, lead_table, final_gain, head_w, head_b)))
    log_prior = jnp.log(lead_prior)
    slot_rows = jnp.transpose(tokens.astype(jnp.float32), (1, 2, 0, 3)).reshape(GROUPS * SLOTS, FINE_LEN, D)
    slot_kinds = slot_kind.reshape(GROUPS * SLOTS)
    lead_pairs = frame_lead.reshape(GROUPS * SLOTS, 2)

    def forward(params_in, rows_in):

        def slot_fn(inputs):
            rows_one, kind_one, pair_one = inputs
            return slot_forward(params_in, rows_one, kind_one, pair_one, log_prior)
        return lax.map(jax.checkpoint(slot_fn), (rows_in, slot_kinds, lead_pairs))
    expert_rows, pullback, lead_parts = jax.vjp(forward, params, slot_rows, has_aux=True)
    cotangent = jnp.transpose(gate_cot, (2, 3, 1, 0)).reshape(GROUPS * SLOTS, FINE_LEN, EXPERTS)
    param_grads, row_grads = pullback(cotangent)
    lead_totals = lax.optimization_barrier(jnp.sum(lead_parts[0], axis=0))
    lead_counts = lax.optimization_barrier(jnp.sum(lead_parts[1], axis=0))
    lead_average = 0.5 * lead_prior + 0.5 * lead_totals / jnp.maximum(lead_counts, 1.0)[:, None]
    expert_weights = jnp.transpose(expert_rows.reshape(GROUPS, SLOTS, FINE_LEN, EXPERTS), (3, 2, 0, 1))
    token_grad = jnp.transpose(row_grads.reshape(GROUPS, SLOTS, FINE_LEN, D), (2, 0, 1, 3)).astype(jnp.bfloat16)
    return (expert_weights, lead_average, token_grad, param_grads[0], param_grads[1], param_grads[2], param_grads[3], param_grads[4], param_grads[5], param_grads[6], param_grads[7], param_grads[8], param_grads[9], param_grads[10])
```

```python
import functools
import math

import jax
import jax.numpy as jnp
from jax import lax
from jax.experimental import pallas as pl
from jax.experimental.pallas import tpu as pltpu
from jax.sharding import PartitionSpec as P

HEAD_DIM = 64
LEADS = 40
LAYERS = 2
EXPERTS = 3
LANES = 128
norm_eps = 1e-06
gelu_in = math.sqrt(2.0 / math.pi)
gelu_cubic = 0.044715
MESH = pl.DeviceIdType.MESH
HIGHEST = lax.Precision.HIGHEST
F32 = jnp.float32
BF16 = jnp.bfloat16
VMEM = pl.BlockSpec(memory_space=pltpu.VMEM)
ANY = pl.BlockSpec(memory_space=pl.ANY)

KIND_ROW, LEAD_ROW = 3, 4
ROW_NORM1, ROW_MLP, ROW_HEAD, SMALL_ROWS = 40, 56, 72, 96


def pick(layer, array):
    return pl.BlockSpec((None,) + array.shape[1:], lambda *_: (layer, 0, 0))


def params(collective_id=None):
    if collective_id is None:
        return pltpu.CompilerParams(vmem_limit_bytes=60 * 2**20)
    return pltpu.CompilerParams(
        vmem_limit_bytes=60 * 2**20, collective_id=collective_id, has_side_effects=True
    )


def dot(a, b, dims=(1, 0), precision=None):
    return lax.dot_general(
        a, b, (((dims[0],), (dims[1],)), ((), ())), precision=precision, preferred_element_type=F32
    )


def normalize(x):
    centered = x - jnp.mean(x, axis=-1, keepdims=True)
    rstd = lax.rsqrt(jnp.mean(centered * centered, axis=-1, keepdims=True) + norm_eps)
    return centered * rstd, rstd


def normalize_back(dg, xhat, rstd):
    return (
        dg - jnp.mean(dg, axis=-1, keepdims=True) - xhat * jnp.mean(dg * xhat, axis=-1, keepdims=True)
    ) * rstd


def column_sum(x):
    return jnp.sum(x, axis=0, keepdims=True)


class Place:
    def __init__(self, n):
        self.n = n
        dp, self.b = lax.axis_index("dp"), lax.axis_index("blk")
        self.core, self.e = lax.rem(dp, 2), lax.div(dp, 2)
        half = n // 2
        self.side = lax.div(self.b, half)
        self.moves = self.core != self.side
        far = lax.rem(self.b + half, n)
        self.band = jnp.where(self.moves, far, self.b)
        self.partner = (self.e * 2 + 1 - self.core, far)

    def peer(self, step):
        half = self.n // 2
        band = lax.rem(self.band + step, self.n)
        near = lax.div(band, half) == self.side
        b = jnp.where(near, band, lax.rem(band + half, self.n))
        core = jnp.where(near, self.side, 1 - self.side)
        return (self.e * 2 + core, b)


def signal(sem, device):
    pl.semaphore_signal(sem, inc=1, device_id=device, device_id_type=MESH)


def send(src, dst, ssem, rsem, device):
    return pltpu.make_async_remote_copy(
        src_ref=src, dst_ref=dst, send_sem=ssem, recv_sem=rsem, device_id=device, device_id_type=MESH
    )


def row_step(rows):
    step = 16
    while step * 2 <= 128 and rows % (step * 2) == 0:
        step *= 2
    return step


def add_rows(out, out_at, sources, rows):
    step = row_step(rows)

    def body(i, carry):
        total = 0.0
        for ref, at in sources:
            total = total + ref[pl.ds(pl.multiple_of(at + i * step, 16), step), :].astype(F32)
        out[pl.ds(pl.multiple_of(out_at + i * step, 16), step), :] = total.astype(BF16)
        return carry

    lax.fori_loop(0, rows // step, body, 0)


def sum_sizes(n, chips):
    return [2, n, chips // 4, 4]


class Axes:
    def __init__(self, n, chips):
        dp, b = lax.axis_index("dp"), lax.axis_index("blk")
        core, e = lax.rem(dp, 2), lax.div(dp, 2)
        inner = chips // 4
        slow, fast = lax.div(e, inner), lax.rem(e, inner)
        self.sizes = sum_sizes(n, chips)
        across = lambda i: (dp, i)
        within = lambda i: ((slow * inner + i) * 2 + core, b)
        along = lambda i: ((i * inner + fast) * 2 + core, b)
        self.index = [core, b, fast, slow]
        self.device = [lambda i: (e * 2 + i, b), across, within, along]
        if n == inner:
            swap = core == 1
            pick_one = lambda f, g: lambda i: tuple(jnp.where(swap, y, x) for x, y in zip(f(i), g(i)))
            self.device[1], self.device[2] = pick_one(across, within), pick_one(within, across)
            self.index[1], self.index[2] = jnp.where(swap, fast, b), jnp.where(swap, b, fast)

    def peers(self, phase):
        size = self.sizes[phase]
        for step in range(1, size):
            i = lax.rem(self.index[phase] + step, size)
            yield step, i, self.device[phase](i)

    def greet(self, bar, phases=range(4)):
        met = 0
        for phase in phases:
            for _, _, device in self.peers(phase):
                signal(bar, device)
                met += 1
        return met


class Region:
    def __init__(self, axes, rows):
        self.axes, self.at, self.rows = axes, [0], [rows]
        for phase in range(4):
            self.rows.append(self.rows[-1] // axes.sizes[phase])
            self.at.append(self.at[-1] + axes.index[phase] * self.rows[-1])


class Reduce(Region):
    def __init__(self, axes, src, refs):
        super().__init__(axes, src.shape[0])
        self.src, (self.shard, self.work, *self.recv, self.ssem, self.rsem, self.lsem) = src, refs

    def own(self):
        rows = self.rows[1]
        at = pl.ds(pl.multiple_of(self.at[1], 16), rows)
        return pltpu.make_async_copy(self.src.at[at], self.work, self.lsem.at[0])

    def copies(self, phase):
        rows = self.rows[phase + 1]
        for step, i, device in self.axes.peers(phase):
            first = pl.multiple_of(self.at[phase] - self.at[min(phase, 1)] + i * rows, 16)
            src = self.src if phase == 0 else self.work
            yield send(
                src.at[pl.ds(first, rows)],
                self.recv[phase].at[step - 1],
                self.ssem.at[phase, step - 1],
                self.rsem.at[phase, step - 1],
                device,
            )

    def start(self, phase):
        for copy in self.copies(phase):
            copy.start()

    def finish(self, phase):
        if phase == 0:
            self.own().wait()
        for copy in self.copies(phase):
            copy.wait()
        at = self.at[phase + 1] - self.at[1]
        sources = [(self.work, at)] + [(self.recv[phase].at[i], 0) for i in range(self.axes.sizes[phase] - 1)]
        if phase < 3:
            add_rows(self.work, at, sources, self.rows[phase + 1])
        else:
            add_rows(self.shard, 0, sources, self.rows[4])

    def finish_start(self, phase):
        self.finish(phase)
        self.start(phase + 1)


def reduce_scratch(n, chips, rows, width):
    sizes = sum_sizes(n, chips)
    shapes = [pltpu.VMEM((rows // 2, width), BF16)]
    for size in sizes:
        rows //= size
        shapes.append(pltpu.VMEM((size - 1, rows, width), BF16))
    most = max(sizes) - 1
    return shapes + [pltpu.SemaphoreType.DMA((4, most))] * 2 + [pltpu.SemaphoreType.DMA((1,))]


class Gather(Region):
    def __init__(self, axes, shard, out, refs):
        super().__init__(axes, out.shape[0])
        self.shard, self.out, (self.ssem, self.rsem, self.lsem) = shard, out, refs

    def region(self, phase):
        return self.out.at[pl.ds(pl.multiple_of(self.at[phase + 1], 16), self.rows[phase + 1])]

    def own(self):
        return pltpu.make_async_copy(self.shard, self.region(3), self.lsem.at[0])

    def copies(self, phase):
        src = self.shard if phase == 3 else self.region(phase)
        for step, _, device in self.axes.peers(phase):
            yield send(
                src, self.region(phase), self.ssem.at[phase, step - 1], self.rsem.at[phase, step - 1], device
            )

    def start(self, phase):
        if phase == 3:
            self.own().start()
        for copy in self.copies(phase):
            copy.start()

    def finish(self, phase):
        if phase == 3:
            self.own().wait()
        for copy in self.copies(phase):
            copy.wait()

    def finish_start(self, phase):
        self.finish(phase)
        self.start(phase - 1)


def gather_scratch(n, chips):
    most = max(sum_sizes(n, chips)) - 1
    return [pltpu.SemaphoreType.DMA((4, most))] * 2 + [pltpu.SemaphoreType.DMA((1,))]


def project_kernel(n, layer, *refs):
    first = layer == 0
    if first:
        tok_in, cot, kind, leads, table, gain, w, h_out, n1_out, q_out, k_all, v_all, aux_out, tok, kbuf, vbuf, aux_in, ssem, rsem, ksem, krsem, lsem = refs
    else:
        h_in, gain, w, n1_out, q_out, k_all, v_all, kbuf, vbuf, ksem, krsem, lsem = refs
    place = Place(n)
    rows, width = kbuf.shape
    block = min(256, rows // 2)
    blocks = rows // block
    bar = pltpu.get_barrier_semaphore()
    for step in range(1, n):
        signal(bar, place.peer(step))
    if first:
        aux_in[0:EXPERTS, :] = cot[...]
        kind_one = kind[...].astype(F32)
        lead_one = leads[...].astype(F32)
        first_lead = lead_one[:, 0:1]
        second_lead = jnp.where(kind_one == 1.0, lead_one[:, 1:2], first_lead)
        for row, value in ((KIND_ROW, kind_one), (LEAD_ROW, first_lead), (LEAD_ROW + 1, second_lead)):
            aux_in[row : row + 1, :] = jnp.broadcast_to(value, (1, rows))
        aux_in[LEAD_ROW + 2 :, :] = jnp.zeros((8 - LEAD_ROW - 2, rows), F32)

        @pl.when(place.moves)
        def _():
            signal(bar, place.partner)
            pl.semaphore_wait(bar, n)

        @pl.when(jnp.logical_not(place.moves))
        def _():
            pl.semaphore_wait(bar, n - 1)

        swaps = [send(aux_in, aux_out, ssem.at[blocks], rsem.at[blocks], place.partner)]
        for i in range(blocks):
            at = pl.ds(i * block, block)
            swaps.append(send(tok_in.at[at], tok.at[at], ssem.at[i], rsem.at[i], place.partner))

        @pl.when(place.moves)
        def _():
            for copy in swaps:
                copy.start()
            swaps[0].wait_recv()

        @pl.when(jnp.logical_not(place.moves))
        def _():
            tok[...] = tok_in[...]
            aux_out[...] = aux_in[...]

        lead_index = lax.broadcasted_iota(jnp.int32, (table.shape[0], 1), 0).astype(F32)
        lead_rows = []
        for half in range(2):
            lead = aux_out[LEAD_ROW + half : LEAD_ROW + half + 1, 0:1]
            lead_rows.append(column_sum(jnp.where(lead_index == lead, table[...], 0.0)))

    gain_row = gain[layer : layer + 1, :]
    copies = []
    for i in range(blocks):
        at = pl.ds(i * block, block)
        if first:

            @pl.when(place.moves)
            def _():
                swaps[1 + i].wait_recv()

            x = tok[at, :].astype(F32) + lead_rows[i * block // (rows // 2)]
            h_out[at, :] = x
        else:
            x = h_in[at, :]
        n1 = (normalize(x)[0] * gain_row).astype(BF16)
        n1_out[at, :] = n1
        kv = dot(n1, w[:, width:]).astype(BF16)
        if i == 0 and not first:
            pl.semaphore_wait(bar, n - 1)
        for part, (buf, whole) in enumerate(((kbuf, k_all), (vbuf, v_all))):
            buf[at, :] = kv[:, part * width : (part + 1) * width]
            copies.append(pltpu.make_async_copy(buf.at[at], whole.at[0, at], lsem.at[part, i]))
            copies[-1].start()
            for step in range(1, n):
                copies.append(
                    send(
                        buf.at[at],
                        whole.at[step, at],
                        ksem.at[step - 1, part, i],
                        krsem.at[step - 1, part, i],
                        place.peer(n - step),
                    )
                )
                copies[-1].start()
    for i in range(blocks):
        at = pl.ds(i * block, block)
        q_out[at, :] = (dot(n1_out[at, :], w[:, :width]) * HEAD_DIM**-0.5).astype(BF16)
    for copy in copies:
        copy.wait()
    if first:

        @pl.when(place.moves)
        def _():
            for copy in swaps:
                copy.wait_send()


def project(n, layer, collective_id, *args):
    rows, width = args[0].shape
    first = layer == 0
    blocks = rows // min(256, rows // 2)
    shapes = [
        jax.ShapeDtypeStruct((rows, width), BF16),
        jax.ShapeDtypeStruct((rows, width), BF16),
        jax.ShapeDtypeStruct((n, rows, width), BF16),
        jax.ShapeDtypeStruct((n, rows, width), BF16),
    ]
    specs = [VMEM, VMEM, ANY, ANY]
    scratch = [
        pltpu.VMEM((rows, width), BF16),
        pltpu.VMEM((rows, width), BF16),
        pltpu.SemaphoreType.DMA((n - 1, 2, blocks)),
        pltpu.SemaphoreType.DMA((n - 1, 2, blocks)),
        pltpu.SemaphoreType.DMA((2, blocks)),
    ]
    if first:
        shapes = [jax.ShapeDtypeStruct((rows, width), F32)] + shapes + [jax.ShapeDtypeStruct((8, rows), F32)]
        specs = [VMEM] + specs + [VMEM]
        scratch = (
            [pltpu.VMEM((rows, width), BF16)]
            + scratch[:2]
            + [pltpu.VMEM((8, rows), F32)]
            + [pltpu.SemaphoreType.DMA((blocks + 1,))] * 2
            + scratch[2:]
        )
    return pl.pallas_call(
        functools.partial(project_kernel, n, layer),
        grid=(1,),
        out_shape=shapes,
        in_specs=[VMEM] * (len(args) - 1) + [pick(layer, args[-1])],
        out_specs=specs,
        scratch_shapes=scratch,
        compiler_params=params(collective_id),
        name="project_first" if first else "project",
    )(*args)


def head_lanes(x, head):
    lane = lax.broadcasted_iota(jnp.int32, x.shape, 1)
    return jnp.where(lane // HEAD_DIM == head, x, jnp.zeros_like(x))


def attend_kernel(band, q_ref, k_ref, v_ref, aux_ref, e_ref, ob_ref, li_ref, vte):
    j = pl.program_id(1)
    keys, queries = e_ref.shape[1:]
    chunk = band // 2
    own_half = lax.rem(j, 2)
    coarse = aux_ref[KIND_ROW : KIND_ROW + 1, 0:1]
    coarse_flag = jnp.max(coarse) > 0.5

    @pl.when(j == 0)
    def _():
        turned = v_ref[...].astype(F32).T
        key_half = lax.rem(lax.broadcasted_iota(jnp.int32, (1, keys), 1) // chunk, 2)
        for half in range(2):
            seen = jnp.where(key_half == half, 1.0, 1.0 - coarse)
            for head in range(2):
                rows = turned[head * HEAD_DIM : (head + 1) * HEAD_DIM, :] * seen
                vte[head, half, :HEAD_DIM, :] = rows.astype(BF16)
                vte[head, half, HEAD_DIM:, :] = jnp.broadcast_to(seen, (HEAD_DIM, keys)).astype(BF16)

    def finish(head, total, norm):
        inverse = 1.0 / norm
        ob_ref[head * HEAD_DIM : (head + 1) * HEAD_DIM, :] = (total * inverse).astype(BF16)
        li_ref[head : head + 1, :] = inverse

    li_ref[...] = jnp.zeros_like(li_ref)
    least, largest = None, None
    for head in range(2):
        e = jnp.exp(dot(k_ref[...], head_lanes(q_ref[...], head), (1, 1))).astype(BF16)
        e_ref[head, :, :] = e
        total = dot(vte[head, own_half], e)
        norm = total[HEAD_DIM : HEAD_DIM + 1, :]
        finish(head, total[:HEAD_DIM, :], norm)
        least = norm if least is None else jnp.minimum(least, norm)
        largest = norm if largest is None else jnp.maximum(largest, norm)

    @pl.when(coarse_flag)
    def _():
        for c in range(keys // (2 * chunk)):
            at = pl.ds(pl.multiple_of((2 * c + 1 - own_half) * chunk, chunk), chunk)
            for head in range(2):
                e_ref[head, at, :] = jnp.zeros((chunk, queries), BF16)

    fits = jnp.logical_and(least > 1e-20, largest < 1e25)

    @pl.when(jnp.min(fits.astype(F32)) < 0.5)
    def _():
        for head in range(2):
            queries_one = head_lanes(q_ref[...], head)

            def scores(c):
                at = pl.ds(pl.multiple_of(c * chunk, chunk), chunk)
                hidden = jnp.logical_and(coarse > 0.5, lax.rem(c, 2) != own_half)
                return at, hidden, jnp.where(hidden, -1e30, dot(k_ref[at, :], queries_one, (1, 1)))

            def highest_step(c, top):
                return jnp.maximum(top, jnp.max(scores(c)[2], axis=0, keepdims=True))

            top = lax.fori_loop(0, keys // chunk, highest_step, jnp.full((1, queries), -1e30, F32))

            def total_step(c, total):
                at, hidden, s = scores(c)
                e = jnp.where(hidden, 0.0, jnp.exp(s - top)).astype(BF16)
                e_ref[head, at, :] = e
                return total + dot(vte[head, own_half, :, at], e)

            total = lax.fori_loop(
                0, keys // chunk, total_step, jnp.zeros((LANES, queries), F32)
            )
            finish(head, total[:HEAD_DIM, :], total[HEAD_DIM : HEAD_DIM + 1, :])


def attend(q, k, v, aux):
    rows, width = q.shape
    keys, queries, pairs = k.shape[0], rows // 2, width // LANES
    return pl.pallas_call(
        functools.partial(attend_kernel, rows),
        grid=(pairs, 2),
        out_shape=[
            jax.ShapeDtypeStruct((2 * pairs, keys, rows), BF16),
            jax.ShapeDtypeStruct((width, rows), BF16),
            jax.ShapeDtypeStruct((8 * pairs, rows), F32),
        ],
        in_specs=[
            pl.BlockSpec((queries, LANES), lambda p, j: (j, p)),
            pl.BlockSpec((keys, LANES), lambda p, j: (0, p)),
            pl.BlockSpec((keys, LANES), lambda p, j: (0, p)),
            pl.BlockSpec(aux.shape, lambda p, j: (0, 0)),
        ],
        out_specs=[
            pl.BlockSpec((2, keys, queries), lambda p, j: (p, 0, j)),
            pl.BlockSpec((LANES, queries), lambda p, j: (p, j)),
            pl.BlockSpec((8, queries), lambda p, j: (p, j)),
        ],
        scratch_shapes=[pltpu.VMEM((2, 2, LANES, keys), BF16)],
        compiler_params=params(),
        name="attend",
    )(q, k, v, aux)


def attend_back_kernel(n, chips, plan, jobs, *refs):
    q_ref, k_ref, v_ref, e_ref, do_ref, dl_ref = refs[:6]
    sources, refs = refs[6 : 6 + jobs], refs[6 + jobs :]
    dq_ref, dk_ref, dv_ref = refs[:3]
    gathers = [job for job, (_, gather) in enumerate(plan) if gather]
    shards, refs = refs[3 : 3 + jobs], refs[3 + jobs :]
    outs, refs = refs[: len(gathers)], refs[len(gathers) :]
    kt, vext, dk_sum, dv_sum, rhs = refs[:5]
    refs = refs[5:]
    t = pl.program_id(0) * pl.num_programs(1) + pl.program_id(1)
    keys, queries = e_ref.shape[1:]

    axes = Axes(n, chips)
    bar = pltpu.get_barrier_semaphore()
    schedule = {}
    met = sum(size - 1 for size in axes.sizes)

    def enter(reduces):
        axes.greet(bar)
        for reduce in reduces:
            reduce.own().start()

    reduces = []
    for job in range(jobs):
        scratch, refs = refs[:8], refs[8:]
        reduces.append(Reduce(axes, sources[job], (shards[job],) + tuple(scratch)))
    schedule[0] = [lambda: pl.semaphore_wait(bar, met)] + [functools.partial(reduce.start, 0) for reduce in reduces]
    for job in range(jobs):
        points, gather_points = plan[job]
        reduce = reduces[job]
        for phase, point in enumerate(points):
            act = reduce.finish_start if phase < 3 else reduce.finish
            schedule.setdefault(point, []).append(functools.partial(act, phase))
        if gather_points:
            scratch, refs = refs[:3], refs[3:]
            gather = Gather(axes, shards[job], outs[gathers.index(job)], scratch)
            schedule.setdefault(points[3], []).append(functools.partial(gather.start, 3))
            for phase, point in zip((3, 2, 1, 0), gather_points):
                act = gather.finish_start if phase > 0 else gather.finish
                schedule.setdefault(point, []).append(functools.partial(act, phase))

    def points(part):
        for point in sorted(schedule):
            if point % 2 == part:

                @pl.when(t == point // 2)
                def _():
                    for act in schedule[point]:
                        act()

    @pl.when(t == 0)
    def _():
        enter(reduces)

    @pl.when(pl.program_id(1) == 0)
    def _():
        kt[...] = k_ref[...].astype(F32).T.astype(BF16)
        vext[:, :LANES] = v_ref[...]
        vext[:, LANES:] = jnp.ones((keys, LANES), BF16)
        dk_sum[...] = jnp.zeros_like(dk_sum)
        dv_sum[...] = jnp.zeros_like(dv_sum)

    do = do_ref[...].astype(F32)
    row_head = lax.broadcasted_iota(jnp.int32, (LANES, 1), 0) // HEAD_DIM
    for head in range(2):
        rhs[head, :LANES, :] = jnp.where(row_head == head, do, 0.0).astype(BF16)
        rhs[head, LANES : LANES + 16, :] = dl_ref[16 * head : 16 * head + 16, :]
        rhs[head, LANES + 16 :, :] = jnp.zeros((LANES - 16, queries), BF16)
    do_rows = jnp.concatenate([rhs[head, :LANES, :].astype(F32).T.astype(BF16) for head in range(2)], axis=0)
    q_rows = jnp.concatenate([head_lanes(q_ref[...], head) for head in range(2)], axis=0)
    dv_sum[...] += dot(jnp.concatenate([e_ref[0], e_ref[1]], axis=1), do_rows)
    ds, dq = [], []
    for head in range(2):
        ds.append((e_ref[head].astype(F32) * dot(vext[...], rhs[head])).astype(BF16))
        dq.append(dot(kt[...], ds[head])[head * HEAD_DIM : (head + 1) * HEAD_DIM])
        if head == 0:
            points(0)
    dk_sum[...] += dot(jnp.concatenate(ds, axis=1), q_rows)
    dq_ref[...] = (jnp.concatenate(dq, axis=0) * HEAD_DIM**-0.5).T.astype(BF16)

    @pl.when(pl.program_id(1) == pl.num_programs(1) - 1)
    def _():
        dk_ref[...] = dk_sum[...].astype(BF16)
        dv_ref[...] = dv_sum[...].astype(BF16)

    points(1)


def attend_back(n, chips, collective_id, plan, q, k, v, e, do, dl, *jobs):
    rows, width = q.shape
    keys, queries, pairs = k.shape[0], rows // 2, width // LANES
    gathered = [job for job, (_, gather) in zip(jobs, plan) if gather]
    devices = 2 * n * chips
    scratch = []
    for job in jobs:
        scratch += reduce_scratch(n, chips, *job.shape)
    scratch += gather_scratch(n, chips) * len(gathered)
    return pl.pallas_call(
        functools.partial(attend_back_kernel, n, chips, plan, len(jobs)),
        grid=(pairs, 2),
        out_shape=[
            jax.ShapeDtypeStruct((rows, width), BF16),
            jax.ShapeDtypeStruct((keys, width), BF16),
            jax.ShapeDtypeStruct((keys, width), BF16),
        ]
        + [jax.ShapeDtypeStruct((job.shape[0] // devices, width), BF16) for job in jobs]
        + [jax.ShapeDtypeStruct(job.shape, BF16) for job in gathered],
        in_specs=[
            pl.BlockSpec((queries, LANES), lambda p, j: (j, p)),
            pl.BlockSpec((keys, LANES), lambda p, j: (0, p)),
            pl.BlockSpec((keys, LANES), lambda p, j: (0, p)),
            pl.BlockSpec((2, keys, queries), lambda p, j: (p, 0, j)),
            pl.BlockSpec((LANES, queries), lambda p, j: (p, j)),
            pl.BlockSpec((32, queries), lambda p, j: (p, j)),
        ]
        + [ANY] * len(jobs),
        out_specs=[
            pl.BlockSpec((queries, LANES), lambda p, j: (j, p)),
            pl.BlockSpec((keys, LANES), lambda p, j: (0, p)),
            pl.BlockSpec((keys, LANES), lambda p, j: (0, p)),
        ]
        + [VMEM] * len(jobs)
        + [ANY] * len(gathered),
        scratch_shapes=[
            pltpu.VMEM((LANES, keys), BF16),
            pltpu.VMEM((keys, 2 * LANES), BF16),
            pltpu.VMEM((keys, LANES), F32),
            pltpu.VMEM((keys, LANES), F32),
            pltpu.VMEM((2, 2 * LANES, queries), BF16),
        ]
        + scratch,
        compiler_params=params(collective_id),
        name="attend_back",
    )(q, k, v, e, do, dl, *jobs)


def mlp_block(at, h, ob, w_out, gain2, w1, b1, w2, h2_ref, n2_ref, a_ref, gp_ref):
    h2 = h + dot(ob, w_out[...], (0, 0))
    h2_ref[at, :] = h2
    n2 = (normalize(h2)[0] * gain2[...]).astype(BF16)
    n2_ref[at, :] = n2
    u = dot(n2, w1[...]) + b1[...]
    square = u * u
    t = jnp.tanh(gelu_in * u * (1.0 + gelu_cubic * square))
    half = 0.5 + 0.5 * t
    a = (u * half).astype(BF16)
    a_ref[at, :] = a
    slope = half + (0.5 * gelu_in) * u * (1.0 - t * t) * (1.0 + 3.0 * gelu_cubic * square)
    gp_ref[at, :] = slope.astype(BF16)
    return h2 + dot(a, w2[...])


def mlp_kernel(layer, h_ref, ob_ref, w_out, gain2, w1, b1, w2, h2_ref, n2_ref, a_ref, gp_ref, h3_ref):
    rows = h_ref.shape[0]
    gain2, b1 = gain2.at[pl.ds(layer, 1)], b1.at[pl.ds(layer, 1)]
    block = min(512, rows)
    for i in range(rows // block):
        at = pl.ds(i * block, block)
        h3_ref[at, :] = mlp_block(
            at, h_ref[at, :], ob_ref[:, at], w_out, gain2, w1, b1, w2, h2_ref, n2_ref, a_ref, gp_ref
        )


def mlp(layer, h, ob, w_out, gain2, w1, b1, w2):
    rows, width = h.shape
    hidden = w1.shape[2]
    return pl.pallas_call(
        functools.partial(mlp_kernel, layer),
        grid=(1,),
        out_shape=[
            jax.ShapeDtypeStruct((rows, width), F32),
            jax.ShapeDtypeStruct((rows, width), BF16),
            jax.ShapeDtypeStruct((rows, hidden), BF16),
            jax.ShapeDtypeStruct((rows, hidden), BF16),
            jax.ShapeDtypeStruct((rows, width), F32),
        ],
        in_specs=[VMEM, VMEM, pick(layer, w_out), VMEM, pick(layer, w1), VMEM, pick(layer, w2)],
        out_specs=[VMEM] * 5,
        compiler_params=params(),
        name="mlp",
    )(h, ob, w_out, gain2, w1, b1, w2)


def mlp_back_block(at, dh, gp, h2, ob, li, w_out, gain2, w1, w2, dz_ref, du_ref, dy_ref, dh2_ref, do_ref, dl_ref):
    dz = dh.astype(BF16)
    dz_ref[at, :] = dz
    du = (dot(dz, w2[...], (1, 1)) * gp.astype(F32)).astype(BF16)
    du_ref[at, :] = du
    bias_sum = column_sum(du.astype(F32))
    dn2 = dot(du, w1[...], (1, 1))
    xhat, rstd = normalize(h2)
    gain_sum = column_sum(dn2 * xhat)
    dh2 = dh + normalize_back(dn2 * gain2[...], xhat, rstd)
    dh2_ref[at, :] = dh2
    dy = dh2.astype(BF16)
    dy_ref[at, :] = dy
    do = dot(w_out[...], dy, (1, 1))
    product = do * ob.astype(F32)
    for head in range(do.shape[0] // HEAD_DIM):
        rows = slice(head * HEAD_DIM, (head + 1) * HEAD_DIM)
        inverse = li[8 * (head // 2) + head % 2 : 8 * (head // 2) + head % 2 + 1, :]
        do_ref[rows, at] = (do[rows] * inverse).astype(BF16)
        rest = -column_sum(product[rows]) * inverse
        terms = []
        for _ in range(3):
            terms.append(rest.astype(BF16).astype(F32))
            rest = rest - terms[-1]
        row = lax.broadcasted_iota(jnp.int32, (16, 1), 0)
        block = jnp.where(row == 0, terms[0], jnp.where(row == 1, terms[1], jnp.where(row == 2, terms[2], 0.0)))
        dl_ref[16 * head : 16 * head + 16, at] = block.astype(BF16)
    return bias_sum, gain_sum


def weight_sums(g_ref, a, dz, n2, du, ob, dy):
    hidden, width = a.shape[1], dz.shape[1]
    g_ref[:hidden, :] = dot(a[...], dz[...], (0, 0)).astype(BF16)
    for part in range(hidden // width):
        at = slice(part * width, (part + 1) * width)
        g_ref[hidden + part * width : hidden + (part + 1) * width, :] = dot(n2[...], du[:, at], (0, 0)).astype(BF16)
    g_ref[2 * hidden : 2 * hidden + width, :] = dot(ob[...], dy[...]).astype(BF16)
    if g_ref.shape[0] > 2 * hidden + width:
        g_ref[2 * hidden + width :, :] = jnp.zeros((g_ref.shape[0] - 2 * hidden - width, width), BF16)


def put_rows(small_ref, row, value, width):
    for part in range(value.shape[1] // width):
        small_ref[row + part : row + part + 1, :] = value[:, part * width : (part + 1) * width]


def back_shapes(rows, width, hidden, grad_rows):
    return [
        jax.ShapeDtypeStruct((grad_rows, width), BF16),
        jax.ShapeDtypeStruct((8, width), F32),
        jax.ShapeDtypeStruct((rows, width), F32),
        jax.ShapeDtypeStruct((width, rows), BF16),
        jax.ShapeDtypeStruct((16 * width // HEAD_DIM, rows), BF16),
    ]


def turn_kernel(
    layer, h_ref, ob_ref, li_ref, aux_ref, w_out, gain2, w1, b1, w2, fgain, head_w, head_b, prior_ref,
    g_ref, small_ref, dh2_ref, do_ref, dl_ref, expert_ref, head_ref, dz, du, dy, h2_ref, n2_ref, a_ref, gp_ref, wide, tall,
):
    rows, width = h_ref.shape
    gain2, b1 = gain2.at[pl.ds(layer, 1)], b1.at[pl.ds(layer, 1)]
    block = rows // 2
    wide[...] = jnp.zeros_like(wide)
    wide[:, 0:EXPERTS] = head_w[...]
    hw = wide[...].T[0:8, :]
    tall[...] = jnp.ones_like(tall)
    tall[0:LEADS, 0:EXPERTS] = prior_ref[...]
    logp = jnp.log(tall[...]).T[0:8, :]
    tall[0:1, 0:EXPERTS] = head_b[...]
    hb = tall[...].T[0:8, 0:1]
    lane = lax.broadcasted_iota(jnp.int32, (8, LANES), 1).astype(F32)
    expert = lax.broadcasted_iota(jnp.int32, (8, 1), 0)
    bias_sum, gain_sum, final_sum, head_sum, hbias_sum, lead_sum = 0.0, 0.0, 0.0, 0.0, 0.0, 0.0
    for i in range(2):
        at = pl.ds(i * block, block)
        h3 = mlp_block(at, h_ref[at, :], ob_ref[:, at], w_out, gain2, w1, b1, w2, h2_ref, n2_ref, a_ref, gp_ref)
        xhat, rstd = normalize(h3)
        nf = xhat * fgain[...]
        own_lead = lane == aux_ref[LEAD_ROW + i : LEAD_ROW + i + 1, 0:1]
        prior = jnp.sum(jnp.where(own_lead, logp, 0.0), axis=1, keepdims=True)
        logits = dot(hw, nf, (1, 1), HIGHEST) + hb - prior
        logits = jnp.where(expert < EXPERTS, logits, -1e30)
        power = jnp.exp(logits - jnp.max(logits, axis=0, keepdims=True))
        weights = power / jnp.sum(power, axis=0, keepdims=True)
        expert_ref[:, at] = weights
        counted = jnp.where(expert == EXPERTS, 1.0, weights)
        lead_sum = lead_sum + jnp.where(own_lead, jnp.sum(counted, axis=1, keepdims=True), 0.0)
        cot = jnp.where(expert < EXPERTS, aux_ref[:, at], 0.0)
        dlogits = weights * (cot - jnp.sum(weights * cot, axis=0, keepdims=True))
        head_sum = head_sum + dot(dlogits, nf, (1, 0), HIGHEST)
        hbias_sum = hbias_sum + jnp.sum(dlogits, axis=1, keepdims=True)
        dnf = dot(dlogits, hw, (0, 0), HIGHEST)
        final_sum = final_sum + column_sum(dnf * xhat)
        dh = normalize_back(dnf * fgain[...], xhat, rstd)
        sums = mlp_back_block(
            at, dh, gp_ref[at, :], h2_ref[at, :], ob_ref[:, at], li_ref[:, at], w_out, gain2, w1, w2,
            dz, du, dy, dh2_ref, do_ref, dl_ref,
        )
        bias_sum, gain_sum = bias_sum + sums[0], gain_sum + sums[1]
    small_ref[...] = jnp.zeros_like(small_ref)
    put_rows(small_ref, 0, gain_sum, width)
    put_rows(small_ref, 1, final_sum, width)
    put_rows(small_ref, 4, bias_sum, width)
    head_ref[0:8, :] = head_sum
    head_ref[8:16, :] = jnp.zeros((8, width), F32)
    head_ref[8:16, 0:LANES] = lead_sum
    head_ref[16:24, :] = jnp.broadcast_to(hbias_sum, (8, width))
    weight_sums(g_ref, a_ref, dz, n2_ref, du, ob_ref, dy)


def turn(layer, h, ob, li, aux, w_out, gain2, w1, b1, w2, fgain, head_w, head_b, prior, grad_rows):
    rows, width = h.shape
    hidden = w1.shape[2]
    return pl.pallas_call(
        functools.partial(turn_kernel, layer),
        grid=(1,),
        out_shape=back_shapes(rows, width, hidden, grad_rows)
        + [jax.ShapeDtypeStruct((8, rows), F32), jax.ShapeDtypeStruct((24, width), F32)],
        in_specs=[VMEM] * 4 + [pick(layer, w_out), VMEM, pick(layer, w1), VMEM, pick(layer, w2)] + [VMEM] * 4,
        out_specs=[VMEM] * 7,
        scratch_shapes=[
            pltpu.VMEM((rows, width), BF16),
            pltpu.VMEM((rows, hidden), BF16),
            pltpu.VMEM((rows, width), BF16),
            pltpu.VMEM((rows, width), F32),
            pltpu.VMEM((rows, width), BF16),
            pltpu.VMEM((rows, hidden), BF16),
            pltpu.VMEM((rows, hidden), BF16),
            pltpu.VMEM((width, LANES), F32),
            pltpu.VMEM((LANES, LANES), F32),
        ],
        compiler_params=params(),
        name="turn",
    )(h, ob, li, aux, w_out, gain2, w1, b1, w2, fgain, head_w, head_b, prior)


class KeyGrads:
    def __init__(self, place, dk, dv, recv, dkv, ssem, rsem):
        self.place, self.parts, self.recv, self.dkv, self.ssem, self.rsem = place, (dk, dv), recv, dkv, ssem, rsem

    def copies(self):
        for step in range(1, self.place.n):
            for part, src in enumerate(self.parts):
                at = step - 1, part
                yield send(src.at[step], self.recv.at[at], self.ssem.at[at], self.rsem.at[at], self.place.peer(step))

    def start(self):
        for copy in self.copies():
            copy.start()

    def finish(self):
        for copy in self.copies():
            copy.wait()
        width = self.dkv.shape[1] // 2
        for part, own in enumerate(self.parts):
            total = own[0].astype(F32)
            for step in range(self.place.n - 1):
                total = total + self.recv[step, part].astype(F32)
            self.dkv[:, part * width : (part + 1) * width] = total.astype(BF16)


def key_scratch(n, rows, width):
    return [
        pltpu.VMEM((n - 1, 2, rows, width), BF16),
        pltpu.VMEM((rows, 2 * width), BF16),
        pltpu.SemaphoreType.DMA((n - 1, 2)),
        pltpu.SemaphoreType.DMA((n - 1, 2)),
    ]


def project_back_block(at, dn1_q, dkv, w, gain_row, h, dh2):
    width = h.shape[1]
    dn1 = dn1_q + dot(dkv[at, :], w[:, width:], (1, 1))
    xhat, rstd = normalize(h[at, :])
    return dh2[at, :] + normalize_back(dn1 * gain_row, xhat, rstd), column_sum(dn1 * xhat)


def key_weight_sums(g_ref, n1, dkv):
    width = n1.shape[1]
    for part in range(2):
        at = slice(part * width, (part + 1) * width)
        g_ref[(part + 1) * width : (part + 2) * width, :] = dot(n1[...], dkv[:, at], (0, 0)).astype(BF16)


def between_kernel(
    n, chips, dq, dk, dv, n1, h3, dh2_in, w, gain1, gp_ref, h2_ref, ob_ref, li_ref, n2_ref, a_ref, w_out, gain2, w1, w2, shard,
    gq_ref, norm_ref, g_ref, small_ref, dh2_ref, do_ref, dl_ref, sum_ref,
    gp, a, dz, du, dy, late, krecv, dkv, ksem, krsem, *gather_refs,
):
    place, axes = Place(n), Axes(n, chips)
    rows, width = dq.shape
    block = rows // 2
    bar = pltpu.get_barrier_semaphore()
    met = axes.greet(bar)
    for step in range(1, n):
        signal(bar, place.peer(step))
    fetch = [pltpu.make_async_copy(src, dst, late.at[i]) for i, (src, dst) in enumerate(((gp_ref, gp), (a_ref, a)))]
    for copy in fetch:
        copy.start()
    gq_ref[:width, :] = dot(n1[...], dq[...], (0, 0)).astype(BF16)
    pl.semaphore_wait(bar, met + n - 1)
    keys = KeyGrads(place, dk, dv, krecv, dkv, ksem, krsem)
    keys.start()
    gather = Gather(axes, shard, sum_ref, gather_refs)
    gather.start(3)
    dn1_q = [dot(dq[pl.ds(i * block, block), :], w[:, :width], (1, 1)) for i in range(2)]
    keys.finish()
    gain_sum = 0.0
    dh = []
    for i in range(2):
        at = pl.ds(i * block, block)
        dh_one, part = project_back_block(at, dn1_q[i], dkv, w, gain1[1:2, :], h3, dh2_in)
        dh.append(dh_one)
        gain_sum = gain_sum + part
    norm_ref[...] = jnp.broadcast_to(gain_sum, norm_ref.shape)
    key_weight_sums(gq_ref, n1, dkv)
    if gq_ref.shape[0] > 3 * width:
        gq_ref[3 * width :, :] = jnp.zeros((gq_ref.shape[0] - 3 * width, width), BF16)
    gather.finish_start(3)
    for copy in fetch:
        copy.wait()
    bias_sum, gain_sum = 0.0, 0.0
    for i in range(2):
        at = pl.ds(i * block, block)
        sums = mlp_back_block(
            at, dh[i], gp[at, :], h2_ref[at, :], ob_ref[:, at], li_ref[:, at], w_out, gain2.at[pl.ds(0, 1)], w1, w2,
            dz, du, dy, dh2_ref, do_ref, dl_ref,
        )
        bias_sum, gain_sum = bias_sum + sums[0], gain_sum + sums[1]
        if i == 0:
            gather.finish_start(2)
    small_ref[...] = jnp.zeros_like(small_ref)
    put_rows(small_ref, 0, gain_sum, width)
    put_rows(small_ref, 4, bias_sum, width)
    weight_sums(g_ref, a, dz, n2_ref, du, ob_ref, dy)
    gather.finish_start(1)
    gather.finish(0)


def between(n, chips, collective_id, qkv_rows, mlp_rows, dq, dk, dv, n1, h3, dh2, w, gain1, gp, h2, ob, li, n2, a, w_out, gain2, w1, w2, shard, sum_rows):
    rows, width = dq.shape
    hidden = a.shape[1]
    return pl.pallas_call(
        functools.partial(between_kernel, n, chips),
        grid=(1,),
        out_shape=[jax.ShapeDtypeStruct((qkv_rows, width), BF16), jax.ShapeDtypeStruct((8, width), F32)]
        + back_shapes(rows, width, hidden, mlp_rows)
        + [jax.ShapeDtypeStruct((sum_rows, width), BF16)],
        in_specs=[VMEM] * 6
        + [pick(1, w), VMEM, ANY, VMEM, VMEM, VMEM, VMEM, ANY, pick(0, w_out), VMEM, pick(0, w1), pick(0, w2), VMEM],
        out_specs=[VMEM] * 7 + [ANY],
        scratch_shapes=[
            pltpu.VMEM((rows, hidden), BF16),
            pltpu.VMEM((rows, hidden), BF16),
            pltpu.VMEM((rows, width), BF16),
            pltpu.VMEM((rows, hidden), BF16),
            pltpu.VMEM((rows, width), BF16),
            pltpu.SemaphoreType.DMA((2,)),
        ]
        + key_scratch(n, rows, width)
        + gather_scratch(n, chips),
        compiler_params=params(collective_id),
        name="between",
    )(dq, dk, dv, n1, h3, dh2, w, gain1, gp, h2, ob, li, n2, a, w_out, gain2, w1, w2, shard)


def last_kernel(
    n, chips, dq, dk, dv, n1, h, dh2, w, gain, aux, expert, norm_b, small_a, small_b, head, shard,
    tg_out, ex_out, mlp_ref, sum_ref,
    tg, g_ref, own_shard, krecv, dkv, ksem, krsem, ssem, rsem, *refs,
):
    place, axes = Place(n), Axes(n, chips)
    rows, width = dq.shape
    block = rows // 2
    bar = pltpu.get_barrier_semaphore()
    met = axes.greet(bar) + n - 1
    for step in range(1, n):
        signal(bar, place.peer(step))

    @pl.when(place.moves)
    def _():
        signal(bar, place.partner)

    g_ref[:width, :] = dot(n1[...], dq[...], (0, 0)).astype(BF16)

    @pl.when(place.moves)
    def _():
        pl.semaphore_wait(bar, met + 1)

    @pl.when(jnp.logical_not(place.moves))
    def _():
        pl.semaphore_wait(bar, met)

    keys = KeyGrads(place, dk, dv, krecv, dkv, ksem, krsem)
    keys.start()
    earlier = Gather(axes, shard, mlp_ref, refs[:3])
    earlier.start(3)
    dn1_q = [dot(dq[pl.ds(i * block, block), :], w[:, :width], (1, 1)) for i in range(2)]
    keys.finish()
    gain_sum = 0.0
    half_sums = []
    for i in range(2):
        at = pl.ds(i * block, block)
        dh, part = project_back_block(at, dn1_q[i], dkv, w, gain[0:1, :], h, dh2)
        gain_sum = gain_sum + part
        half_sums.append(column_sum(dh))
        tg[at, :] = dh.astype(BF16)
    lead_index = lax.broadcasted_iota(jnp.int32, (LEADS, 1), 0).astype(F32)
    table = 0.0
    for half in range(2):
        lead = aux[LEAD_ROW + half : LEAD_ROW + half + 1, 0:1]
        table = table + jnp.where(lead_index == lead, half_sums[half], 0.0)
    at = 3 * width
    for piece in (table, jnp.broadcast_to(gain_sum, (8, width)), norm_b[...], small_a[...], small_b[...], head[...]):
        g_ref[at : at + piece.shape[0], :] = piece.astype(BF16)
        at += piece.shape[0]
    g_ref[at:, :] = jnp.zeros((g_ref.shape[0] - at, width), BF16)
    key_weight_sums(g_ref, n1, dkv)
    reduce = Reduce(axes, g_ref, (own_shard,) + refs[3:11])
    gather = Gather(axes, own_shard, sum_ref, refs[11:])
    reduce.own().start()
    reduce.start(0)
    swaps = [
        send(tg, tg_out, ssem.at[0], rsem.at[0], place.partner),
        send(expert, ex_out, ssem.at[1], rsem.at[1], place.partner),
    ]

    @pl.when(place.moves)
    def _():
        for copy in swaps:
            copy.start()

    @pl.when(jnp.logical_not(place.moves))
    def _():
        tg_out[...] = tg[...]
        ex_out[...] = expert[...]

    reduce.finish_start(0)
    earlier.finish_start(3)
    reduce.finish_start(1)
    earlier.finish_start(2)
    reduce.finish_start(2)
    earlier.finish_start(1)
    reduce.finish(3)
    gather.start(3)
    earlier.finish(0)
    for phase in (3, 2, 1):
        gather.finish_start(phase)
    gather.finish(0)

    @pl.when(place.moves)
    def _():
        for copy in swaps:
            copy.wait()


def last(n, chips, collective_id, qkv_rows, mlp_rows, *args):
    rows, width = args[0].shape
    devices = 2 * n * chips
    return pl.pallas_call(
        functools.partial(last_kernel, n, chips),
        grid=(1,),
        out_shape=[
            jax.ShapeDtypeStruct((rows, width), BF16),
            jax.ShapeDtypeStruct((8, rows), F32),
            jax.ShapeDtypeStruct((mlp_rows, width), BF16),
            jax.ShapeDtypeStruct((qkv_rows, width), BF16),
        ],
        in_specs=[VMEM] * 6 + [pick(0, args[6])] + [VMEM] * (len(args) - 7),
        out_specs=[VMEM, VMEM, ANY, ANY],
        scratch_shapes=[
            pltpu.VMEM((rows, width), BF16),
            pltpu.VMEM((qkv_rows, width), BF16),
            pltpu.VMEM((qkv_rows // devices, width), BF16),
        ]
        + key_scratch(n, rows, width)
        + [pltpu.SemaphoreType.DMA((2,))] * 2
        + gather_scratch(n, chips)
        + reduce_scratch(n, chips, qkv_rows, width)
        + gather_scratch(n, chips),
        compiler_params=params(collective_id),
        name="last",
    )(*args)


def unpack_kernel(
    mlp_a, mlp_b, fc1_a, fc1_b, out_a, out_b, q_a, k_a, v_a, q_b, k_b, v_b, small, prior, tg_in, expert_in,
    fc2, fc1, out, qkv, tg, expert, lead_average, norm1, norm2, bias, table, final, head, head_bias, wide, tall,
):
    layer, step = pl.program_id(0), pl.program_id(1)
    width = fc1.shape[2]

    def layer_part(own, sources):
        @pl.when(layer == own)
        def _():
            for source, target, at in sources:
                target[0, :, at] = source[...].astype(F32)

    everything = slice(0, width)
    layer_part(0, [(mlp_a, fc2, everything), (fc1_a, fc1, everything), (out_a, out, everything)])
    layer_part(1, [(mlp_b, fc2, everything), (fc1_b, fc1, everything), (out_b, out, everything)])
    thirds = [slice(i * width, (i + 1) * width) for i in range(3)]
    layer_part(0, [(source, qkv, at) for source, at in zip((q_a, k_a, v_a), thirds)])
    layer_part(1, [(source, qkv, at) for source, at in zip((q_b, k_b, v_b), thirds)])
    tg[...] = tg_in[...]

    @pl.when(jnp.logical_and(layer == 0, step == 0))
    def _():
        rows = small[...].astype(F32)
        expert[...] = expert_in[0:EXPERTS, :]
        table[...] = rows[:LEADS]
        for own in range(2):
            norm1[own : own + 1, :] = rows[ROW_NORM1 + 8 * own : ROW_NORM1 + 8 * own + 1]
            base = ROW_MLP + 8 * own
            norm2[own : own + 1, :] = rows[base : base + 1]
            for part in range(bias.shape[1] // width):
                bias[own : own + 1, part * width : (part + 1) * width] = rows[base + 4 + part : base + 5 + part]
        final[...] = rows[ROW_MLP + 9 : ROW_MLP + 10]
        wide[...] = jnp.zeros_like(wide)
        wide[0:8, :] = rows[ROW_HEAD : ROW_HEAD + 8]
        head[...] = wide[...].T[:, 0:EXPERTS]
        tall[...] = jnp.zeros_like(tall)
        tall[0:8, :] = rows[ROW_HEAD + 8 : ROW_HEAD + 16, 0:LANES]
        tall[8:16, :] = rows[ROW_HEAD + 16 : ROW_HEAD + 24, 0:LANES]
        turned = tall[...].T
        totals = turned[0:LEADS, 0:EXPERTS] / jnp.maximum(turned[0:LEADS, EXPERTS : EXPERTS + 1], 1.0)
        lead_average[...] = 0.5 * prior[...] + 0.5 * totals
        head_bias[...] = turned[0:1, 8 : 8 + EXPERTS]


def unpack(mlp_a, mlp_b, qkv_a, qkv_b, prior, token_grad, expert, hidden):
    rows, width = token_grad.shape
    steps = hidden // width
    slab = width // steps

    def at(own, block, first):
        start = first // block
        if own == 0:
            return pl.BlockSpec((block, width), lambda l, j: (start + jnp.where(l == 0, j, steps - 1), 0))
        return pl.BlockSpec((block, width), lambda l, j: (start + jnp.where(l == 1, j, 0), 0))

    fixed = lambda shape: pl.BlockSpec(shape, lambda l, j: (0,) * len(shape))
    moving = pl.BlockSpec((rows // (2 * steps), width), lambda l, j: (l * steps + j, 0))
    in_specs = [at(own, width, 0) for own in range(2)]
    in_specs += [at(own, width, hidden) for own in range(2)]
    in_specs += [at(own, slab, 2 * hidden) for own in range(2)]
    in_specs += [at(own, slab, part * width) for own in range(2) for part in range(3)]
    in_specs += [pl.BlockSpec((SMALL_ROWS, width), lambda l, j: (3 * width // SMALL_ROWS, 0)), fixed(prior.shape), moving]
    in_specs += [fixed(expert.shape)]
    small_shapes = [
        (EXPERTS, rows), prior.shape, (2, width), (2, width), (2, hidden), (LEADS, width), (1, width),
        (width, EXPERTS), (1, EXPERTS),
    ]
    shapes = [(2, hidden, width), (2, width, hidden), (2, width, width), (2, width, 3 * width)]
    out_specs = [
        pl.BlockSpec((1, width, width), lambda l, j: (l, j, 0)),
        pl.BlockSpec((1, width, width), lambda l, j: (l, 0, j)),
        pl.BlockSpec((1, slab, width), lambda l, j: (l, j, 0)),
        pl.BlockSpec((1, slab, 3 * width), lambda l, j: (l, j, 0)),
        moving,
    ] + [fixed(shape) for shape in small_shapes]
    return pl.pallas_call(
        unpack_kernel,
        grid=(2, steps),
        out_shape=[jax.ShapeDtypeStruct(shape, F32) for shape in shapes]
        + [jax.ShapeDtypeStruct((rows, width), BF16)]
        + [jax.ShapeDtypeStruct(shape, F32) for shape in small_shapes],
        in_specs=in_specs,
        out_specs=out_specs,
        scratch_shapes=[pltpu.VMEM((LANES, width), F32), pltpu.VMEM((LANES, LANES), F32)],
        compiler_params=params(),
        name="unpack",
    )(*([mlp_a, mlp_b] * 3 + [qkv_a] * 3 + [qkv_b] * 3 + [qkv_a, prior, token_grad, expert]))


def on_device(
    tokens, slot_kind, frame_lead, norm1_gain, w_qkv, w_out, norm2_gain, w_fc1, b_fc1, w_fc2,
    lead_table, final_gain, head_w, head_b, lead_prior, gate_cot,
):
    rows, width = tokens.shape[0], tokens.shape[3]
    hidden = w_fc1.shape[2]
    n, devices = lax.axis_size("blk"), lax.axis_size("blk") * lax.axis_size("dp")
    chips = lax.axis_size("dp") // 2
    pad = lambda count: -(-count // (16 * devices)) * 16 * devices
    mlp_rows, qkv_rows = pad(2 * hidden + width), pad(3 * width + SMALL_ROWS)
    flat = lambda x: x.reshape(n * rows, width)
    split = lambda x: x.reshape(n, rows, width)

    h, n1, q, k, v, aux = project(
        n, 0, 0, tokens.reshape(rows, width), gate_cot.reshape(EXPERTS, rows), slot_kind, frame_lead.reshape(1, 2),
        lead_table, norm1_gain, w_qkv,
    )
    k, v = flat(k), flat(v)
    e, ob, li = attend(q, k, v, aux)
    h2, n2, a, gp, h3 = mlp(0, h, ob, w_out, norm2_gain, w_fc1, b_fc1, w_fc2)
    n1b, qb, kb, vb = project(n, 1, 1, h3, norm1_gain, w_qkv)
    kb, vb = flat(kb), flat(vb)
    eb, obb, lib = attend(qb, kb, vb, aux)
    g_mlp_b, small_b, dh2, do, dl, expert, head = turn(
        1, h3, obb, lib, aux, w_out, norm2_gain, w_fc1, b_fc1, w_fc2,
        final_gain[None], head_w, head_b[None], lead_prior, mlp_rows,
    )
    dq, dk, dv, shard = attend_back(n, chips, 2, [((1, 5, 7, 11), ())], qb, kb, vb, eb, do, dl, g_mlp_b)
    g_qkv_b, norm_b, g_mlp_a, small_a, dh2, do, dl, g_mlp_b = between(
        n, chips, 3, qkv_rows, mlp_rows, dq, split(dk), split(dv), n1b, h3, dh2, w_qkv, norm1_gain, gp, h2, ob, li, n2, a,
        w_out, norm2_gain, w_fc1, w_fc2, shard, mlp_rows,
    )
    dq, dk, dv, shard, _, g_qkv_b = attend_back(
        n, chips, 4, [((1, 5, 7, 11), ()), ((1, 3, 4, 6), (8, 9, 10, 11))], q, k, v, e, do, dl, g_mlp_a, g_qkv_b
    )
    token_grad, expert, g_mlp_a, g_qkv_a = last(
        n, chips, 5, qkv_rows, mlp_rows, dq, split(dk), split(dv), n1, h, dh2, w_qkv, norm1_gain, aux, expert, norm_b,
        small_a, small_b, head, shard,
    )
    fc2, fc1, out, qkv, token_grad, expert, lead_average, norm1, norm2, bias, table, final, head, head_bias = unpack(
        g_mlp_a, g_mlp_b, g_qkv_a, g_qkv_b, lead_prior, token_grad, expert, hidden
    )
    return (
        expert[:, :, None, None],
        lead_average,
        token_grad.reshape(rows, 1, 1, width),
        norm1,
        qkv,
        out,
        norm2,
        fc1,
        bias,
        fc2,
        table,
        final.reshape(-1),
        head,
        head_bias.reshape(-1),
    )


def solution(mesh):
    return jax.shard_map(
        on_device,
        mesh=mesh,
        in_specs=(P("blk", "dp", None, None), P("dp", None), P("dp", None, None))
        + (P(),) * 12
        + (P(None, "blk", "dp", None),),
        out_specs=(P(None, "blk", "dp", None), P(), P("blk", "dp", None, None)) + (P(),) * 11,
        check_vma=False,
    )
```

```python
import functools
import math

import jax
import jax.numpy as jnp
from jax import lax
from jax.experimental import pallas as pl
from jax.experimental.pallas import tpu as pltpu
from jax.sharding import PartitionSpec as P

HEAD_DIM = 64
LEADS = 40
LAYERS = 2
EXPERTS = 3
LANES = 128
norm_eps = 1e-06
gelu_in = math.sqrt(2.0 / math.pi)
gelu_cubic = 0.044715
MESH = pl.DeviceIdType.MESH
HIGHEST = lax.Precision.HIGHEST
F32 = jnp.float32
BF16 = jnp.bfloat16
VMEM = pl.BlockSpec(memory_space=pltpu.VMEM)
ANY = pl.BlockSpec(memory_space=pl.ANY)

KIND_ROW, LEAD_ROW = 3, 4
ROW_NORM1, ROW_MLP, ROW_HEAD, SMALL_ROWS = 40, 56, 72, 96


class Late:
    def __init__(self, src, buf, sem):
        self.copy, self.buf, self.waiting = pltpu.make_async_copy(src, buf, sem), buf, True
        self.shape = buf.shape
        self.copy.start()

    def ready(self):
        if self.waiting:
            self.copy.wait()
            self.waiting = False
        return self.buf

    def __getitem__(self, at):
        return self.ready()[at]


class Ship:
    def __init__(self, sems):
        self.sems, self.copies = sems, []

    def __call__(self, src, dst):
        self.copies.append(pltpu.make_async_copy(src, dst, self.sems.at[len(self.copies)]))
        self.copies[-1].start()

    def finish(self):
        for copy in self.copies:
            copy.wait()


def run(kernel, name, collective_id, late, ins, in_specs, out_shape, out_specs, scratch):
    late = [item if isinstance(item, tuple) else (item, None) for item in late]
    count = len(late)

    def body(*refs):
        buffers, sems = refs[len(refs) - count - 1 : -1], refs[-1]
        arriving = [
            Late(ref if layer is None else ref.at[layer], buffer, sems.at[i])
            for i, (ref, buffer, (_, layer)) in enumerate(zip(refs[:count], buffers, late))
        ]
        kernel(arriving, *refs[count : len(refs) - count - 1])

    shape = lambda array, layer: array.shape if layer is None else array.shape[1:]
    return pl.pallas_call(
        body,
        out_shape=out_shape,
        in_specs=[ANY] * count + in_specs,
        out_specs=out_specs,
        scratch_shapes=scratch
        + [pltpu.VMEM(shape(array, layer), array.dtype) for array, layer in late]
        + [pltpu.SemaphoreType.DMA((count,))],
        compiler_params=params(collective_id),
        name=name,
    )(*[array for array, _ in late], *ins)


def params(collective_id=None):
    if collective_id is None:
        return pltpu.CompilerParams(vmem_limit_bytes=60 * 2**20)
    return pltpu.CompilerParams(
        vmem_limit_bytes=60 * 2**20, collective_id=collective_id, has_side_effects=True
    )


def dot(a, b, dims=(1, 0), precision=None):
    return lax.dot_general(
        a, b, (((dims[0],), (dims[1],)), ((), ())), precision=precision, preferred_element_type=F32
    )


def normalize(x):
    centered = x - jnp.mean(x, axis=-1, keepdims=True)
    rstd = lax.rsqrt(jnp.mean(centered * centered, axis=-1, keepdims=True) + norm_eps)
    return centered * rstd, rstd


def normalize_back(dg, xhat, rstd):
    return (
        dg - jnp.mean(dg, axis=-1, keepdims=True) - xhat * jnp.mean(dg * xhat, axis=-1, keepdims=True)
    ) * rstd


def diagonal(shape):
    return lax.broadcasted_iota(jnp.int32, shape, 0) == lax.broadcasted_iota(jnp.int32, shape, 1)


def column_sum(x):
    return jnp.sum(x, axis=0, keepdims=True)


class Place:
    def __init__(self, n):
        self.n = n
        dp, self.b = lax.axis_index("dp"), lax.axis_index("blk")
        self.core, self.e = lax.rem(dp, 2), lax.div(dp, 2)
        half = n // 2
        self.side = lax.div(self.b, half)
        self.moves = self.core != self.side
        far = lax.rem(self.b + half, n)
        self.band = jnp.where(self.moves, far, self.b)
        self.partner = (self.e * 2 + 1 - self.core, far)

    def peer(self, step):
        half = self.n // 2
        band = lax.rem(self.band + step, self.n)
        near = lax.div(band, half) == self.side
        b = jnp.where(near, band, lax.rem(band + half, self.n))
        core = jnp.where(near, self.side, 1 - self.side)
        return (self.e * 2 + core, b)


def signal(sem, device):
    pl.semaphore_signal(sem, inc=1, device_id=device, device_id_type=MESH)


def send(src, dst, ssem, rsem, device):
    return pltpu.make_async_remote_copy(
        src_ref=src, dst_ref=dst, send_sem=ssem, recv_sem=rsem, device_id=device, device_id_type=MESH
    )


def row_step(rows):
    step = 16
    while step * 2 <= 128 and rows % (step * 2) == 0:
        step *= 2
    return step


def add_rows(out, out_at, sources, rows):
    step = row_step(rows)

    def body(i, carry):
        total = 0.0
        for ref, at in sources:
            total = total + ref[pl.ds(pl.multiple_of(at + i * step, 16), step), :].astype(F32)
        out[pl.ds(pl.multiple_of(out_at + i * step, 16), step), :] = total.astype(BF16)
        return carry

    lax.fori_loop(0, rows // step, body, 0)


def sum_sizes(n, chips):
    return [2, n, chips // 4, 4]


class Axes:
    def __init__(self, n, chips):
        dp, b = lax.axis_index("dp"), lax.axis_index("blk")
        core, e = lax.rem(dp, 2), lax.div(dp, 2)
        inner = chips // 4
        slow, fast = lax.div(e, inner), lax.rem(e, inner)
        self.sizes = sum_sizes(n, chips)
        across = lambda i: (dp, i)
        within = lambda i: ((slow * inner + i) * 2 + core, b)
        along = lambda i: ((i * inner + fast) * 2 + core, b)
        self.index = [core, b, fast, slow]
        self.device = [lambda i: (e * 2 + i, b), across, within, along]
        if n == inner:
            swap = core == 1
            pick_one = lambda f, g: lambda i: tuple(jnp.where(swap, y, x) for x, y in zip(f(i), g(i)))
            self.device[1], self.device[2] = pick_one(across, within), pick_one(within, across)
            self.index[1], self.index[2] = jnp.where(swap, fast, b), jnp.where(swap, b, fast)

    def peers(self, phase):
        size = self.sizes[phase]
        for step in range(1, size):
            i = lax.rem(self.index[phase] + step, size)
            yield step, i, self.device[phase](i)

    def greet(self, bar, phases=range(4)):
        met = 0
        for phase in phases:
            for _, _, device in self.peers(phase):
                signal(bar, device)
                met += 1
        return met


class Region:
    def __init__(self, axes, rows):
        self.axes, self.at, self.rows = axes, [0], [rows]
        for phase in range(4):
            self.rows.append(self.rows[-1] // axes.sizes[phase])
            self.at.append(self.at[-1] + axes.index[phase] * self.rows[-1])


class Reduce(Region):
    def __init__(self, axes, total, first, last, src, dst, refs):
        super().__init__(axes, total)
        self.first, self.last, self.src, self.dst = first, last, src, dst
        self.work, *recv, self.ssem, self.rsem, self.lsem = refs
        self.recv = dict(zip(range(first, last + 1), recv))

    def own(self):
        rows = self.rows[self.first + 1]
        at = pl.ds(pl.multiple_of(self.at[self.first + 1] - self.at[self.first], 16), rows)
        return pltpu.make_async_copy(self.src.at[at], self.work, self.lsem.at[0])

    def copies(self, phase):
        rows = self.rows[phase + 1]
        base = self.at[self.first] if phase == self.first else self.at[self.first + 1]
        src = self.src if phase == self.first else self.work
        for step, i, device in self.axes.peers(phase):
            begin = pl.multiple_of(self.at[phase] - base + i * rows, 16)
            at = phase - self.first, step - 1
            yield send(src.at[pl.ds(begin, rows)], self.recv[phase].at[step - 1], self.ssem.at[at], self.rsem.at[at], device)

    def start(self, phase):
        for copy in self.copies(phase):
            copy.start()

    def finish(self, phase):
        if phase == self.first:
            self.own().wait()
        for copy in self.copies(phase):
            copy.wait()
        at = self.at[phase + 1] - self.at[self.first + 1]
        sources = [(self.work, at)] + [(self.recv[phase].at[i], 0) for i in range(self.axes.sizes[phase] - 1)]
        if phase < self.last:
            add_rows(self.work, at, sources, self.rows[phase + 1])
        else:
            add_rows(self.dst, 0, sources, self.rows[phase + 1])

    def finish_start(self, phase):
        self.finish(phase)
        self.start(phase + 1)

    def act(self, phase):
        return functools.partial(self.finish_start if phase < self.last else self.finish, phase)


def rows_after(n, chips, total, phases):
    for size in sum_sizes(n, chips)[:phases]:
        total //= size
    return total


def reduce_scratch(n, chips, total, first, last, width):
    sizes = sum_sizes(n, chips)
    shapes = [pltpu.VMEM((rows_after(n, chips, total, first + 1), width), BF16)]
    for phase in range(first, last + 1):
        shapes.append(pltpu.VMEM((sizes[phase] - 1, rows_after(n, chips, total, phase + 1), width), BF16))
    most = max(sizes[first : last + 1]) - 1
    return shapes + [pltpu.SemaphoreType.DMA((last + 1 - first, most))] * 2 + [pltpu.SemaphoreType.DMA((1,))]


class Gather(Region):
    def __init__(self, axes, total, first, last, src, out, refs):
        super().__init__(axes, total)
        self.first, self.last, self.src, self.out, (self.ssem, self.rsem, self.lsem) = first, last, src, out, refs

    def region(self, phase):
        begin = self.at[phase + 1] - self.at[self.last]
        return self.out.at[pl.ds(pl.multiple_of(begin, 16), self.rows[phase + 1])]

    def own(self):
        return pltpu.make_async_copy(self.src, self.region(self.first), self.lsem.at[0])

    def copies(self, phase):
        src = self.src if phase == self.first else self.region(phase)
        for step, _, device in self.axes.peers(phase):
            at = self.first - phase, step - 1
            yield send(src, self.region(phase), self.ssem.at[at], self.rsem.at[at], device)

    def start(self, phase):
        if phase == self.first:
            self.own().start()
        for copy in self.copies(phase):
            copy.start()

    def finish(self, phase):
        if phase == self.first:
            self.own().wait()
        for copy in self.copies(phase):
            copy.wait()

    def finish_start(self, phase):
        self.finish(phase)
        self.start(phase - 1)

    def act(self, phase):
        return functools.partial(self.finish_start if phase > self.last else self.finish, phase)


def gather_scratch(n, chips, first, last):
    most = max(sum_sizes(n, chips)[last : first + 1]) - 1
    return [pltpu.SemaphoreType.DMA((first + 1 - last, most))] * 2 + [pltpu.SemaphoreType.DMA((1,))]


class Keys:
    def __init__(self, place, whole, bufs, ssem, rsem, lsem):
        self.place, self.whole, self.bufs, self.ssem, self.rsem, self.lsem = place, whole, bufs, ssem, rsem, lsem
        self.copies = []

    def start(self, i, at, kv):
        n = self.place.n
        for part, (buf, whole) in enumerate(zip(self.bufs, self.whole)):
            width = buf.shape[1]
            buf[at, :] = kv[:, part * width : (part + 1) * width]
            self.copies.append(pltpu.make_async_copy(buf.at[at], whole.at[0, at], self.lsem.at[part, i]))
            for step in range(1, n):
                to = step - 1, part, i
                self.copies.append(
                    send(buf.at[at], whole.at[step, at], self.ssem.at[to], self.rsem.at[to], self.place.peer(n - step))
                )
            for copy in self.copies[-n:]:
                copy.start()

    def finish(self):
        for copy in self.copies:
            copy.wait()


def keys_scratch(n, rows, width, blocks):
    return [
        pltpu.VMEM((rows, width), BF16),
        pltpu.VMEM((rows, width), BF16),
        pltpu.SemaphoreType.DMA((n - 1, 2, blocks)),
        pltpu.SemaphoreType.DMA((n - 1, 2, blocks)),
        pltpu.SemaphoreType.DMA((2, blocks)),
    ]


def block_of(rows):
    return min(256, rows // 2)


def project_kernel(
    n, late, tok_in, cot, kind, leads, table, gain, h_out, n1_out, q_out, k_all, v_all, aux_out,
    tok, aux_in, ssem, rsem, kbuf, vbuf, ksem, krsem, lsem,
):
    (w,) = late
    place = Place(n)
    rows, width = kbuf.shape
    block = block_of(rows)
    blocks = rows // block
    bar = pltpu.get_barrier_semaphore()
    for step in range(1, n):
        signal(bar, place.peer(step))

    @pl.when(place.moves)
    def _():
        signal(bar, place.partner)

    for i in range(EXPERTS):
        aux_in[i : i + 1, :] = cot[i]
    kind_one = kind[...].astype(F32)
    lead_one = leads[...].astype(F32)
    first_lead = lead_one[:, 0:1]
    second_lead = jnp.where(kind_one == 1.0, lead_one[:, 1:2], first_lead)
    for row, value in ((KIND_ROW, kind_one), (LEAD_ROW, first_lead), (LEAD_ROW + 1, second_lead)):
        aux_in[row : row + 1, :] = jnp.broadcast_to(value, (1, rows))
    aux_in[LEAD_ROW + 2 :, :] = jnp.zeros((8 - LEAD_ROW - 2, rows), F32)

    @pl.when(place.moves)
    def _():
        pl.semaphore_wait(bar, n)

    @pl.when(jnp.logical_not(place.moves))
    def _():
        pl.semaphore_wait(bar, n - 1)

    swaps = [send(aux_in, aux_out, ssem.at[blocks], rsem.at[blocks], place.partner)]
    stays = []
    for i in range(blocks):
        at = pl.ds(i * block, block)
        swaps.append(send(tok_in.at[at], tok.at[at], ssem.at[i], rsem.at[i], place.partner))
        stays.append(pltpu.make_async_copy(tok_in.at[at], tok.at[at], rsem.at[i]))

    @pl.when(place.moves)
    def _():
        for copy in swaps:
            copy.start()
        swaps[0].wait_recv()

    @pl.when(jnp.logical_not(place.moves))
    def _():
        for copy in stays:
            copy.start()
        aux_out[...] = aux_in[...]

    lead_index = lax.broadcasted_iota(jnp.int32, (table.shape[0], 1), 0).astype(F32)
    lead_rows = []
    for half in range(2):
        lead = aux_out[LEAD_ROW + half : LEAD_ROW + half + 1, 0:1]
        lead_rows.append(column_sum(jnp.where(lead_index == lead, table[...], 0.0)))

    keys = Keys(place, (k_all, v_all), (kbuf, vbuf), ksem, krsem, lsem)
    for i in range(blocks):
        at = pl.ds(i * block, block)

        @pl.when(place.moves)
        def _():
            swaps[1 + i].wait_recv()

        @pl.when(jnp.logical_not(place.moves))
        def _():
            stays[i].wait()

        x = tok[at, :].astype(F32) + lead_rows[i * block // (rows // 2)]
        h_out[at, :] = x
        n1 = (normalize(x)[0] * gain[0:1, :]).astype(BF16)
        n1_out[at, :] = n1
        keys.start(i, at, dot(n1, w[:, width:]).astype(BF16))
        q_out[at, :] = (dot(n1, w[:, :width]) * HEAD_DIM**-0.5).astype(BF16)
    keys.finish()

    @pl.when(place.moves)
    def _():
        for copy in swaps:
            copy.wait_send()


def project(n, collective_id, tokens, cot, kind, leads, table, gain, w):
    rows, width = tokens.shape
    blocks = rows // block_of(rows)
    half = jax.ShapeDtypeStruct((rows, width), BF16)
    whole = jax.ShapeDtypeStruct((n, rows, width), BF16)
    return run(
        functools.partial(project_kernel, n),
        "project",
        collective_id,
        [(w, 0)],
        [tokens, cot, kind, leads, table, gain],
        [ANY] + [VMEM] * 5,
        [jax.ShapeDtypeStruct((rows, width), F32), half, half, whole, whole, jax.ShapeDtypeStruct((8, rows), F32)],
        [VMEM, VMEM, VMEM, ANY, ANY, VMEM],
        [pltpu.VMEM((rows, width), BF16), pltpu.VMEM((8, rows), F32)]
        + [pltpu.SemaphoreType.DMA((blocks + 1,))] * 2
        + keys_scratch(n, rows, width, blocks),
    )


def head_lanes(x, head):
    lane = lax.broadcasted_iota(jnp.int32, x.shape, 1)
    return jnp.where(lane // HEAD_DIM == head, x, jnp.zeros_like(x))


def attend_kernel(band, q_ref, k_ref, v_ref, aux_ref, e_ref, ob_ref, li_ref, vte):
    j = pl.program_id(1)
    keys, queries = e_ref.shape[1:]
    chunk = band // 2
    own_half = lax.rem(j, 2)
    coarse = aux_ref[KIND_ROW : KIND_ROW + 1, 0:1]
    coarse_flag = jnp.max(coarse) > 0.5

    @pl.when(j == 0)
    def _():
        turned = v_ref[...].astype(F32).T
        key_half = lax.rem(lax.broadcasted_iota(jnp.int32, (1, keys), 1) // chunk, 2)
        for half in range(2):
            seen = jnp.where(key_half == half, 1.0, 1.0 - coarse)
            for head in range(2):
                rows = turned[head * HEAD_DIM : (head + 1) * HEAD_DIM, :] * seen
                vte[head, half, :HEAD_DIM, :] = rows.astype(BF16)
                vte[head, half, HEAD_DIM:, :] = jnp.broadcast_to(seen, (HEAD_DIM, keys)).astype(BF16)

    def finish(head, total, norm):
        inverse = 1.0 / norm
        ob_ref[head * HEAD_DIM : (head + 1) * HEAD_DIM, :] = (total * inverse).astype(BF16)
        li_ref[head : head + 1, :] = inverse

    li_ref[...] = jnp.zeros_like(li_ref)
    least, largest = None, None
    for head in range(2):
        e = jnp.exp(dot(k_ref[...], head_lanes(q_ref[...], head), (1, 1))).astype(BF16)
        e_ref[head, :, :] = e
        total = dot(vte[head, own_half], e)
        norm = total[HEAD_DIM : HEAD_DIM + 1, :]
        finish(head, total[:HEAD_DIM, :], norm)
        least = norm if least is None else jnp.minimum(least, norm)
        largest = norm if largest is None else jnp.maximum(largest, norm)

    @pl.when(coarse_flag)
    def _():
        for c in range(keys // (2 * chunk)):
            at = pl.ds(pl.multiple_of((2 * c + 1 - own_half) * chunk, chunk), chunk)
            for head in range(2):
                e_ref[head, at, :] = jnp.zeros((chunk, queries), BF16)

    fits = jnp.logical_and(least > 1e-20, largest < 1e25)

    @pl.when(jnp.min(fits.astype(F32)) < 0.5)
    def _():
        for head in range(2):
            queries_one = head_lanes(q_ref[...], head)

            def scores(c):
                at = pl.ds(pl.multiple_of(c * chunk, chunk), chunk)
                hidden = jnp.logical_and(coarse > 0.5, lax.rem(c, 2) != own_half)
                return at, hidden, jnp.where(hidden, -1e30, dot(k_ref[at, :], queries_one, (1, 1)))

            def highest_step(c, top):
                return jnp.maximum(top, jnp.max(scores(c)[2], axis=0, keepdims=True))

            top = lax.fori_loop(0, keys // chunk, highest_step, jnp.full((1, queries), -1e30, F32))

            def total_step(c, total):
                at, hidden, s = scores(c)
                e = jnp.where(hidden, 0.0, jnp.exp(s - top)).astype(BF16)
                e_ref[head, at, :] = e
                return total + dot(vte[head, own_half, :, at], e)

            total = lax.fori_loop(
                0, keys // chunk, total_step, jnp.zeros((LANES, queries), F32)
            )
            finish(head, total[:HEAD_DIM, :], total[HEAD_DIM : HEAD_DIM + 1, :])


def attend(q, k, v, aux):
    rows, width = q.shape
    keys, queries, pairs = k.shape[0], rows // 2, width // LANES
    return pl.pallas_call(
        functools.partial(attend_kernel, rows),
        grid=(pairs, 2),
        out_shape=[
            jax.ShapeDtypeStruct((2 * pairs, keys, rows), BF16),
            jax.ShapeDtypeStruct((width, rows), BF16),
            jax.ShapeDtypeStruct((8 * pairs, rows), F32),
        ],
        in_specs=[
            pl.BlockSpec((queries, LANES), lambda p, j: (j, p)),
            pl.BlockSpec((keys, LANES), lambda p, j: (0, p)),
            pl.BlockSpec((keys, LANES), lambda p, j: (0, p)),
            pl.BlockSpec(aux.shape, lambda p, j: (0, 0)),
        ],
        out_specs=[
            pl.BlockSpec((2, keys, queries), lambda p, j: (p, 0, j)),
            pl.BlockSpec((LANES, queries), lambda p, j: (p, j)),
            pl.BlockSpec((8, queries), lambda p, j: (p, j)),
        ],
        scratch_shapes=[pltpu.VMEM((2, 2, LANES, keys), BF16)],
        compiler_params=params(),
        name="attend",
    )(q, k, v, aux)


POINTS = 3


class Task:
    def __init__(self, reduces, total, phases, ends, array=None, begin=0):
        self.reduces, self.total, self.phases, self.ends, self.array = reduces, total, phases, ends, array
        self.begin = begin


def attend_back_kernel(n, chips, tasks, *refs):
    q_ref, k_ref, v_ref, e_ref, do_ref, dl_ref = refs[:6]
    refs = refs[6:]
    given = sum(task.array is not None for task in tasks)
    sources, refs = list(refs[:given]), refs[given:]
    dq_ref, dk_ref, dv_ref = refs[:3]
    refs = refs[3:]
    results, refs = refs[: len(tasks)], refs[len(tasks) :]
    kt, vext, dk_sum, dv_sum, rhs = refs[:5]
    refs = refs[5:]
    t = pl.program_id(0) * pl.num_programs(1) + pl.program_id(1)
    keys, queries = e_ref.shape[1:]

    axes = Axes(n, chips)
    bar = pltpu.get_barrier_semaphore()
    schedule = {0: [lambda: pl.semaphore_wait(bar, sum(size - 1 for size in axes.sizes))]}
    reduces = []
    begin = 0
    for index, (task, result) in enumerate(zip(tasks, results)):
        if task.array is None:
            source, begin = results[index - 1], tasks[index - 1].ends[-1]
        else:
            source, begin = sources.pop(0), task.begin
        first, last = task.phases[0], task.phases[-1]
        count = (4 + len(task.phases)) if task.reduces else 3
        scratch, refs = refs[:count], refs[count:]
        if task.reduces:
            move = Reduce(axes, task.total, first, last, source, result, scratch)
            reduces.append(move)
        else:
            move = Gather(axes, task.total, first, last, source, result, scratch)
        schedule.setdefault(begin, []).append(functools.partial(move.start, first))
        for phase, point in zip(task.phases, task.ends):
            schedule.setdefault(point, []).append(move.act(phase))

    def points(part):
        for point in sorted(schedule):
            if point % POINTS == part:

                @pl.when(t == point // POINTS)
                def _():
                    for act in schedule[point]:
                        act()

    @pl.when(t == 0)
    def _():
        axes.greet(bar)
        for reduce in reduces:
            reduce.own().start()

    @pl.when(pl.program_id(1) == 0)
    def _():
        kt[...] = k_ref[...].astype(F32).T.astype(BF16)
        vext[:, :LANES] = v_ref[...]
        vext[:, LANES:] = jnp.ones((keys, LANES), BF16)
        dk_sum[...] = jnp.zeros_like(dk_sum)
        dv_sum[...] = jnp.zeros_like(dv_sum)

    do = do_ref[...].astype(F32)
    row_head = lax.broadcasted_iota(jnp.int32, (LANES, 1), 0) // HEAD_DIM
    for head in range(2):
        rhs[head, :LANES, :] = jnp.where(row_head == head, do, 0.0).astype(BF16)
        rhs[head, LANES : LANES + 16, :] = dl_ref[16 * head : 16 * head + 16, :]
        rhs[head, LANES + 16 :, :] = jnp.zeros((LANES - 16, queries), BF16)
    do_rows = jnp.concatenate([rhs[head, :LANES, :].astype(F32).T.astype(BF16) for head in range(2)], axis=0)
    q_rows = jnp.concatenate([head_lanes(q_ref[...], head) for head in range(2)], axis=0)
    dv_sum[...] += dot(jnp.concatenate([e_ref[0], e_ref[1]], axis=1), do_rows)
    ds, dq = [], []
    for head in range(2):
        ds.append((e_ref[head].astype(F32) * dot(vext[...], rhs[head])).astype(BF16))
        dq.append(dot(kt[...], ds[head])[head * HEAD_DIM : (head + 1) * HEAD_DIM])
        points(head)
    dk_sum[...] += dot(jnp.concatenate(ds, axis=1), q_rows)
    dq_ref[...] = (jnp.concatenate(dq, axis=0) * HEAD_DIM**-0.5).T.astype(BF16)

    @pl.when(pl.program_id(1) == pl.num_programs(1) - 1)
    def _():
        dk_ref[...] = dk_sum[...].astype(BF16)
        dv_ref[...] = dv_sum[...].astype(BF16)

    points(2)


def attend_back(n, chips, collective_id, q, k, v, e, do, dl, tasks):
    rows, width = q.shape
    keys, queries, pairs = k.shape[0], rows // 2, width // LANES
    scratch, results = [], []
    for task in tasks:
        first, last = task.phases[0], task.phases[-1]
        if task.reduces:
            scratch += reduce_scratch(n, chips, task.total, first, last, width)
            height = rows_after(n, chips, task.total, last + 1)
        else:
            scratch += gather_scratch(n, chips, first, last)
            height = rows_after(n, chips, task.total, last)
        results.append(jax.ShapeDtypeStruct((height, width), BF16))
    return pl.pallas_call(
        functools.partial(attend_back_kernel, n, chips, tasks),
        grid=(pairs, 2),
        out_shape=[
            jax.ShapeDtypeStruct((rows, width), BF16),
            jax.ShapeDtypeStruct((keys, width), BF16),
            jax.ShapeDtypeStruct((keys, width), BF16),
        ]
        + results,
        in_specs=[
            pl.BlockSpec((queries, LANES), lambda p, j: (j, p)),
            pl.BlockSpec((keys, LANES), lambda p, j: (0, p)),
            pl.BlockSpec((keys, LANES), lambda p, j: (0, p)),
            pl.BlockSpec((2, keys, queries), lambda p, j: (p, 0, j)),
            pl.BlockSpec((LANES, queries), lambda p, j: (p, j)),
            pl.BlockSpec((32, queries), lambda p, j: (p, j)),
        ]
        + [ANY if task.reduces and task.phases[0] == 0 else VMEM for task in tasks if task.array is not None],
        out_specs=[
            pl.BlockSpec((queries, LANES), lambda p, j: (j, p)),
            pl.BlockSpec((keys, LANES), lambda p, j: (0, p)),
            pl.BlockSpec((keys, LANES), lambda p, j: (0, p)),
        ]
        + [VMEM if task.reduces else ANY for task in tasks],
        scratch_shapes=[
            pltpu.VMEM((LANES, keys), BF16),
            pltpu.VMEM((keys, 2 * LANES), BF16),
            pltpu.VMEM((keys, LANES), F32),
            pltpu.VMEM((keys, LANES), F32),
            pltpu.VMEM((2, 2 * LANES, queries), BF16),
        ]
        + scratch,
        compiler_params=params(collective_id),
        name="attend_back",
    )(q, k, v, e, do, dl, *[task.array for task in tasks if task.array is not None])


def mlp_block(at, h, ob, w_out, gain2, w1, b1, w2, h2_ref, n2_ref, a_ref, gp_ref):
    h2 = h + dot(ob, w_out[...], (0, 0))
    h2_ref[at, :] = h2
    n2 = (normalize(h2)[0] * gain2[...]).astype(BF16)
    n2_ref[at, :] = n2
    u = dot(n2, w1[...]) + b1[...]
    square = u * u
    t = jnp.tanh(gelu_in * u * (1.0 + gelu_cubic * square))
    half = 0.5 + 0.5 * t
    a = (u * half).astype(BF16)
    a_ref[at, :] = a
    slope = half + (0.5 * gelu_in) * u * (1.0 - t * t) * (1.0 + 3.0 * gelu_cubic * square)
    gp_ref[at, :] = slope.astype(BF16)
    return h2 + dot(a, w2[...])


def middle_kernel(
    n, late, gain2, b1, gain1, h2_out, n2_out, a_out, gp_out, h3_out, n1_out, q_out, k_all, v_all,
    h2_ref, n2_ref, a_ref, gp_ref, h3_ref, n1_ref, q_ref, ship_sems, kbuf, vbuf, ksem, krsem, lsem,
):
    h, ob, w_out, w1, w2, w = late
    place = Place(n)
    rows, width = h.shape
    block = block_of(rows)
    bar = pltpu.get_barrier_semaphore()
    for step in range(1, n):
        signal(bar, place.peer(step))
    keys = Keys(place, (k_all, v_all), (kbuf, vbuf), ksem, krsem, lsem)
    ship = Ship(ship_sems)
    gain2, b1 = gain2.at[pl.ds(0, 1)], b1.at[pl.ds(0, 1)]
    pairs = ((h2_ref, h2_out), (n2_ref, n2_out), (a_ref, a_out), (gp_ref, gp_out), (h3_ref, h3_out), (n1_ref, n1_out), (q_ref, q_out))
    for i in range(rows // block):
        at = pl.ds(i * block, block)
        h3 = mlp_block(at, h[at, :], ob[:, at], w_out, gain2, w1, b1, w2, h2_ref, n2_ref, a_ref, gp_ref)
        h3_ref[at, :] = h3
        n1 = (normalize(h3)[0] * gain1[1:2, :]).astype(BF16)
        n1_ref[at, :] = n1
        kv = dot(n1, w[:, width:]).astype(BF16)
        if i == 0:
            pl.semaphore_wait(bar, n - 1)
        keys.start(i, at, kv)
        q_ref[at, :] = (dot(n1, w[:, :width]) * HEAD_DIM**-0.5).astype(BF16)
        for src, dst in pairs:
            ship(src.at[at], dst.at[at])
    keys.finish()
    ship.finish()


def middle(n, collective_id, h, ob, w_out, gain2, w1, b1, w2, gain1, w):
    rows, width = h.shape
    hidden = w1.shape[2]
    blocks = rows // block_of(rows)
    shapes = [
        ((rows, width), F32), ((rows, width), BF16), ((rows, hidden), BF16), ((rows, hidden), BF16), ((rows, width), F32),
        ((rows, width), BF16), ((rows, width), BF16),
    ]
    return run(
        functools.partial(middle_kernel, n),
        "middle",
        collective_id,
        [h, ob, (w_out, 0), (w1, 0), (w2, 0), (w, 1)],
        [gain2, b1, gain1],
        [VMEM] * 3,
        [jax.ShapeDtypeStruct(*shape) for shape in shapes] + [jax.ShapeDtypeStruct((n, rows, width), BF16)] * 2,
        [ANY] * 9,
        [pltpu.VMEM(*shape) for shape in shapes]
        + [pltpu.SemaphoreType.DMA((blocks * len(shapes),))]
        + keys_scratch(n, rows, width, blocks),
    )


def mlp_back_block(at, dh, gp, h2, ob, li, w_out, gain2, w1, w2, dz_ref, du_ref, dy_ref, dh2_ref, do_ref, dl_ref):
    dz = dh.astype(BF16)
    dz_ref[at, :] = dz
    du = (dot(dz, w2[...], (1, 1)) * gp.astype(F32)).astype(BF16)
    du_ref[at, :] = du
    bias_sum = column_sum(du.astype(F32))
    dn2 = dot(du, w1[...], (1, 1))
    xhat, rstd = normalize(h2)
    gain_sum = column_sum(dn2 * xhat)
    dh2 = dh + normalize_back(dn2 * gain2[...], xhat, rstd)
    dh2_ref[at, :] = dh2
    dy = dh2.astype(BF16)
    dy_ref[at, :] = dy
    do = dot(w_out[...], dy, (1, 1))
    product = do * ob.astype(F32)
    for head in range(do.shape[0] // HEAD_DIM):
        rows = slice(head * HEAD_DIM, (head + 1) * HEAD_DIM)
        inverse = li[8 * (head // 2) + head % 2 : 8 * (head // 2) + head % 2 + 1, :]
        do_ref[rows, at] = (do[rows] * inverse).astype(BF16)
        rest = -column_sum(product[rows]) * inverse
        terms = []
        for _ in range(3):
            terms.append(rest.astype(BF16).astype(F32))
            rest = rest - terms[-1]
        row = lax.broadcasted_iota(jnp.int32, (16, 1), 0)
        block = jnp.where(row == 0, terms[0], jnp.where(row == 1, terms[1], jnp.where(row == 2, terms[2], 0.0)))
        dl_ref[16 * head : 16 * head + 16, at] = block.astype(BF16)
    return bias_sum, gain_sum


def weight_sums(g_ref, a, dz, n2, du, ship=None):
    hidden, width = a.shape[1], dz.shape[1]
    g_ref[:hidden, :] = dot(a[...], dz[...], (0, 0)).astype(BF16)
    if ship:
        ship(pl.ds(0, hidden))
    for part in range(hidden // width):
        at = slice(part * width, (part + 1) * width)
        g_ref[hidden + part * width : hidden + (part + 1) * width, :] = dot(n2[...], du[:, at], (0, 0)).astype(BF16)
    if ship:
        ship(pl.ds(hidden, g_ref.shape[0] - hidden))


def out_sums(g_ref, at, ob, dy):
    width = dy.shape[1]
    g_ref[at : at + width, :] = dot(ob[...], dy[...]).astype(BF16)
    if g_ref.shape[0] > at + width:
        g_ref[at + width :, :] = jnp.zeros((g_ref.shape[0] - at - width, width), BF16)


def put_rows(small_ref, row, value, width):
    for part in range(value.shape[1] // width):
        small_ref[row + part : row + part + 1, :] = value[:, part * width : (part + 1) * width]


def back_shapes(rows, width, hidden, grad_rows):
    return [
        jax.ShapeDtypeStruct((grad_rows, width), BF16),
        jax.ShapeDtypeStruct((8, width), F32),
        jax.ShapeDtypeStruct((rows, width), F32),
        jax.ShapeDtypeStruct((width, rows), BF16),
        jax.ShapeDtypeStruct((16 * width // HEAD_DIM, rows), BF16),
    ]


def turn_kernel(
    late, li_ref, aux_ref, gain2, b1, fgain, head_w, head_b, prior_ref,
    g_out, small_ref, dh2_out, do_out, dl_out, expert_ref, head_ref, out_ref,
    g_ref, dh2_ref, do_ref, dl_ref, dz, du, dy, h2_ref, n2_ref, a_ref, gp_ref, wide, tall, ship_sems,
):
    h_ref, ob_ref, w_out, w1, w2 = late
    rows, width = h_ref.shape
    gain2, b1 = gain2.at[pl.ds(1, 1)], b1.at[pl.ds(1, 1)]
    block = rows // 2
    ship = Ship(ship_sems)
    wide[...] = jnp.zeros_like(wide)
    wide[0:EXPERTS, :] = head_w[...]
    hw = wide[...]
    fgain_row = fgain[...].reshape(1, width)
    tall[...] = jnp.ones_like(tall)
    tall[0:EXPERTS, 0:LEADS] = prior_ref[...]
    logp = jnp.log(tall[...])
    tall[...] = jnp.zeros_like(tall)
    tall[0:1, 0:EXPERTS] = head_b[...]
    hb = jnp.sum(jnp.where(diagonal((8, LANES)), tall[0:1, :], 0.0), axis=1, keepdims=True)
    lane = lax.broadcasted_iota(jnp.int32, (8, LANES), 1).astype(F32)
    expert = lax.broadcasted_iota(jnp.int32, (8, 1), 0)
    bias_sum, gain_sum, final_sum, head_sum, hbias_sum, lead_sum = 0.0, 0.0, 0.0, 0.0, 0.0, 0.0
    for i in range(2):
        at = pl.ds(i * block, block)
        h3 = mlp_block(at, h_ref[at, :], ob_ref[:, at], w_out, gain2, w1, b1, w2, h2_ref, n2_ref, a_ref, gp_ref)
        xhat, rstd = normalize(h3)
        nf = xhat * fgain_row
        own_lead = lane == aux_ref[LEAD_ROW + i : LEAD_ROW + i + 1, 0:1]
        prior = jnp.sum(jnp.where(own_lead, logp, 0.0), axis=1, keepdims=True)
        logits = dot(hw, nf, (1, 1), HIGHEST) + hb - prior
        logits = jnp.where(expert < EXPERTS, logits, -1e30)
        power = jnp.exp(logits - jnp.max(logits, axis=0, keepdims=True))
        weights = power / jnp.sum(power, axis=0, keepdims=True)
        expert_ref[:, at] = weights
        counted = jnp.where(expert == EXPERTS, 1.0, weights)
        lead_sum = lead_sum + jnp.where(own_lead, jnp.sum(counted, axis=1, keepdims=True), 0.0)
        cot = jnp.where(expert < EXPERTS, aux_ref[:, at], 0.0)
        dlogits = weights * (cot - jnp.sum(weights * cot, axis=0, keepdims=True))
        head_sum = head_sum + dot(dlogits, nf, (1, 0), HIGHEST)
        hbias_sum = hbias_sum + jnp.sum(dlogits, axis=1, keepdims=True)
        dnf = dot(dlogits, hw, (0, 0), HIGHEST)
        final_sum = final_sum + column_sum(dnf * xhat)
        dh = normalize_back(dnf * fgain_row, xhat, rstd)
        sums = mlp_back_block(
            at, dh, gp_ref[at, :], h2_ref[at, :], ob_ref[:, at], li_ref[:, at], w_out, gain2, w1, w2,
            dz, du, dy, dh2_ref, do_ref, dl_ref,
        )
        bias_sum, gain_sum = bias_sum + sums[0], gain_sum + sums[1]
        ship(dh2_ref.at[at], dh2_out.at[at])
        ship(do_ref.at[:, at], do_out.at[:, at])
        ship(dl_ref.at[:, at], dl_out.at[:, at])
    small_ref[...] = jnp.zeros_like(small_ref)
    put_rows(small_ref, 0, gain_sum, width)
    put_rows(small_ref, 1, final_sum, width)
    put_rows(small_ref, 4, bias_sum, width)
    head_ref[0:8, :] = head_sum
    head_ref[8:16, :] = jnp.zeros((8, width), F32)
    head_ref[8:16, 0:LANES] = lead_sum
    head_ref[16:24, :] = jnp.broadcast_to(hbias_sum, (8, width))
    weight_sums(g_ref, a_ref, dz, n2_ref, du, lambda at: ship(g_ref.at[at], g_out.at[at]))
    out_sums(out_ref, 0, ob_ref, dy)
    ship.finish()


def turn(h, ob, li, aux, w_out, gain2, w1, b1, w2, fgain, head_w, head_b, prior, grad_rows):
    rows, width = h.shape
    hidden = w1.shape[2]
    shapes = back_shapes(rows, width, hidden, grad_rows)
    kept = [shapes[0]] + shapes[2:]
    return run(
        turn_kernel,
        "turn",
        None,
        [h, ob, (w_out, 1), (w1, 1), (w2, 1)],
        [li, aux, gain2, b1, fgain, head_w, head_b, prior],
        [VMEM] * 8,
        shapes
        + [
            jax.ShapeDtypeStruct((8, rows), F32),
            jax.ShapeDtypeStruct((24, width), F32),
            jax.ShapeDtypeStruct((width, width), BF16),
        ],
        [ANY, VMEM, ANY, ANY, ANY, VMEM, VMEM, VMEM],
        [pltpu.VMEM(shape.shape, shape.dtype) for shape in kept]
        + [
            pltpu.VMEM((rows, width), BF16),
            pltpu.VMEM((rows, hidden), BF16),
            pltpu.VMEM((rows, width), BF16),
            pltpu.VMEM((rows, width), F32),
            pltpu.VMEM((rows, width), BF16),
            pltpu.VMEM((rows, hidden), BF16),
            pltpu.VMEM((rows, hidden), BF16),
            pltpu.VMEM((8, width), F32),
            pltpu.VMEM((8, LANES), F32),
            pltpu.SemaphoreType.DMA((8,)),
        ],
    )


class KeyGrads:
    def __init__(self, place, parts, own, recv, dkv, ssem, rsem):
        self.place, self.parts, self.own, self.recv, self.dkv, self.ssem, self.rsem = place, parts, own, recv, dkv, ssem, rsem

    def copies(self):
        for step in range(1, self.place.n):
            for part, src in enumerate(self.parts):
                at = step - 1, part
                yield send(src.at[step], self.recv.at[at], self.ssem.at[at], self.rsem.at[at], self.place.peer(step))

    def start(self):
        for copy in self.copies():
            copy.start()

    def finish(self):
        for copy in self.copies():
            copy.wait()
        width = self.dkv.shape[1] // 2
        for part, own in enumerate(self.own):
            total = own[...].astype(F32)
            for step in range(self.place.n - 1):
                total = total + self.recv[step, part].astype(F32)
            self.dkv[:, part * width : (part + 1) * width] = total.astype(BF16)


def key_scratch(n, rows, width):
    return [
        pltpu.VMEM((n - 1, 2, rows, width), BF16),
        pltpu.VMEM((rows, 2 * width), BF16),
        pltpu.SemaphoreType.DMA((n - 1, 2)),
        pltpu.SemaphoreType.DMA((n - 1, 2)),
    ]


def project_back_block(at, dn1_q, dkv, w, gain_row, h, dh2):
    width = h.shape[1]
    dn1 = dn1_q + dot(dkv[at, :], w[:, width:], (1, 1))
    xhat, rstd = normalize(h[at, :])
    return dh2[at, :] + normalize_back(dn1 * gain_row, xhat, rstd), column_sum(dn1 * xhat)


def key_weight_sums(g_ref, n1, dkv):
    width = n1.shape[1]
    for part in range(2):
        at = slice(part * width, (part + 1) * width)
        g_ref[(part + 1) * width : (part + 2) * width, :] = dot(n1[...], dkv[:, at], (0, 0)).astype(BF16)


def between_kernel(
    n, chips, late, dk, dv, gain1, li_ref, gain2,
    norm_ref, small_ref, g_out, dh2_out, do_out, dl_out, earlier_ref, next_ref,
    gq_ref, g_ref, dh2_ref, do_ref, dl_ref, dz, du, dy, ship_sems, krecv, dkv, ksem, krsem, *refs,
):
    n1, dq, shard, dk_own, dv_own, w, h3, dh2_in, out_b, w2, gp, w1, h2_ref, w_out, ob_ref, a, n2_ref = late
    place, axes = Place(n), Axes(n, chips)
    rows, width = dq.shape
    block = rows // 2
    bar = pltpu.get_barrier_semaphore()
    met = axes.greet(bar)
    for step in range(1, n):
        signal(bar, place.peer(step))
    ship = Ship(ship_sems)
    gq_ref[:width, :] = dot(n1[...], dq[...], (0, 0)).astype(BF16)
    pl.semaphore_wait(bar, met + n - 1)
    keys = KeyGrads(place, (dk, dv), (dk_own, dv_own), krecv, dkv, ksem, krsem)
    keys.start()
    earlier = shard.shape[0] * 2 * n * chips
    gather = Gather(axes, earlier, 3, 2, shard.ready(), earlier_ref, refs[:3])
    reduce = Reduce(axes, gq_ref.shape[0], 0, 1, gq_ref, next_ref, refs[3:])
    gather.start(3)
    dn1_q = [dot(dq[pl.ds(i * block, block), :], w[:, :width], (1, 1)) for i in range(2)]
    keys.finish()
    gain_sum = 0.0
    dh = []
    for i in range(2):
        at = pl.ds(i * block, block)
        dh_one, part = project_back_block(at, dn1_q[i], dkv, w, gain1[1:2, :], h3, dh2_in)
        dh.append(dh_one)
        gain_sum = gain_sum + part
    norm_ref[...] = jnp.broadcast_to(gain_sum, norm_ref.shape)
    key_weight_sums(gq_ref, n1, dkv)
    gq_ref[3 * width : 4 * width, :] = out_b[...]
    if gq_ref.shape[0] > 4 * width:
        gq_ref[4 * width :, :] = jnp.zeros((gq_ref.shape[0] - 4 * width, width), BF16)
    reduce.own().start()
    reduce.start(0)
    gather.finish_start(3)
    bias_sum, gain_sum = 0.0, 0.0
    for i in range(2):
        at = pl.ds(i * block, block)
        sums = mlp_back_block(
            at, dh[i], gp[at, :], h2_ref[at, :], ob_ref[:, at], li_ref[:, at], w_out, gain2.at[pl.ds(0, 1)], w1, w2,
            dz, du, dy, dh2_ref, do_ref, dl_ref,
        )
        bias_sum, gain_sum = bias_sum + sums[0], gain_sum + sums[1]
        if i == 0:
            reduce.finish_start(0)
        ship(dh2_ref.at[at], dh2_out.at[at])
        ship(do_ref.at[:, at], do_out.at[:, at])
        ship(dl_ref.at[:, at], dl_out.at[:, at])
    small_ref[...] = jnp.zeros_like(small_ref)
    put_rows(small_ref, 0, gain_sum, width)
    put_rows(small_ref, 4, bias_sum, width)
    hidden = a.shape[1]
    weight_sums(g_ref, a, dz, n2_ref, du)
    ship(g_ref.at[pl.ds(0, 2 * hidden)], g_out.at[pl.ds(0, 2 * hidden)])
    out_sums(g_ref, 2 * hidden, ob_ref, dy)
    rest = pl.ds(2 * hidden, g_ref.shape[0] - 2 * hidden)
    ship(g_ref.at[rest], g_out.at[rest])
    reduce.finish(1)
    gather.finish(2)
    ship.finish()


def between(n, chips, collective_id, qkv_rows, grad_rows, dq, dk, dv, n1, h3, dh2, w, gain1, gp, h2, ob, li, n2, a, w_out, gain2, w1, w2, out_b, shard):
    rows, width = dq.shape
    hidden = a.shape[1]
    shapes = back_shapes(rows, width, hidden, grad_rows)
    kept = [shapes[0]] + shapes[2:]
    return run(
        functools.partial(between_kernel, n, chips),
        "between",
        collective_id,
        [n1, dq, shard, (dk, 0), (dv, 0), (w, 1), h3, dh2, out_b, (w2, 0), gp, (w1, 0), h2, (w_out, 0), ob, a, n2],
        [dk, dv, gain1, li, gain2],
        [ANY, ANY, VMEM, VMEM, VMEM],
        [
            jax.ShapeDtypeStruct((8, width), F32),
            shapes[1],
            *kept,
            jax.ShapeDtypeStruct((rows_after(n, chips, shard.shape[0] * 2 * n * chips, 2), width), BF16),
            jax.ShapeDtypeStruct((rows_after(n, chips, qkv_rows, 2), width), BF16),
        ],
        [VMEM, VMEM, ANY, ANY, ANY, ANY, ANY, VMEM],
        [pltpu.VMEM((qkv_rows, width), BF16)]
        + [pltpu.VMEM(shape.shape, shape.dtype) for shape in kept]
        + [
            pltpu.VMEM((rows, width), BF16),
            pltpu.VMEM((rows, hidden), BF16),
            pltpu.VMEM((rows, width), BF16),
            pltpu.SemaphoreType.DMA((8,)),
        ]
        + key_scratch(n, rows, width)
        + gather_scratch(n, chips, 3, 2)
        + reduce_scratch(n, chips, qkv_rows, 0, 1, width),
    )


def last_kernel(
    n, chips, late, dk, dv, gain, aux, expert, norm_b, small_a, small_b, head,
    tg_out, ex_out, mlp_ref, middle_ref, sum_ref,
    tg, g_ref, own_shard, krecv, dkv, ksem, krsem, ssem, rsem, *refs,
):
    n1, dq, shard, middle, dk_own, dv_own, w, h, dh2 = late
    place, axes = Place(n), Axes(n, chips)
    rows, width = dq.shape
    block = rows // 2
    bar = pltpu.get_barrier_semaphore()
    met = axes.greet(bar) + n - 1
    for step in range(1, n):
        signal(bar, place.peer(step))

    @pl.when(place.moves)
    def _():
        signal(bar, place.partner)

    g_ref[:width, :] = dot(n1[...], dq[...], (0, 0)).astype(BF16)

    @pl.when(place.moves)
    def _():
        pl.semaphore_wait(bar, met + 1)

    @pl.when(jnp.logical_not(place.moves))
    def _():
        pl.semaphore_wait(bar, met)

    keys = KeyGrads(place, (dk, dv), (dk_own, dv_own), krecv, dkv, ksem, krsem)
    keys.start()
    earlier = Gather(axes, mlp_ref.shape[0], 3, 0, shard.ready(), mlp_ref, refs[:3])
    between = Gather(axes, middle_ref.shape[0], 1, 0, middle.ready(), middle_ref, refs[3:6])
    earlier.start(3)
    between.start(1)
    dn1_q = [dot(dq[pl.ds(i * block, block), :], w[:, :width], (1, 1)) for i in range(2)]
    keys.finish()
    gain_sum = 0.0
    half_sums = []
    for i in range(2):
        at = pl.ds(i * block, block)
        dh, part = project_back_block(at, dn1_q[i], dkv, w, gain[0:1, :], h, dh2)
        gain_sum = gain_sum + part
        half_sums.append(column_sum(dh))
        tg[at, :] = dh.astype(BF16)
    lead_index = lax.broadcasted_iota(jnp.int32, (LEADS, 1), 0).astype(F32)
    table = 0.0
    for half in range(2):
        lead = aux[LEAD_ROW + half : LEAD_ROW + half + 1, 0:1]
        table = table + jnp.where(lead_index == lead, half_sums[half], 0.0)
    at = 3 * width
    for piece in (table, jnp.broadcast_to(gain_sum, (8, width)), norm_b[...], small_a[...], small_b[...], head[...]):
        g_ref[at : at + piece.shape[0], :] = piece.astype(BF16)
        at += piece.shape[0]
    g_ref[at:, :] = jnp.zeros((g_ref.shape[0] - at, width), BF16)
    key_weight_sums(g_ref, n1, dkv)
    reduce = Reduce(axes, g_ref.shape[0], 0, 3, g_ref, own_shard, refs[6:14])
    gather = Gather(axes, g_ref.shape[0], 3, 0, own_shard, sum_ref, refs[14:])
    reduce.own().start()
    reduce.start(0)
    swaps = [
        send(tg, tg_out, ssem.at[0], rsem.at[0], place.partner),
        send(expert, ex_out, ssem.at[1], rsem.at[1], place.partner),
    ]

    @pl.when(place.moves)
    def _():
        for copy in swaps:
            copy.start()

    @pl.when(jnp.logical_not(place.moves))
    def _():
        tg_out[...] = tg[...]
        ex_out[...] = expert[...]

    reduce.finish_start(0)
    earlier.finish_start(3)
    between.finish_start(1)
    reduce.finish_start(1)
    between.finish(0)
    earlier.finish_start(2)
    reduce.finish_start(2)
    earlier.finish_start(1)
    reduce.finish(3)
    gather.start(3)
    earlier.finish(0)
    for phase in (3, 2, 1):
        gather.finish_start(phase)
    gather.finish(0)

    @pl.when(place.moves)
    def _():
        for copy in swaps:
            copy.wait()


def last(
    n, chips, collective_id, rows_a, rows_b, mlp_rows, dq, dk, dv, n1, h, dh2, w, gain, aux, expert, norm_b, small_a, small_b,
    head, shard, middle,
):
    rows, width = dq.shape
    devices = 2 * n * chips
    return run(
        functools.partial(last_kernel, n, chips),
        "last",
        collective_id,
        [n1, dq, shard, middle, (dk, 0), (dv, 0), (w, 0), h, dh2],
        [dk, dv, gain, aux, expert, norm_b, small_a, small_b, head],
        [ANY, ANY] + [VMEM] * 7,
        [
            jax.ShapeDtypeStruct((rows, width), BF16),
            jax.ShapeDtypeStruct((8, rows), F32),
            jax.ShapeDtypeStruct((mlp_rows, width), BF16),
            jax.ShapeDtypeStruct((rows_b, width), BF16),
            jax.ShapeDtypeStruct((rows_a, width), BF16),
        ],
        [VMEM, VMEM, ANY, ANY, ANY],
        [
            pltpu.VMEM((rows, width), BF16),
            pltpu.VMEM((rows_a, width), BF16),
            pltpu.VMEM((rows_a // devices, width), BF16),
        ]
        + key_scratch(n, rows, width)
        + [pltpu.SemaphoreType.DMA((2,))] * 2
        + gather_scratch(n, chips, 3, 0)
        + gather_scratch(n, chips, 1, 0)
        + reduce_scratch(n, chips, rows_a, 0, 3, width)
        + gather_scratch(n, chips, 3, 0),
    )


def unpack_kernel(
    mlp_a, mlp_b, fc1_a, fc1_b, out_a, out_b, q_a, k_a, v_a, q_b, k_b, v_b, small, prior, tg_in, expert_in,
    fc2, fc1, out, qkv, tg, expert, lead_average, norm1, norm2, bias, table, final, head, head_bias,
):
    layer, step = pl.program_id(0), pl.program_id(1)
    width = fc1.shape[2]

    def layer_part(own, sources):
        @pl.when(layer == own)
        def _():
            for source, target, at in sources:
                target[0, :, at] = source[...].astype(F32)

    everything = slice(0, width)
    layer_part(0, [(mlp_a, fc2, everything), (fc1_a, fc1, everything), (out_a, out, everything)])
    layer_part(1, [(mlp_b, fc2, everything), (fc1_b, fc1, everything), (out_b, out, everything)])
    thirds = [slice(i * width, (i + 1) * width) for i in range(3)]
    layer_part(0, [(source, qkv, at) for source, at in zip((q_a, k_a, v_a), thirds)])
    layer_part(1, [(source, qkv, at) for source, at in zip((q_b, k_b, v_b), thirds)])
    tg[...] = tg_in[...]

    @pl.when(jnp.logical_and(layer == 0, step == 0))
    def _():
        rows = small[...].astype(F32)
        for i in range(EXPERTS):
            expert[i] = expert_in[i : i + 1, :]
        table[...] = rows[:LEADS]
        for own in range(2):
            norm1[own : own + 1, :] = rows[ROW_NORM1 + 8 * own : ROW_NORM1 + 8 * own + 1]
            base = ROW_MLP + 8 * own
            norm2[own : own + 1, :] = rows[base : base + 1]
            for part in range(bias.shape[1] // width):
                bias[own : own + 1, part * width : (part + 1) * width] = rows[base + 4 + part : base + 5 + part]
        final[...] = rows[ROW_MLP + 9].reshape(final.shape)
        head[...] = rows[ROW_HEAD : ROW_HEAD + EXPERTS]
        totals = rows[ROW_HEAD + 8 : ROW_HEAD + 16, 0:LEADS]
        means = totals[0:EXPERTS] / jnp.maximum(totals[EXPERTS : EXPERTS + 1], 1.0)
        lead_average[...] = 0.5 * prior[...] + 0.5 * means
        column = rows[ROW_HEAD + 16 : ROW_HEAD + 24, 0:LANES]
        head_bias[...] = column_sum(jnp.where(diagonal((8, LANES)), column, 0.0))[:, 0:EXPERTS]


def unpack(mlp_a, mlp_b, qkv_a, qkv_b, prior, token_grad, expert, hidden):
    rows, width = token_grad.shape
    steps = hidden // width
    slab = width // steps

    def at(own, block, first):
        start = first // block
        if own == 0:
            return pl.BlockSpec((block, width), lambda l, j: (start + jnp.where(l == 0, j, steps - 1), 0))
        return pl.BlockSpec((block, width), lambda l, j: (start + jnp.where(l == 1, j, 0), 0))

    fixed = lambda shape: pl.BlockSpec(shape, lambda l, j: (0,) * len(shape))
    moving = pl.BlockSpec((rows // (2 * steps), width), lambda l, j: (l * steps + j, 0))
    in_specs = [at(own, width, 0) for own in range(2)]
    in_specs += [at(own, width, hidden) for own in range(2)]
    in_specs += [at(0, slab, 2 * hidden), at(1, slab, 3 * width)]
    in_specs += [at(own, slab, part * width) for own in range(2) for part in range(3)]
    in_specs += [pl.BlockSpec((SMALL_ROWS, width), lambda l, j: (3 * width // SMALL_ROWS, 0)), fixed(prior.shape), moving]
    in_specs += [fixed(expert.shape)]
    small_shapes = [
        (EXPERTS, 1, rows), prior.shape, (2, width), (2, width), (2, hidden), (LEADS, width), (width,),
        (EXPERTS, width), (1, EXPERTS),
    ]
    shapes = [(2, hidden, width), (2, width, hidden), (2, width, width), (2, width, 3 * width)]
    out_specs = [
        pl.BlockSpec((1, width, width), lambda l, j: (l, j, 0)),
        pl.BlockSpec((1, width, width), lambda l, j: (l, 0, j)),
        pl.BlockSpec((1, slab, width), lambda l, j: (l, j, 0)),
        pl.BlockSpec((1, slab, 3 * width), lambda l, j: (l, j, 0)),
        moving,
    ] + [fixed(shape) for shape in small_shapes]
    return pl.pallas_call(
        unpack_kernel,
        grid=(2, steps),
        out_shape=[jax.ShapeDtypeStruct(shape, F32) for shape in shapes]
        + [jax.ShapeDtypeStruct((rows, width), BF16)]
        + [jax.ShapeDtypeStruct(shape, F32) for shape in small_shapes],
        in_specs=in_specs,
        out_specs=out_specs,
        compiler_params=params(),
        name="unpack",
    )(*([mlp_a, mlp_b] * 2 + [mlp_a, qkv_b] + [qkv_a] * 3 + [qkv_b] * 3 + [qkv_a, prior, token_grad, expert]))


def on_device(
    tokens, slot_kind, frame_lead, norm1_gain, w_qkv, w_out, norm2_gain, w_fc1, b_fc1, w_fc2,
    lead_table, final_gain, head_w, head_b, lead_prior, gate_cot,
):
    rows, width = tokens.shape[0], tokens.shape[3]
    hidden = w_fc1.shape[2]
    n, devices = lax.axis_size("blk"), lax.axis_size("blk") * lax.axis_size("dp")
    chips = lax.axis_size("dp") // 2
    pad = lambda count: -(-count // (16 * devices)) * 16 * devices
    mlp_rows_a, mlp_rows_b = pad(2 * hidden + width), pad(2 * hidden)
    rows_a, rows_b = pad(3 * width + SMALL_ROWS), pad(4 * width)
    flat = lambda x: x.reshape(n * rows, width)
    split = lambda x: x.reshape(n, rows, width)

    h, n1, q, k, v, aux = project(
        n, 0, tokens.reshape(rows, width), gate_cot.reshape(EXPERTS, 1, rows), slot_kind, frame_lead.reshape(1, 2),
        lead_table, norm1_gain, w_qkv,
    )
    k, v = flat(k), flat(v)
    e, ob, li = attend(q, k, v, aux)
    h2, n2, a, gp, h3, n1b, qb, kb, vb = middle(
        n, 1, h, ob, w_out, norm2_gain, w_fc1, b_fc1, w_fc2, norm1_gain, w_qkv
    )
    kb, vb = flat(kb), flat(vb)
    eb, obb, lib = attend(qb, kb, vb, aux)
    g_mlp_b, small_b, dh2, do, dl, expert, head, out_b = turn(
        h3, obb, lib, aux, w_out, norm2_gain, w_fc1, b_fc1, w_fc2,
        final_gain, head_w.T, head_b[None], lead_prior.T, mlp_rows_b,
    )
    dq, dk, dv, shard = attend_back(
        n, chips, 2, qb, kb, vb, eb, do, dl, [Task(True, mlp_rows_b, (0, 1, 2, 3), (2, 8, 12, 17), g_mlp_b)]
    )
    norm_b, small_a, g_mlp_a, dh2, do, dl, earlier, qkv_part = between(
        n, chips, 3, rows_b, mlp_rows_a, dq, split(dk), split(dv), n1b, h3, dh2, w_qkv, norm1_gain, gp, h2, ob, li, n2, a,
        w_out, norm2_gain, w_fc1, w_fc2, out_b, shard,
    )
    dq, dk, dv, shard, g_mlp_b, _, qkv_part = attend_back(
        n, chips, 4, q, k, v, e, do, dl,
        [
            Task(True, mlp_rows_a, (0, 1, 2, 3), (2, 9, 13, 17), g_mlp_a, begin=0),
            Task(False, mlp_rows_b, (1, 0), (14, 17), earlier, begin=9),
            Task(True, rows_b, (2, 3), (5, 8), qkv_part, begin=0),
            Task(False, rows_b, (3, 2), (12, 16)),
        ],
    )
    token_grad, expert, g_mlp_a, g_qkv_b, g_qkv_a = last(
        n, chips, 5, rows_a, rows_b, mlp_rows_a, dq, split(dk), split(dv), n1, h, dh2, w_qkv, norm1_gain, aux, expert,
        norm_b, small_a, small_b, head, shard, qkv_part,
    )
    fc2, fc1, out, qkv, token_grad, expert, lead_average, norm1, norm2, bias, table, final, head, head_bias = unpack(
        g_mlp_a, g_mlp_b, g_qkv_a, g_qkv_b, lead_prior.T, token_grad, expert, hidden
    )
    return (
        expert.reshape(EXPERTS, rows, 1, 1),
        lead_average.T,
        token_grad.reshape(rows, 1, 1, width),
        norm1,
        qkv,
        out,
        norm2,
        fc1,
        bias,
        fc2,
        table,
        final,
        head.T,
        head_bias.reshape(-1),
    )


def solution(mesh):
    return jax.shard_map(
        on_device,
        mesh=mesh,
        in_specs=(P("blk", "dp", None, None), P("dp", None), P("dp", None, None))
        + (P(),) * 12
        + (P(None, "blk", "dp", None),),
        out_specs=(P(None, "blk", "dp", None), P(), P("blk", "dp", None, None)) + (P(),) * 11,
        check_vma=False,
    )
```

```python
import functools
import math

import jax
import jax.numpy as jnp
from jax import lax
from jax.experimental import pallas as pl
from jax.experimental.pallas import tpu as pltpu
from jax.sharding import PartitionSpec as P

HEAD_DIM = 64
LEADS = 40
LAYERS = 2
EXPERTS = 3
LANES = 128
norm_eps = 1e-06
gelu_in = math.sqrt(2.0 / math.pi)
gelu_cubic = 0.044715
MESH = pl.DeviceIdType.MESH
F32 = jnp.float32
BF16 = jnp.bfloat16
VMEM = pl.BlockSpec(memory_space=pltpu.VMEM)
ANY = pl.BlockSpec(memory_space=pl.ANY)

KIND_ROW, LEAD_ROW = 3, 4
ROW_NORM1, ROW_MLP, ROW_HEAD, SMALL_ROWS = 40, 56, 72, 96


class Late:
    def __init__(self, src, buf, sem):
        self.copy, self.buf, self.waiting = pltpu.make_async_copy(src, buf, sem), buf, True
        self.shape = buf.shape
        self.copy.start()

    def ready(self):
        if self.waiting:
            self.copy.wait()
            self.waiting = False
        return self.buf

    def __getitem__(self, at):
        return self.ready()[at]


class Ship:
    def __init__(self, sems):
        self.sems, self.copies = sems, []

    def __call__(self, src, dst):
        self.copies.append(pltpu.make_async_copy(src, dst, self.sems.at[len(self.copies)]))
        self.copies[-1].start()

    def finish(self):
        for copy in self.copies:
            copy.wait()


def run(kernel, name, collective_id, late, ins, in_specs, out_shape, out_specs, scratch):
    late = [item if isinstance(item, tuple) else (item, None) for item in late]
    count = len(late)

    def body(*refs):
        buffers, sems = refs[len(refs) - count - 1 : -1], refs[-1]
        arriving = [
            Late(ref if layer is None else ref.at[layer], buffer, sems.at[i])
            for i, (ref, buffer, (_, layer)) in enumerate(zip(refs[:count], buffers, late))
        ]
        kernel(arriving, *refs[count : len(refs) - count - 1])

    shape = lambda array, layer: array.shape if layer is None else array.shape[1:]
    return pl.pallas_call(
        body,
        out_shape=out_shape,
        in_specs=[ANY] * count + in_specs,
        out_specs=out_specs,
        scratch_shapes=scratch
        + [pltpu.VMEM(shape(array, layer), array.dtype) for array, layer in late]
        + [pltpu.SemaphoreType.DMA((count,))],
        compiler_params=params(collective_id),
        name=name,
    )(*[array for array, _ in late], *ins)


def params(collective_id=None):
    if collective_id is None:
        return pltpu.CompilerParams(vmem_limit_bytes=60 * 2**20)
    return pltpu.CompilerParams(
        vmem_limit_bytes=60 * 2**20, collective_id=collective_id, has_side_effects=True
    )


def dot(a, b, dims=(1, 0)):
    return lax.dot_general(
        a, b, (((dims[0],), (dims[1],)), ((), ())), preferred_element_type=F32
    )


def dot_split(a, b, dims=(1, 0)):
    a_high, b_high = a.astype(BF16), b.astype(BF16)
    a_low, b_low = (a - a_high.astype(F32)).astype(BF16), (b - b_high.astype(F32)).astype(BF16)
    return dot(a_high, b_high, dims) + (dot(a_high, b_low, dims) + dot(a_low, b_high, dims))


def normalize(x):
    centered = x - jnp.mean(x, axis=-1, keepdims=True)
    rstd = lax.rsqrt(jnp.mean(centered * centered, axis=-1, keepdims=True) + norm_eps)
    return centered * rstd, rstd


def normalize_back(dg, xhat, rstd):
    return (
        dg - jnp.mean(dg, axis=-1, keepdims=True) - xhat * jnp.mean(dg * xhat, axis=-1, keepdims=True)
    ) * rstd


def diagonal(shape):
    return lax.broadcasted_iota(jnp.int32, shape, 0) == lax.broadcasted_iota(jnp.int32, shape, 1)


def column_sum(x):
    return jnp.sum(x, axis=0, keepdims=True)


class Place:
    def __init__(self, n):
        self.n = n
        dp, self.b = lax.axis_index("dp"), lax.axis_index("blk")
        self.core, self.e = lax.rem(dp, 2), lax.div(dp, 2)
        half = n // 2
        self.side = lax.div(self.b, half)
        self.moves = self.core != self.side
        far = lax.rem(self.b + half, n)
        self.band = jnp.where(self.moves, far, self.b)
        self.partner = (self.e * 2 + 1 - self.core, far)

    def peer(self, step):
        half = self.n // 2
        band = lax.rem(self.band + step, self.n)
        near = lax.div(band, half) == self.side
        b = jnp.where(near, band, lax.rem(band + half, self.n))
        core = jnp.where(near, self.side, 1 - self.side)
        return (self.e * 2 + core, b)


def signal(sem, device):
    pl.semaphore_signal(sem, inc=1, device_id=device, device_id_type=MESH)


def send(src, dst, ssem, rsem, device):
    return pltpu.make_async_remote_copy(
        src_ref=src, dst_ref=dst, send_sem=ssem, recv_sem=rsem, device_id=device, device_id_type=MESH
    )


def row_step(rows):
    step = 16
    while step * 2 <= 128 and rows % (step * 2) == 0:
        step *= 2
    return step


def add_rows(out, out_at, sources, rows):
    step = row_step(rows)

    def body(i, carry):
        total = 0.0
        for ref, at in sources:
            total = total + ref[pl.ds(pl.multiple_of(at + i * step, 16), step), :].astype(F32)
        out[pl.ds(pl.multiple_of(out_at + i * step, 16), step), :] = total.astype(BF16)
        return carry

    lax.fori_loop(0, rows // step, body, 0)


def sum_sizes(n, chips):
    return [2, n, chips // 4, 4]


def direct_sizes(n, chips):
    return [2, n * chips]


class Axes:
    def __init__(self, n, chips):
        dp, b = lax.axis_index("dp"), lax.axis_index("blk")
        core, e = lax.rem(dp, 2), lax.div(dp, 2)
        inner = chips // 4
        slow, fast = lax.div(e, inner), lax.rem(e, inner)
        self.sizes = sum_sizes(n, chips)
        across = lambda i: (dp, i)
        within = lambda i: ((slow * inner + i) * 2 + core, b)
        along = lambda i: ((i * inner + fast) * 2 + core, b)
        self.index = [core, b, fast, slow]
        self.device = [lambda i: (e * 2 + i, b), across, within, along]
        if n == inner:
            swap = core == 1
            pick_one = lambda f, g: lambda i: tuple(jnp.where(swap, y, x) for x, y in zip(f(i), g(i)))
            self.device[1], self.device[2] = pick_one(across, within), pick_one(within, across)
            self.index[1], self.index[2] = jnp.where(swap, fast, b), jnp.where(swap, b, fast)

    def peers(self, phase):
        size = self.sizes[phase]
        for step in range(1, size):
            i = lax.rem(self.index[phase] + step, size)
            yield step, i, self.device[phase](i)

    def greet(self, bar):
        met = 0
        for phase in range(len(self.sizes)):
            for _, _, device in self.peers(phase):
                signal(bar, device)
                met += 1
        return met


class DirectAxes(Axes):
    def __init__(self, n, chips):
        dp, b = lax.axis_index("dp"), lax.axis_index("blk")
        core, e = lax.rem(dp, 2), lax.div(dp, 2)
        self.sizes = direct_sizes(n, chips)
        self.index = [core, b * chips + e]
        self.device = [lambda i: (e * 2 + i, b), lambda i: (lax.rem(i, chips) * 2 + core, lax.div(i, chips))]


class Region:
    def __init__(self, axes, rows):
        self.axes, self.at, self.rows = axes, [0], [rows]
        for phase in range(len(axes.sizes)):
            self.rows.append(self.rows[-1] // axes.sizes[phase])
            self.at.append(self.at[-1] + axes.index[phase] * self.rows[-1])


class Reduce(Region):
    def __init__(self, axes, total, first, last, src, dst, refs):
        super().__init__(axes, total)
        self.first, self.last, self.src, self.dst = first, last, src, dst
        self.work, *recv, self.ssem, self.rsem, self.lsem = refs
        self.recv = dict(zip(range(first, last + 1), recv))

    def own(self):
        rows = self.rows[self.first + 1]
        at = pl.ds(pl.multiple_of(self.at[self.first + 1] - self.at[self.first], 16), rows)
        return pltpu.make_async_copy(self.src.at[at], self.work, self.lsem.at[0])

    def copies(self, phase):
        rows = self.rows[phase + 1]
        base = self.at[self.first] if phase == self.first else self.at[self.first + 1]
        src = self.src if phase == self.first else self.work
        for step, i, device in self.axes.peers(phase):
            begin = pl.multiple_of(self.at[phase] - base + i * rows, 16)
            at = phase - self.first, step - 1
            yield send(src.at[pl.ds(begin, rows)], self.recv[phase].at[step - 1], self.ssem.at[at], self.rsem.at[at], device)

    def start(self, phase):
        for copy in self.copies(phase):
            copy.start()

    def finish(self, phase):
        if phase == self.first:
            self.own().wait()
        for copy in self.copies(phase):
            copy.wait()
        at = self.at[phase + 1] - self.at[self.first + 1]
        sources = [(self.work, at)] + [(self.recv[phase].at[i], 0) for i in range(self.axes.sizes[phase] - 1)]
        if phase < self.last:
            add_rows(self.work, at, sources, self.rows[phase + 1])
        else:
            add_rows(self.dst, 0, sources, self.rows[phase + 1])

    def finish_start(self, phase):
        self.finish(phase)
        self.start(phase + 1)

    def act(self, phase):
        return functools.partial(self.finish_start if phase < self.last else self.finish, phase)


def rows_after(sizes, total, phases):
    for size in sizes[:phases]:
        total //= size
    return total


def reduce_scratch(sizes, total, first, last, width):
    shapes = [pltpu.VMEM((rows_after(sizes, total, first + 1), width), BF16)]
    for phase in range(first, last + 1):
        shapes.append(pltpu.VMEM((sizes[phase] - 1, rows_after(sizes, total, phase + 1), width), BF16))
    most = max(sizes[first : last + 1]) - 1
    return shapes + [pltpu.SemaphoreType.DMA((last + 1 - first, most))] * 2 + [pltpu.SemaphoreType.DMA((1,))]


class Gather(Region):
    def __init__(self, axes, total, first, last, src, out, refs):
        super().__init__(axes, total)
        self.first, self.last, self.src, self.out, (self.ssem, self.rsem, self.lsem) = first, last, src, out, refs

    def region(self, phase):
        begin = self.at[phase + 1] - self.at[self.last]
        return self.out.at[pl.ds(pl.multiple_of(begin, 16), self.rows[phase + 1])]

    def own(self):
        return pltpu.make_async_copy(self.src, self.region(self.first), self.lsem.at[0])

    def copies(self, phase):
        src = self.src if phase == self.first else self.region(phase)
        for step, _, device in self.axes.peers(phase):
            at = self.first - phase, step - 1
            yield send(src, self.region(phase), self.ssem.at[at], self.rsem.at[at], device)

    def start(self, phase):
        if phase == self.first:
            self.own().start()
        for copy in self.copies(phase):
            copy.start()

    def finish(self, phase):
        if phase == self.first:
            self.own().wait()
        for copy in self.copies(phase):
            copy.wait()

    def finish_start(self, phase):
        self.finish(phase)
        self.start(phase - 1)

    def act(self, phase):
        return functools.partial(self.finish_start if phase > self.last else self.finish, phase)


class Spread(Gather):
    def __init__(self, axes, direct, total, src, out, refs):
        super().__init__(axes, total, 1, 0, src, out, refs)
        self.direct = direct

    def region(self, phase):
        which = 4 if phase == 1 else 1
        return self.out.at[pl.ds(pl.multiple_of(self.at[which], 16), self.rows[which])]

    def copies(self, phase):
        src = self.src if phase == 1 else self.region(0)
        for step, _, device in self.direct.peers(phase):
            at = 1 - phase, step - 1
            yield send(src, self.region(phase), self.ssem.at[at], self.rsem.at[at], device)


def gather_scratch(sizes, first, last):
    most = max(sizes[last : first + 1]) - 1
    return [pltpu.SemaphoreType.DMA((first + 1 - last, most))] * 2 + [pltpu.SemaphoreType.DMA((1,))]


class Keys:
    def __init__(self, place, whole, bufs, ssem, rsem, lsem):
        self.place, self.whole, self.bufs, self.ssem, self.rsem, self.lsem = place, whole, bufs, ssem, rsem, lsem
        self.copies = []

    def start(self, i, at, kv):
        n = self.place.n
        for part, (buf, whole) in enumerate(zip(self.bufs, self.whole)):
            width = buf.shape[1]
            buf[at, :] = kv[:, part * width : (part + 1) * width]
            self.copies.append(pltpu.make_async_copy(buf.at[at], whole.at[0, at], self.lsem.at[part, i]))
            for step in range(1, n):
                to = step - 1, part, i
                self.copies.append(
                    send(buf.at[at], whole.at[step, at], self.ssem.at[to], self.rsem.at[to], self.place.peer(n - step))
                )
            for copy in self.copies[-n:]:
                copy.start()

    def finish(self):
        for copy in self.copies:
            copy.wait()


def keys_scratch(n, rows, width, blocks):
    return [
        pltpu.VMEM((rows, width), BF16),
        pltpu.VMEM((rows, width), BF16),
        pltpu.SemaphoreType.DMA((n - 1, 2, blocks)),
        pltpu.SemaphoreType.DMA((n - 1, 2, blocks)),
        pltpu.SemaphoreType.DMA((2, blocks)),
    ]


def block_of(rows):
    return min(256, rows // 2)


def project_kernel(
    n, late, tok_in, cot, kind, leads, table, gain, h_out, n1_out, q_out, k_all, v_all, aux_out,
    tok, aux_in, ssem, rsem, kbuf, vbuf, ksem, krsem, lsem,
):
    (w,) = late
    place = Place(n)
    rows, width = kbuf.shape
    block = block_of(rows)
    blocks = rows // block
    bar = pltpu.get_barrier_semaphore()
    for step in range(1, n):
        signal(bar, place.peer(step))

    @pl.when(place.moves)
    def _():
        signal(bar, place.partner)

    for i in range(EXPERTS):
        aux_in[i : i + 1, :] = cot[i]
    kind_one = kind[...].astype(F32)
    lead_one = leads[...].astype(F32)
    first_lead = lead_one[:, 0:1]
    second_lead = jnp.where(kind_one == 1.0, lead_one[:, 1:2], first_lead)
    for row, value in ((KIND_ROW, kind_one), (LEAD_ROW, first_lead), (LEAD_ROW + 1, second_lead)):
        aux_in[row : row + 1, :] = jnp.broadcast_to(value, (1, rows))
    aux_in[LEAD_ROW + 2 :, :] = jnp.zeros((8 - LEAD_ROW - 2, rows), F32)

    @pl.when(place.moves)
    def _():
        pl.semaphore_wait(bar, n)

    @pl.when(jnp.logical_not(place.moves))
    def _():
        pl.semaphore_wait(bar, n - 1)

    swaps = [send(aux_in, aux_out, ssem.at[blocks], rsem.at[blocks], place.partner)]
    stays = []
    for i in range(blocks):
        at = pl.ds(i * block, block)
        swaps.append(send(tok_in.at[at], tok.at[at], ssem.at[i], rsem.at[i], place.partner))
        stays.append(pltpu.make_async_copy(tok_in.at[at], tok.at[at], rsem.at[i]))

    @pl.when(place.moves)
    def _():
        for copy in swaps:
            copy.start()
        swaps[0].wait_recv()

    @pl.when(jnp.logical_not(place.moves))
    def _():
        for copy in stays:
            copy.start()
        aux_out[...] = aux_in[...]

    lead_index = lax.broadcasted_iota(jnp.int32, (table.shape[0], 1), 0).astype(F32)
    lead_rows = []
    for half in range(2):
        lead = aux_out[LEAD_ROW + half : LEAD_ROW + half + 1, 0:1]
        lead_rows.append(column_sum(jnp.where(lead_index == lead, table[...], 0.0)))

    keys = Keys(place, (k_all, v_all), (kbuf, vbuf), ksem, krsem, lsem)
    for i in range(blocks):
        at = pl.ds(i * block, block)

        @pl.when(place.moves)
        def _():
            swaps[1 + i].wait_recv()

        @pl.when(jnp.logical_not(place.moves))
        def _():
            stays[i].wait()

        x = tok[at, :].astype(F32) + lead_rows[i * block // (rows // 2)]
        h_out[at, :] = x
        n1 = (normalize(x)[0] * gain[0:1, :]).astype(BF16)
        n1_out[at, :] = n1
        keys.start(i, at, dot(n1, w[:, width:]).astype(BF16))
        q_out[at, :] = (dot(n1, w[:, :width]) * HEAD_DIM**-0.5).astype(BF16)
    keys.finish()

    @pl.when(place.moves)
    def _():
        for copy in swaps:
            copy.wait_send()


def project(n, collective_id, tokens, cot, kind, leads, table, gain, w):
    rows, width = tokens.shape
    blocks = rows // block_of(rows)
    half = jax.ShapeDtypeStruct((rows, width), BF16)
    whole = jax.ShapeDtypeStruct((n, rows, width), BF16)
    return run(
        functools.partial(project_kernel, n),
        "project",
        collective_id,
        [(w, 0)],
        [tokens, cot, kind, leads, table, gain],
        [ANY] + [VMEM] * 5,
        [jax.ShapeDtypeStruct((rows, width), F32), half, half, whole, whole, jax.ShapeDtypeStruct((8, rows), F32)],
        [VMEM, VMEM, VMEM, ANY, ANY, VMEM],
        [pltpu.VMEM((rows, width), BF16), pltpu.VMEM((8, rows), F32)]
        + [pltpu.SemaphoreType.DMA((blocks + 1,))] * 2
        + keys_scratch(n, rows, width, blocks),
    )


def head_lanes(x, head):
    lane = lax.broadcasted_iota(jnp.int32, x.shape, 1)
    return jnp.where(lane // HEAD_DIM == head, x, jnp.zeros_like(x))


def attend_kernel(band, q_ref, k_ref, v_ref, aux_ref, e_ref, ob_ref, li_ref, vte):
    j = pl.program_id(1)
    keys, queries = e_ref.shape[1:]
    chunk = band // 2
    own_half = lax.rem(j, 2)
    coarse = aux_ref[KIND_ROW : KIND_ROW + 1, 0:1]
    coarse_flag = jnp.max(coarse) > 0.5

    @pl.when(j == 0)
    def _():
        turned = v_ref[...].astype(F32).T
        key_half = lax.rem(lax.broadcasted_iota(jnp.int32, (1, keys), 1) // chunk, 2)
        for half in range(2):
            seen = jnp.where(key_half == half, 1.0, 1.0 - coarse)
            for head in range(2):
                rows = turned[head * HEAD_DIM : (head + 1) * HEAD_DIM, :] * seen
                vte[head, half, :HEAD_DIM, :] = rows.astype(BF16)
                vte[head, half, HEAD_DIM:, :] = jnp.broadcast_to(seen, (HEAD_DIM, keys)).astype(BF16)

    def finish(head, total, norm):
        inverse = 1.0 / norm
        ob_ref[head * HEAD_DIM : (head + 1) * HEAD_DIM, :] = (total * inverse).astype(BF16)
        li_ref[head : head + 1, :] = inverse

    li_ref[...] = jnp.zeros_like(li_ref)
    least, largest = None, None
    for head in range(2):
        e = jnp.exp(dot(k_ref[...], head_lanes(q_ref[...], head), (1, 1))).astype(BF16)
        e_ref[head, :, :] = e
        total = dot(vte[head, own_half], e)
        norm = total[HEAD_DIM : HEAD_DIM + 1, :]
        finish(head, total[:HEAD_DIM, :], norm)
        least = norm if least is None else jnp.minimum(least, norm)
        largest = norm if largest is None else jnp.maximum(largest, norm)

    @pl.when(coarse_flag)
    def _():
        for c in range(keys // (2 * chunk)):
            at = pl.ds(pl.multiple_of((2 * c + 1 - own_half) * chunk, chunk), chunk)
            for head in range(2):
                e_ref[head, at, :] = jnp.zeros((chunk, queries), BF16)

    fits = jnp.logical_and(least > 1e-20, largest < 1e25)

    @pl.when(jnp.min(fits.astype(F32)) < 0.5)
    def _():
        for head in range(2):
            queries_one = head_lanes(q_ref[...], head)

            def scores(c):
                at = pl.ds(pl.multiple_of(c * chunk, chunk), chunk)
                hidden = jnp.logical_and(coarse > 0.5, lax.rem(c, 2) != own_half)
                return at, hidden, jnp.where(hidden, -1e30, dot(k_ref[at, :], queries_one, (1, 1)))

            def highest_step(c, top):
                return jnp.maximum(top, jnp.max(scores(c)[2], axis=0, keepdims=True))

            top = lax.fori_loop(0, keys // chunk, highest_step, jnp.full((1, queries), -1e30, F32))

            def total_step(c, total):
                at, hidden, s = scores(c)
                e = jnp.where(hidden, 0.0, jnp.exp(s - top)).astype(BF16)
                e_ref[head, at, :] = e
                return total + dot(vte[head, own_half, :, at], e)

            total = lax.fori_loop(
                0, keys // chunk, total_step, jnp.zeros((LANES, queries), F32)
            )
            finish(head, total[:HEAD_DIM, :], total[HEAD_DIM : HEAD_DIM + 1, :])


def attend(q, k, v, aux):
    rows, width = q.shape
    keys, queries, pairs = k.shape[0], rows // 2, width // LANES
    return pl.pallas_call(
        functools.partial(attend_kernel, rows),
        grid=(pairs, 2),
        out_shape=[
            jax.ShapeDtypeStruct((2 * pairs, keys, rows), BF16),
            jax.ShapeDtypeStruct((width, rows), BF16),
            jax.ShapeDtypeStruct((8 * pairs, rows), F32),
        ],
        in_specs=[
            pl.BlockSpec((queries, LANES), lambda p, j: (j, p)),
            pl.BlockSpec((keys, LANES), lambda p, j: (0, p)),
            pl.BlockSpec((keys, LANES), lambda p, j: (0, p)),
            pl.BlockSpec(aux.shape, lambda p, j: (0, 0)),
        ],
        out_specs=[
            pl.BlockSpec((2, keys, queries), lambda p, j: (p, 0, j)),
            pl.BlockSpec((LANES, queries), lambda p, j: (p, j)),
            pl.BlockSpec((8, queries), lambda p, j: (p, j)),
        ],
        scratch_shapes=[pltpu.VMEM((2, 2, LANES, keys), BF16)],
        compiler_params=params(),
        name="attend",
    )(q, k, v, aux)


POINT_TIMES = (1.1, 2.2, 2.9, 3.5, 4.2, 4.9)
POINTS = len(POINT_TIMES)


def point(time):
    step = min(int(time / POINT_TIMES[-1]), 5)
    rest = time - step * POINT_TIMES[-1]
    return step * POINTS + next((i for i, end in enumerate(POINT_TIMES) if end >= rest - 0.05), POINTS - 1)


class Task:
    def __init__(self, reduces, total, phases, ends, array=None, begin=0.0):
        self.reduces, self.total, self.phases, self.array = reduces, total, phases, array
        self.ends, self.begin = [point(time) for time in ends], point(begin)


class Early:
    def __init__(self, n1, total, points):
        self.n1, self.total, self.points = n1, total, [point(time) for time in points]

    def shapes(self, n, rows, width, sizes):
        done = width - LANES
        outs = [((rows, done), BF16), ((rows, done), BF16), ((rows_after(sizes, self.total, 2), width), BF16)]
        pairs = done // LANES
        scratch = [
            pltpu.VMEM((rows, width), BF16),
            pltpu.VMEM((pairs, rows, LANES), BF16),
            pltpu.VMEM((pairs, 2, n, rows, LANES), BF16),
            pltpu.VMEM((pairs, 2, n - 1, rows, LANES), BF16),
            pltpu.VMEM((self.total, width), BF16),
            pltpu.SemaphoreType.DMA((1,)),
            pltpu.SemaphoreType.DMA((pairs, 2, n - 1)),
            pltpu.SemaphoreType.DMA((pairs, 2, n - 1)),
        ]
        return outs, scratch + reduce_scratch(sizes, self.total, 0, 1, width)

    def bind(self, axes, place, n1_ref, outs, refs):
        self.place = place
        self.done, result = outs[:2], outs[2]
        self.n1_buf, self.dq, self.parts, self.recv, self.g, n1_sem, self.ssem, self.rsem = refs[:8]
        self.reduce = Reduce(axes, self.total, 0, 1, self.g, result, refs[8:])
        self.fetch = pltpu.make_async_copy(n1_ref, self.n1_buf, n1_sem.at[0])

    def copies(self, pair):
        for step in range(1, self.place.n):
            for part in range(2):
                at = pair, part, step - 1
                yield send(
                    self.parts.at[pair, part, step], self.recv.at[at], self.ssem.at[at], self.rsem.at[at], self.place.peer(step)
                )

    def start(self, pair, dk, dv):
        for part, total in enumerate((dk, dv)):
            self.parts[pair, part] = total.reshape(self.parts.shape[2:]).astype(BF16)
        for copy in self.copies(pair):
            copy.start()

    def finish(self, pair):
        if pair == 0:
            self.fetch.wait()
        for copy in self.copies(pair):
            copy.wait()
        own = [self.dq[pair]]
        for part in range(2):
            total = self.parts[pair, part, 0].astype(F32)
            for step in range(self.place.n - 1):
                total = total + self.recv[pair, part, step].astype(F32)
            own.append(total.astype(BF16))
            self.done[part][:, pair * LANES : (pair + 1) * LANES] = own[-1]
        width = self.n1_buf.shape[1]
        put = dot(self.n1_buf[...], jnp.concatenate(own, axis=1), (0, 0)).astype(BF16)
        self.g[pair * width : (pair + 1) * width, :] = put
        if pair == self.dq.shape[0] - 1:
            end = (pair + 1) * width
            if self.total > end:
                self.g[end:, :] = jnp.zeros((self.total - end, width), BF16)
            self.reduce.own().start()
            self.reduce.start(0)

    def schedule(self):
        pairs = self.dq.shape[0]
        acts = [functools.partial(self.finish, pair) for pair in range(pairs)] + [self.reduce.act(0), self.reduce.act(1)]
        return zip(self.points, acts)


def attend_back_kernel(n, chips, tasks, early, *refs):
    q_ref, k_ref, v_ref, e_ref, do_ref, dl_ref = refs[:6]
    refs = refs[6:]
    if early:
        n1_ref, refs = refs[0], refs[1:]
    given = sum(task.array is not None for task in tasks)
    sources, refs = list(refs[:given]), refs[given:]
    dq_ref, dk_ref, dv_ref = refs[:3]
    refs = refs[3:]
    if early:
        early_outs, refs = refs[:3], refs[3:]
    results, refs = refs[: len(tasks)], refs[len(tasks) :]
    kt, vext, dk_sum, dv_sum, rhs = refs[:5]
    refs = refs[5:]
    t = pl.program_id(0) * pl.num_programs(1) + pl.program_id(1)
    keys, queries = e_ref.shape[1:]

    axes = Axes(n, chips)
    bar = pltpu.get_barrier_semaphore()
    met = sum(size - 1 for size in axes.sizes) + (n - 1 if early else 0)
    schedule = {0: [lambda: pl.semaphore_wait(bar, met)]}
    reduces = []
    begin = 0
    if early:
        place = Place(n)
        early.bind(axes, place, n1_ref, early_outs, refs[:14])
        refs = refs[14:]
        for end, act in early.schedule():
            schedule.setdefault(end, []).append(act)
    for index, (task, result) in enumerate(zip(tasks, results)):
        if task.array is None:
            source, begin = results[index - 1], tasks[index - 1].ends[-1]
        else:
            source, begin = sources.pop(0), task.begin
        first, last = task.phases[0], task.phases[-1]
        count = (4 + len(task.phases)) if task.reduces else 3
        scratch, refs = refs[:count], refs[count:]
        if task.reduces:
            move = Reduce(axes, task.total, first, last, source, result, scratch)
            reduces.append(move)
        else:
            move = Gather(axes, task.total, first, last, source, result, scratch)
        schedule.setdefault(begin, []).append(functools.partial(move.start, first))
        for phase, end in zip(task.phases, task.ends):
            schedule.setdefault(end, []).append(move.act(phase))

    def points(part):
        for place_of in sorted(schedule):
            if place_of % POINTS == part:

                @pl.when(t == place_of // POINTS)
                def _():
                    for act in schedule[place_of]:
                        act()

    @pl.when(t == 0)
    def _():
        axes.greet(bar)
        if early:
            for step in range(1, n):
                signal(bar, place.peer(step))
            early.fetch.start()
        for reduce in reduces:
            reduce.own().start()

    @pl.when(pl.program_id(1) == 0)
    def _():
        kt[...] = k_ref[...].astype(F32).T.astype(BF16)
        vext[:, :LANES] = v_ref[...]
        vext[:, LANES:] = jnp.ones((keys, LANES), BF16)
        dk_sum[...] = jnp.zeros_like(dk_sum)
        dv_sum[...] = jnp.zeros_like(dv_sum)

    do = do_ref[...].astype(F32)
    row_head = lax.broadcasted_iota(jnp.int32, (LANES, 1), 0) // HEAD_DIM
    for head in range(2):
        rhs[head, :LANES, :] = jnp.where(row_head == head, do, 0.0).astype(BF16)
        rhs[head, LANES : LANES + 16, :] = dl_ref[16 * head : 16 * head + 16, :]
        rhs[head, LANES + 16 :, :] = jnp.zeros((LANES - 16, queries), BF16)
    do_rows = jnp.concatenate([rhs[head, :LANES, :].astype(F32).T.astype(BF16) for head in range(2)], axis=0)
    q_rows = jnp.concatenate([head_lanes(q_ref[...], head) for head in range(2)], axis=0)
    ds, dq = [], []
    for head in range(2):
        ds.append((e_ref[head].astype(F32) * dot(vext[...], rhs[head])).astype(BF16))
        dq.append(dot(kt[...], ds[head])[head * HEAD_DIM : (head + 1) * HEAD_DIM])
        points(head)
    halves = [pl.ds(0, keys // 2), pl.ds(keys // 2, keys // 2)]
    for part, at in enumerate(halves):
        dv_sum[at, :] += dot(jnp.concatenate([e_ref[0, at, :], e_ref[1, at, :]], axis=1), do_rows)
        points(2 + part)
    ds = jnp.concatenate(ds, axis=1)
    for part, at in enumerate(halves):
        dk_sum[at, :] += dot(ds[part * (keys // 2) : (part + 1) * (keys // 2)], q_rows)
        if part == 0:
            points(4)
    dq_rows = (jnp.concatenate(dq, axis=0) * HEAD_DIM**-0.5).T.astype(BF16)
    dq_ref[...] = dq_rows
    whole_pair = pl.program_id(1) == pl.num_programs(1) - 1
    if early:
        pair = pl.program_id(0)

        @pl.when(pair < pl.num_programs(0) - 1)
        def _():
            early.dq[pair, pl.ds(pl.multiple_of(pl.program_id(1) * queries, 16), queries), :] = dq_rows

        @pl.when(jnp.logical_and(pair < pl.num_programs(0) - 1, whole_pair))
        def _():
            early.start(pair, dk_sum[...], dv_sum[...])

        whole_pair = jnp.logical_and(pair == pl.num_programs(0) - 1, whole_pair)

    @pl.when(whole_pair)
    def _():
        dk_ref[...] = dk_sum[...].astype(BF16)
        dv_ref[...] = dv_sum[...].astype(BF16)

    points(5)


def attend_back(n, chips, collective_id, q, k, v, e, do, dl, tasks, early=None):
    sizes = sum_sizes(n, chips)
    rows, width = q.shape
    keys, queries, pairs = k.shape[0], rows // 2, width // LANES
    scratch, results = [], []
    for task in tasks:
        first, last = task.phases[0], task.phases[-1]
        if task.reduces:
            scratch += reduce_scratch(sizes, task.total, first, last, width)
            height = rows_after(sizes, task.total, last + 1)
        else:
            scratch += gather_scratch(sizes, first, last)
            height = rows_after(sizes, task.total, last)
        results.append(jax.ShapeDtypeStruct((height, width), BF16))
    key_width, key_spec = width, pl.BlockSpec((keys, LANES), lambda p, j: (0, p))
    early_outs = []
    if early:
        key_width, key_spec = LANES, pl.BlockSpec((keys, LANES), lambda p, j: (0, 0))
        outs, early_scratch = early.shapes(n, rows, width, sizes)
        early_outs = [jax.ShapeDtypeStruct(*out) for out in outs]
        scratch = early_scratch + scratch
    return pl.pallas_call(
        functools.partial(attend_back_kernel, n, chips, tasks, early),
        grid=(pairs, 2),
        out_shape=[
            jax.ShapeDtypeStruct((rows, width), BF16),
            jax.ShapeDtypeStruct((keys, key_width), BF16),
            jax.ShapeDtypeStruct((keys, key_width), BF16),
        ]
        + early_outs
        + results,
        in_specs=[
            pl.BlockSpec((queries, LANES), lambda p, j: (j, p)),
            pl.BlockSpec((keys, LANES), lambda p, j: (0, p)),
            pl.BlockSpec((keys, LANES), lambda p, j: (0, p)),
            pl.BlockSpec((2, keys, queries), lambda p, j: (p, 0, j)),
            pl.BlockSpec((LANES, queries), lambda p, j: (p, j)),
            pl.BlockSpec((32, queries), lambda p, j: (p, j)),
        ]
        + [ANY] * (1 if early else 0)
        + [ANY if task.reduces and task.phases[0] == 0 else VMEM for task in tasks if task.array is not None],
        out_specs=[
            pl.BlockSpec((queries, LANES), lambda p, j: (j, p)),
            key_spec,
            key_spec,
        ]
        + [VMEM] * len(early_outs)
        + [VMEM if task.reduces else ANY for task in tasks],
        scratch_shapes=[
            pltpu.VMEM((LANES, keys), BF16),
            pltpu.VMEM((keys, 2 * LANES), BF16),
            pltpu.VMEM((keys, LANES), F32),
            pltpu.VMEM((keys, LANES), F32),
            pltpu.VMEM((2, 2 * LANES, queries), BF16),
        ]
        + scratch,
        compiler_params=params(collective_id),
        name="attend_back",
    )(q, k, v, e, do, dl, *([early.n1] if early else []), *[task.array for task in tasks if task.array is not None])


def mlp_block(at, h, ob, w_out, gain2, w1, b1, w2, h2_ref, n2_ref, a_ref, gp_ref):
    h2 = h + dot(ob, w_out[...], (0, 0))
    h2_ref[at, :] = h2
    n2 = (normalize(h2)[0] * gain2[...]).astype(BF16)
    n2_ref[at, :] = n2
    u = dot(n2, w1[...]) + b1[...]
    square = u * u
    t = jnp.tanh(gelu_in * u * (1.0 + gelu_cubic * square))
    half = 0.5 + 0.5 * t
    a = (u * half).astype(BF16)
    a_ref[at, :] = a
    slope = half + (0.5 * gelu_in) * u * (1.0 - t * t) * (1.0 + 3.0 * gelu_cubic * square)
    gp_ref[at, :] = slope.astype(BF16)
    return h2 + dot(a, w2[...])


def middle_kernel(
    n, late, gain2, b1, gain1, h2_out, n2_out, a_out, gp_out, h3_out, n1_out, q_out, k_all, v_all,
    h2_ref, n2_ref, a_ref, gp_ref, h3_ref, n1_ref, q_ref, ship_sems, kbuf, vbuf, ksem, krsem, lsem,
):
    h, ob, w_out, w1, w2, w = late
    place = Place(n)
    rows, width = h.shape
    block = rows // 2
    bar = pltpu.get_barrier_semaphore()
    for step in range(1, n):
        signal(bar, place.peer(step))
    keys = Keys(place, (k_all, v_all), (kbuf, vbuf), ksem, krsem, lsem)
    ship = Ship(ship_sems)
    gain2, b1 = gain2.at[pl.ds(0, 1)], b1.at[pl.ds(0, 1)]
    pairs = ((h2_ref, h2_out), (n2_ref, n2_out), (a_ref, a_out), (gp_ref, gp_out), (h3_ref, h3_out), (n1_ref, n1_out), (q_ref, q_out))
    for i in range(rows // block):
        at = pl.ds(i * block, block)
        h3 = mlp_block(at, h[at, :], ob[:, at], w_out, gain2, w1, b1, w2, h2_ref, n2_ref, a_ref, gp_ref)
        h3_ref[at, :] = h3
        n1 = (normalize(h3)[0] * gain1[1:2, :]).astype(BF16)
        n1_ref[at, :] = n1
        kv = dot(n1, w[:, width:]).astype(BF16)
        if i == 0:
            pl.semaphore_wait(bar, n - 1)
        keys.start(i, at, kv)
        q_ref[at, :] = (dot(n1, w[:, :width]) * HEAD_DIM**-0.5).astype(BF16)
        for src, dst in pairs:
            ship(src.at[at], dst.at[at])
    keys.finish()
    ship.finish()


def middle(n, collective_id, h, ob, w_out, gain2, w1, b1, w2, gain1, w):
    rows, width = h.shape
    hidden = w1.shape[2]
    blocks = 2
    shapes = [
        ((rows, width), F32), ((rows, width), BF16), ((rows, hidden), BF16), ((rows, hidden), BF16), ((rows, width), F32),
        ((rows, width), BF16), ((rows, width), BF16),
    ]
    return run(
        functools.partial(middle_kernel, n),
        "middle",
        collective_id,
        [h, ob, (w_out, 0), (w1, 0), (w2, 0), (w, 1)],
        [gain2, b1, gain1],
        [VMEM] * 3,
        [jax.ShapeDtypeStruct(*shape) for shape in shapes] + [jax.ShapeDtypeStruct((n, rows, width), BF16)] * 2,
        [ANY] * 9,
        [pltpu.VMEM(*shape) for shape in shapes]
        + [pltpu.SemaphoreType.DMA((blocks * len(shapes),))]
        + keys_scratch(n, rows, width, blocks),
    )


def mlp_back_block(at, dh, gp, h2, ob, li, w_out, gain2, w1, w2, dz_ref, du_ref, dy_ref, dh2_ref, do_ref, dl_ref):
    dz = dh.astype(BF16)
    dz_ref[at, :] = dz
    du = (dot(dz, w2[...], (1, 1)) * gp.astype(F32)).astype(BF16)
    du_ref[at, :] = du
    bias_sum = column_sum(du.astype(F32))
    dn2 = dot(du, w1[...], (1, 1))
    xhat, rstd = normalize(h2)
    gain_sum = column_sum(dn2 * xhat)
    dh2 = dh + normalize_back(dn2 * gain2[...], xhat, rstd)
    dh2_ref[at, :] = dh2
    dy = dh2.astype(BF16)
    dy_ref[at, :] = dy
    do = dot(w_out[...], dy, (1, 1))
    product = do * ob.astype(F32)
    for head in range(do.shape[0] // HEAD_DIM):
        rows = slice(head * HEAD_DIM, (head + 1) * HEAD_DIM)
        inverse = li[8 * (head // 2) + head % 2 : 8 * (head // 2) + head % 2 + 1, :]
        do_ref[rows, at] = (do[rows] * inverse).astype(BF16)
        rest = -column_sum(product[rows]) * inverse
        terms = []
        for _ in range(3):
            terms.append(rest.astype(BF16).astype(F32))
            rest = rest - terms[-1]
        row = lax.broadcasted_iota(jnp.int32, (16, 1), 0)
        block = jnp.where(row == 0, terms[0], jnp.where(row == 1, terms[1], jnp.where(row == 2, terms[2], 0.0)))
        dl_ref[16 * head : 16 * head + 16, at] = block.astype(BF16)
    return bias_sum, gain_sum


def fc1_sums(g_ref, n2, du):
    width = n2.shape[1]
    for part in range(du.shape[1] // width):
        at = slice(part * width, (part + 1) * width)
        g_ref[at, :] = dot(n2[...], du[:, at], (0, 0)).astype(BF16)
    return du.shape[1]


def fill(g_ref, at):
    if g_ref.shape[0] > at:
        g_ref[at:, :] = jnp.zeros((g_ref.shape[0] - at, g_ref.shape[1]), BF16)


def put_rows(small_ref, row, value, width):
    for part in range(value.shape[1] // width):
        small_ref[row + part : row + part + 1, :] = value[:, part * width : (part + 1) * width]


def back_shapes(rows, width):
    return [
        jax.ShapeDtypeStruct((rows, width), F32),
        jax.ShapeDtypeStruct((width, rows), BF16),
        jax.ShapeDtypeStruct((16 * width // HEAD_DIM, rows), BF16),
    ]


def turn_kernel(
    late, li_ref, aux_ref, gain2, b1, fgain, head_w, head_b, prior_ref,
    g2_out, g1_out, small_ref, dh2_out, do_out, dl_out, expert_ref, head_ref, out_ref,
    g2_ref, g1_ref, dh2_ref, do_ref, dl_ref, dz, du, dy, h2_ref, n2_ref, a_ref, gp_ref, wide, tall, ship_sems,
):
    h_ref, ob_ref, w_out, w1, w2 = late
    rows, width = h_ref.shape
    gain2, b1 = gain2.at[pl.ds(1, 1)], b1.at[pl.ds(1, 1)]
    block = rows // 2
    ship = Ship(ship_sems)
    wide[...] = jnp.zeros_like(wide)
    wide[0:EXPERTS, :] = head_w[...]
    hw = wide[...]
    fgain_row = fgain[...].reshape(1, width)
    tall[...] = jnp.ones_like(tall)
    tall[0:EXPERTS, 0:LEADS] = prior_ref[...]
    logp = jnp.log(tall[...])
    tall[...] = jnp.zeros_like(tall)
    tall[0:1, 0:EXPERTS] = head_b[...]
    hb = jnp.sum(jnp.where(diagonal((8, LANES)), tall[0:1, :], 0.0), axis=1, keepdims=True)
    lane = lax.broadcasted_iota(jnp.int32, (8, LANES), 1).astype(F32)
    expert = lax.broadcasted_iota(jnp.int32, (8, 1), 0)
    bias_sum, gain_sum, final_sum, head_sum, hbias_sum, lead_sum = 0.0, 0.0, 0.0, 0.0, 0.0, 0.0
    for i in range(2):
        at = pl.ds(i * block, block)
        h3 = mlp_block(at, h_ref[at, :], ob_ref[:, at], w_out, gain2, w1, b1, w2, h2_ref, n2_ref, a_ref, gp_ref)
        xhat, rstd = normalize(h3)
        nf = xhat * fgain_row
        own_lead = lane == aux_ref[LEAD_ROW + i : LEAD_ROW + i + 1, 0:1]
        prior = jnp.sum(jnp.where(own_lead, logp, 0.0), axis=1, keepdims=True)
        logits = dot_split(hw, nf, (1, 1)) + hb - prior
        logits = jnp.where(expert < EXPERTS, logits, -1e30)
        power = jnp.exp(logits - jnp.max(logits, axis=0, keepdims=True))
        weights = power / jnp.sum(power, axis=0, keepdims=True)
        expert_ref[:, at] = weights
        counted = jnp.where(expert == EXPERTS, 1.0, weights)
        lead_sum = lead_sum + jnp.where(own_lead, jnp.sum(counted, axis=1, keepdims=True), 0.0)
        cot = jnp.where(expert < EXPERTS, aux_ref[:, at], 0.0)
        dlogits = weights * (cot - jnp.sum(weights * cot, axis=0, keepdims=True))
        head_sum = head_sum + dot_split(dlogits, nf)
        hbias_sum = hbias_sum + jnp.sum(dlogits, axis=1, keepdims=True)
        dnf = dot_split(dlogits, hw, (0, 0))
        final_sum = final_sum + column_sum(dnf * xhat)
        dh = normalize_back(dnf * fgain_row, xhat, rstd)
        sums = mlp_back_block(
            at, dh, gp_ref[at, :], h2_ref[at, :], ob_ref[:, at], li_ref[:, at], w_out, gain2, w1, w2,
            dz, du, dy, dh2_ref, do_ref, dl_ref,
        )
        bias_sum, gain_sum = bias_sum + sums[0], gain_sum + sums[1]
        ship(dh2_ref.at[at], dh2_out.at[at])
        ship(do_ref.at[:, at], do_out.at[:, at])
        ship(dl_ref.at[:, at], dl_out.at[:, at])
    small_ref[...] = jnp.zeros_like(small_ref)
    put_rows(small_ref, 0, gain_sum, width)
    put_rows(small_ref, 1, final_sum, width)
    put_rows(small_ref, 4, bias_sum, width)
    head_ref[0:8, :] = head_sum
    head_ref[8:16, :] = jnp.zeros((8, width), F32)
    head_ref[8:16, 0:LANES] = lead_sum
    head_ref[16:24, :] = jnp.broadcast_to(hbias_sum, (8, width))
    g2_ref[: a_ref.shape[1], :] = dot(a_ref[...], dz[...], (0, 0)).astype(BF16)
    fill(g2_ref, a_ref.shape[1])
    ship(g2_ref, g2_out)
    fill(g1_ref, fc1_sums(g1_ref, n2_ref, du))
    ship(g1_ref, g1_out)
    out_ref[...] = dot(ob_ref[...], dy[...]).astype(BF16)
    ship.finish()


def turn(h, ob, li, aux, w_out, gain2, w1, b1, w2, fgain, head_w, head_b, prior, grad_rows):
    rows, width = h.shape
    hidden = w1.shape[2]
    grads = [jax.ShapeDtypeStruct((grad_rows, width), BF16)] * 2
    shapes = back_shapes(rows, width)
    return run(
        turn_kernel,
        "turn",
        None,
        [h, ob, (w_out, 1), (w1, 1), (w2, 1)],
        [li, aux, gain2, b1, fgain, head_w, head_b, prior],
        [VMEM] * 8,
        grads
        + [jax.ShapeDtypeStruct((8, width), F32)]
        + shapes
        + [
            jax.ShapeDtypeStruct((8, rows), F32),
            jax.ShapeDtypeStruct((24, width), F32),
            jax.ShapeDtypeStruct((width, width), BF16),
        ],
        [ANY, ANY, VMEM, ANY, ANY, ANY, VMEM, VMEM, VMEM],
        [pltpu.VMEM(shape.shape, shape.dtype) for shape in grads + shapes]
        + [
            pltpu.VMEM((rows, width), BF16),
            pltpu.VMEM((rows, hidden), BF16),
            pltpu.VMEM((rows, width), BF16),
            pltpu.VMEM((rows, width), F32),
            pltpu.VMEM((rows, width), BF16),
            pltpu.VMEM((rows, hidden), BF16),
            pltpu.VMEM((rows, hidden), BF16),
            pltpu.VMEM((8, width), F32),
            pltpu.VMEM((8, LANES), F32),
            pltpu.SemaphoreType.DMA((8,)),
        ],
    )


class KeyGrads:
    def __init__(self, place, parts, own, recv, dkv, ssem, rsem):
        self.place, self.parts, self.own, self.recv, self.dkv, self.ssem, self.rsem = place, parts, own, recv, dkv, ssem, rsem

    def copies(self):
        for step in range(1, self.place.n):
            for part, src in enumerate(self.parts):
                at = step - 1, part
                yield send(src.at[step], self.recv.at[at], self.ssem.at[at], self.rsem.at[at], self.place.peer(step))

    def start(self):
        for copy in self.copies():
            copy.start()

    def finish(self):
        for copy in self.copies():
            copy.wait()
        width = self.dkv.shape[1] // 2
        for part, own in enumerate(self.own):
            total = own[...].astype(F32)
            for step in range(self.place.n - 1):
                total = total + self.recv[step, part].astype(F32)
            self.dkv[:, part * width : (part + 1) * width] = total.astype(BF16)


def key_scratch(n, rows, width):
    return [
        pltpu.VMEM((n - 1, 2, rows, width), BF16),
        pltpu.VMEM((rows, 2 * width), BF16),
        pltpu.SemaphoreType.DMA((n - 1, 2)),
        pltpu.SemaphoreType.DMA((n - 1, 2)),
    ]


def project_back_block(at, dn1_q, dkv, w, gain_row, h, dh2):
    width = h.shape[1]
    dn1 = dn1_q + dot(dkv[at, :], w[:, width:], (1, 1))
    xhat, rstd = normalize(h[at, :])
    return dh2[at, :] + normalize_back(dn1 * gain_row, xhat, rstd), column_sum(dn1 * xhat)


def key_weight_sums(g_ref, n1, dkv):
    width = n1.shape[1]
    for part in range(2):
        at = slice(part * width, (part + 1) * width)
        g_ref[(part + 1) * width : (part + 2) * width, :] = dot(n1[...], dkv[:, at], (0, 0)).astype(BF16)


def between_kernel(
    n, chips, late, dk, dv, gain1, li_ref, gain2,
    norm_ref, small_ref, g1_out, dh2_out, do_out, dl_out, fc2_out, fc1_out, qkv_next, fc2_next_ref,
    gq_ref, g2_ref, g1_ref, dh2_ref, do_ref, dl_ref, dz, du, dy, ship_sems, krecv, dkv, ksem, krsem, *refs,
):
    n1, dq, fc2_src, fc1_src, dk_own, dv_own, w, h3, dh2_in, out_b, a, w2, gp, w1, h2_ref, w_out, ob_ref, n2_ref = late
    place, axes = Place(n), Axes(n, chips)
    rows, width = dq.shape
    hidden = a.shape[1]
    block = rows // 2
    bar = pltpu.get_barrier_semaphore()
    met = axes.greet(bar)
    for step in range(1, n):
        signal(bar, place.peer(step))
    ship = Ship(ship_sems)
    refs = list(refs)
    take = lambda count: [refs.pop(0) for _ in range(count)]
    fc2 = Gather(axes, fc2_out.shape[0], 2, 0, fc2_src.buf, fc2_out, take(3))
    fc1 = Gather(axes, fc1_out.shape[0], 3, 0, fc1_src.buf, fc1_out, take(3))
    qkv = Reduce(axes, gq_ref.shape[0], 0, 2, gq_ref, qkv_next, take(7))
    fc2_next = Reduce(axes, g2_ref.shape[0], 0, 1, g2_ref, fc2_next_ref, take(6))
    keys = KeyGrads(place, (dk, dv), (dk_own, dv_own), krecv, dkv, ksem, krsem)

    gq_ref[:width, :] = dot(n1[...], dq[...], (0, 0)).astype(BF16)
    fc2_src.ready()
    fc1_src.ready()
    pl.semaphore_wait(bar, met + n - 1)
    keys.start()
    fc2.start(2)
    fc1.start(3)
    dn1_q = [dot(dq[pl.ds(i * block, block), :], w[:, :width], (1, 1)) for i in range(2)]
    keys.finish()
    gain_sum = 0.0
    dh = []
    for i in range(2):
        at = pl.ds(i * block, block)
        dh_one, part = project_back_block(at, dn1_q[i], dkv, w, gain1[1:2, :], h3, dh2_in)
        dh.append(dh_one)
        dz[at, :] = dh_one.astype(BF16)
        gain_sum = gain_sum + part
    norm_ref[...] = jnp.broadcast_to(gain_sum, norm_ref.shape)
    fc2.finish_start(2)
    key_weight_sums(gq_ref, n1, dkv)
    gq_ref[3 * width : 4 * width, :] = out_b[...]
    fill(gq_ref, 4 * width)
    qkv.own().start()
    qkv.start(0)
    g2_ref[:hidden, :] = dot(a[...], dz[...], (0, 0)).astype(BF16)
    fill(g2_ref, hidden)
    fc2_next.own().start()
    fc2_next.start(0)
    fc1.finish_start(3)
    bias_sum, gain_sum = 0.0, 0.0
    parts = min(4, rows // LANES)
    quarter = rows // parts
    acts = [
        [qkv.act(0), fc2_next.act(0)],
        [fc1.act(2)],
        [fc2.act(1), qkv.act(1)],
        [],
    ]
    dh = jnp.concatenate(dh, axis=0)
    for i in range(parts):
        at = pl.ds(i * quarter, quarter)
        dh_one = dh[i * quarter : (i + 1) * quarter]
        sums = mlp_back_block(
            at, dh_one, gp[at, :], h2_ref[at, :], ob_ref[:, at], li_ref[:, at], w_out, gain2.at[pl.ds(0, 1)], w1, w2,
            dz, du, dy, dh2_ref, do_ref, dl_ref,
        )
        bias_sum, gain_sum = bias_sum + sums[0], gain_sum + sums[1]
        for group in acts[i * 4 // parts : (i + 1) * 4 // parts]:
            for act in group:
                act()
        ship(dh2_ref.at[at], dh2_out.at[at])
        ship(do_ref.at[:, at], do_out.at[:, at])
        ship(dl_ref.at[:, at], dl_out.at[:, at])
    small_ref[...] = jnp.zeros_like(small_ref)
    put_rows(small_ref, 0, gain_sum, width)
    put_rows(small_ref, 4, bias_sum, width)
    at = fc1_sums(g1_ref, n2_ref, du)
    g1_ref[at : at + width, :] = dot(ob_ref[...], dy[...]).astype(BF16)
    fill(g1_ref, at + width)
    ship(g1_ref, g1_out)
    fc1.finish_start(1)
    fc2.finish(0)
    fc2_next.finish(1)
    qkv.finish(2)
    fc1.finish(0)
    ship.finish()


def between(
    n, chips, collective_id, totals, dq, dk, dv, n1, h3, dh2, w, gain1, gp, h2, ob, li, n2, a, w_out, gain2, w1, w2, out_b, fc2, fc1
):
    rows, width = dq.shape
    hidden = a.shape[1]
    sizes = sum_sizes(n, chips)
    half = lambda height: jax.ShapeDtypeStruct((height, width), BF16)
    kept = [half(totals[4])] + back_shapes(rows, width)
    return run(
        functools.partial(between_kernel, n, chips),
        "between",
        collective_id,
        [n1, dq, fc2, fc1, (dk, 0), (dv, 0), (w, 1), h3, dh2, out_b, a, (w2, 0), gp, (w1, 0), h2, (w_out, 0), ob, n2],
        [dk, dv, gain1, li, gain2],
        [ANY, ANY, VMEM, VMEM, VMEM],
        [jax.ShapeDtypeStruct((8, width), F32)] * 2
        + kept
        + [
            half(totals[0]),
            half(totals[1]),
            half(rows_after(sizes, totals[2], 3)),
            half(rows_after(sizes, totals[3], 2)),
        ],
        [VMEM, VMEM] + [ANY] * 6 + [VMEM, VMEM],
        [pltpu.VMEM((totals[2], width), BF16), pltpu.VMEM((totals[3], width), BF16)]
        + [pltpu.VMEM(shape.shape, shape.dtype) for shape in kept]
        + [
            pltpu.VMEM((rows, width), BF16),
            pltpu.VMEM((rows, hidden), BF16),
            pltpu.VMEM((rows, width), BF16),
            pltpu.SemaphoreType.DMA((13,)),
        ]
        + key_scratch(n, rows, width)
        + gather_scratch(sizes, 2, 0)
        + gather_scratch(sizes, 3, 0)
        + reduce_scratch(sizes, totals[2], 0, 2, width)
        + reduce_scratch(sizes, totals[3], 0, 1, width),
    )


def last_axes(n, chips):
    return DirectAxes if n * chips <= 16 else Axes


def last_kernel(
    n, chips, late, dk, dv, gain, aux, expert, norm_b, small_a, small_b, head,
    tg_out, ex_out, fc2_out, fc1_out, early_ref, sum_ref,
    tg, g_ref, own_shard, early_shard, krecv, dkv, ksem, krsem, ssem, rsem, *refs,
):
    n1, dq, fc2_src, fc1_src, early, dk_own, dv_own, w, dk_done, dv_done, h, dh2 = late
    place, axes = Place(n), Axes(n, chips)
    direct = last_axes(n, chips)(n, chips)
    rows, width = dq.shape
    block = rows // 2
    bar = pltpu.get_barrier_semaphore()
    met = axes.greet(bar) + direct.greet(bar) + n - 1
    for step in range(1, n):
        signal(bar, place.peer(step))

    @pl.when(place.moves)
    def _():
        signal(bar, place.partner)

    refs = list(refs)
    take = lambda count: [refs.pop(0) for _ in range(count)]
    top = len(direct.sizes) - 1
    fc2 = Gather(axes, fc2_out.shape[0], 0, 0, fc2_src.buf, fc2_out, take(3))
    fc1 = Gather(axes, fc1_out.shape[0], 3, 0, fc1_src.buf, fc1_out, take(3))
    early_reduce = Reduce(axes, early_ref.shape[0], 2, 3, early.buf, early_shard, take(6))
    if last_axes(n, chips) is DirectAxes:
        early_gather = Spread(axes, direct, early_ref.shape[0], early_shard, early_ref, take(3))
    else:
        early_gather = Gather(axes, early_ref.shape[0], 3, 0, early_shard, early_ref, take(3))
    reduce = Reduce(direct, g_ref.shape[0], 0, top, g_ref, own_shard, take(5 + top))
    gather = Gather(direct, g_ref.shape[0], top, 0, own_shard, sum_ref, take(3))
    keys = KeyGrads(place, (dk, dv), (dk_own, dv_own), krecv, dkv, ksem, krsem)
    for array in (fc2_src, fc1_src, early):
        array.ready()

    @pl.when(place.moves)
    def _():
        pl.semaphore_wait(bar, met + 1)

    @pl.when(jnp.logical_not(place.moves))
    def _():
        pl.semaphore_wait(bar, met)

    keys.start()
    early_reduce.own().start()
    early_reduce.start(2)
    fc1.start(3)
    fc2.start(0)
    done = dk_done.shape[1]
    dn1 = []
    for i in range(2):
        at = pl.ds(i * block, block)
        part = dot(dq[at, :], w[:, :width], (1, 1)) + dot(dk_done[at, :], w[:, width : width + done], (1, 1))
        dn1.append(part + dot(dv_done[at, :], w[:, 2 * width : 2 * width + done], (1, 1)))
    keys.finish()
    early_reduce.finish_start(2)
    fc1.finish_start(3)
    gain_sum = 0.0
    half_sums = []
    for i in range(2):
        at = pl.ds(i * block, block)
        part = dot(dkv[at, :LANES], w[:, width + done : 2 * width], (1, 1))
        part = dn1[i] + part + dot(dkv[at, LANES:], w[:, 2 * width + done :], (1, 1))
        xhat, rstd = normalize(h[at, :])
        gain_sum = gain_sum + column_sum(part * xhat)
        dh = dh2[at, :] + normalize_back(part * gain[0:1, :], xhat, rstd)
        half_sums.append(column_sum(dh))
        tg[at, :] = dh.astype(BF16)
    lead_index = lax.broadcasted_iota(jnp.int32, (LEADS, 1), 0).astype(F32)
    table = 0.0
    for half in range(2):
        lead = aux[LEAD_ROW + half : LEAD_ROW + half + 1, 0:1]
        table = table + jnp.where(lead_index == lead, half_sums[half], 0.0)
    early_reduce.finish(3)
    early_gather.start(early_gather.first)
    g_ref[:width, :] = dot(n1[...], jnp.concatenate([dq[:, done:], dkv[...]], axis=1), (0, 0)).astype(BF16)
    at = width
    for piece in (table, jnp.broadcast_to(gain_sum, (8, width)), norm_b[...], small_a[...], small_b[...], head[...]):
        g_ref[at : at + piece.shape[0], :] = piece.astype(BF16)
        at += piece.shape[0]
    g_ref[at:, :] = jnp.zeros((g_ref.shape[0] - at, width), BF16)
    reduce.own().start()
    reduce.start(0)

    def turn_round():
        reduce.finish(top)
        gather.start(top)

    swaps = [
        send(tg, tg_out, ssem.at[0], rsem.at[0], place.partner),
        send(expert, ex_out, ssem.at[1], rsem.at[1], place.partner),
    ]

    def swap():
        @pl.when(place.moves)
        def _():
            for copy in swaps:
                copy.start()

        @pl.when(jnp.logical_not(place.moves))
        def _():
            tg_out[...] = tg[...]
            ex_out[...] = expert[...]

    chains = [
        [reduce.act(phase) for phase in range(top)] + [turn_round] + [gather.act(phase) for phase in range(top, -1, -1)],
        [swap],
        [fc1.act(phase) for phase in range(2, -1, -1)],
        [fc2.act(0)],
        [early_gather.act(phase) for phase in range(early_gather.first, -1, -1)],
    ]
    for turn_index in range(max(len(chain) for chain in chains)):
        for chain in chains:
            if turn_index < len(chain):
                chain[turn_index]()

    @pl.when(place.moves)
    def _():
        for copy in swaps:
            copy.wait()


def last(
    n, chips, collective_id, rows_last, rows_early, fc2_rows, fc1_rows, dq, dk, dv, dk_done, dv_done, n1, h, dh2, w, gain, aux,
    expert, norm_b, small_a, small_b, head, fc2, fc1, early,
):
    rows, width = dq.shape
    devices = 2 * n * chips
    sizes = sum_sizes(n, chips)
    direct = direct_sizes(n, chips) if last_axes(n, chips) is DirectAxes else sizes
    half = lambda height: jax.ShapeDtypeStruct((height, width), BF16)
    return run(
        functools.partial(last_kernel, n, chips),
        "last",
        collective_id,
        [n1, dq, fc2, fc1, early, (dk, 0), (dv, 0), (w, 0), dk_done, dv_done, h, dh2],
        [dk, dv, gain, aux, expert, norm_b, small_a, small_b, head],
        [ANY, ANY] + [VMEM] * 7,
        [half(rows), jax.ShapeDtypeStruct((8, rows), F32)] + [half(height) for height in (fc2_rows, fc1_rows, rows_early, rows_last)],
        [VMEM, VMEM, ANY, ANY, ANY, ANY],
        [
            pltpu.VMEM((rows, width), BF16),
            pltpu.VMEM((rows_last, width), BF16),
            pltpu.VMEM((rows_last // devices, width), BF16),
            pltpu.VMEM((rows_early // devices, width), BF16),
        ]
        + key_scratch(n, rows, LANES)
        + [pltpu.SemaphoreType.DMA((2,))] * 2
        + gather_scratch(sizes, 0, 0)
        + gather_scratch(sizes, 3, 0)
        + reduce_scratch(sizes, rows_early, 2, 3, width)
        + gather_scratch(direct, len(direct) - 1, 0)
        + reduce_scratch(direct, rows_last, 0, len(direct) - 1, width)
        + gather_scratch(direct, len(direct) - 1, 0),
    )


def unpack_kernel(
    fc2_a, fc2_b, fc1_a, fc1_b, out_a, out_b, first_a, second_a, third_a, q_b, k_b, v_b, small, prior, tg_in, expert_in,
    fc2, fc1, out, qkv, tg, expert, lead_average, norm1, norm2, bias, table, final, head, head_bias,
):
    layer, step = pl.program_id(0), pl.program_id(1)

    def layer_part(own, sources):
        @pl.when(layer == own)
        def _():
            for source, target, at in sources:
                target[0, :, at] = source[...].astype(F32)
            for source_rows, at in turned:
                fc1[0, :, at] = (fc1_a, fc1_b)[own][source_rows, :].astype(F32)

    width = table.shape[1]
    everything = slice(0, width)
    turned = [(slice(i * width, (i + 1) * width), slice(i * width, (i + 1) * width)) for i in range(fc1.shape[2] // width)]
    layer_part(0, [(fc2_a, fc2, everything), (out_a, out, everything)])
    layer_part(1, [(fc2_b, fc2, everything), (out_b, out, everything)])
    thirds = [slice(i * width, (i + 1) * width) for i in range(3)]

    @pl.when(layer == 0)
    def _():
        for pair, source in enumerate((first_a, second_a, third_a)):
            for part in range(3):
                at = part * width + pair * LANES
                qkv[0, :, at : at + LANES] = source[:, part * LANES : (part + 1) * LANES].astype(F32)


    @pl.when(layer == 1)
    def _():
        for source, at in zip((q_b, k_b, v_b), thirds):
            qkv[0, :, at] = source[...].astype(F32)

    tg[...] = tg_in[...]

    @pl.when(jnp.logical_and(layer == 0, step == 0))
    def _():
        rows = small[...].astype(F32)
        for i in range(EXPERTS):
            expert[i] = expert_in[i : i + 1, :]
        table[...] = rows[:LEADS]
        for own in range(2):
            norm1[own : own + 1, :] = rows[ROW_NORM1 + 8 * own : ROW_NORM1 + 8 * own + 1]
            base = ROW_MLP + 8 * own
            norm2[own : own + 1, :] = rows[base : base + 1]
            for part in range(bias.shape[1] // width):
                bias[own : own + 1, part * width : (part + 1) * width] = rows[base + 4 + part : base + 5 + part]
        final[...] = rows[ROW_MLP + 9].reshape(final.shape)
        head[...] = rows[ROW_HEAD : ROW_HEAD + EXPERTS]
        totals = rows[ROW_HEAD + 8 : ROW_HEAD + 16, 0:LEADS]
        means = totals[0:EXPERTS] / jnp.maximum(totals[EXPERTS : EXPERTS + 1], 1.0)
        lead_average[...] = 0.5 * prior[...] + 0.5 * means
        column = rows[ROW_HEAD + 16 : ROW_HEAD + 24, 0:LANES]
        head_bias[...] = column_sum(jnp.where(diagonal((8, LANES)), column, 0.0))[:, 0:EXPERTS]


def unpack(fc2_a, fc2_b, fc1_a, fc1_b, early_a, last_a, qkv_b, prior, token_grad, expert, hidden):
    rows, width = token_grad.shape
    steps = 2
    slab, tall = width // steps, hidden // steps

    def at(own, block, first):
        start = first // block
        if own == 0:
            return pl.BlockSpec((block, width), lambda l, j: (start + jnp.where(l == 0, j, steps - 1), 0))
        return pl.BlockSpec((block, width), lambda l, j: (start + jnp.where(l == 1, j, 0), 0))

    fixed = lambda shape: pl.BlockSpec(shape, lambda l, j: (0,) * len(shape))
    moving = pl.BlockSpec((rows // (2 * steps), width), lambda l, j: (l * steps + j, 0))
    in_specs = [at(own, tall, 0) for _ in range(2) for own in range(2)]
    in_specs += [at(0, slab, hidden), at(1, slab, 3 * width)]
    in_specs += [at(0, slab, 0), at(0, slab, width), at(0, slab, 0)]
    in_specs += [at(1, slab, part * width) for part in range(3)]
    in_specs += [pl.BlockSpec((SMALL_ROWS, width), lambda l, j: (width // SMALL_ROWS, 0)), fixed(prior.shape), moving]
    in_specs += [fixed(expert.shape)]
    small_shapes = [
        (EXPERTS, 1, rows), prior.shape, (2, width), (2, width), (2, hidden), (LEADS, width), (width,),
        (EXPERTS, width), (1, EXPERTS),
    ]
    shapes = [(2, hidden, width), (2, width, hidden), (2, width, width), (2, width, 3 * width)]
    out_specs = [
        pl.BlockSpec((1, tall, width), lambda l, j: (l, j, 0)),
        pl.BlockSpec((1, width, tall), lambda l, j: (l, 0, j)),
        pl.BlockSpec((1, slab, width), lambda l, j: (l, j, 0)),
        pl.BlockSpec((1, slab, 3 * width), lambda l, j: (l, j, 0)),
        moving,
    ] + [fixed(shape) for shape in small_shapes]
    return pl.pallas_call(
        unpack_kernel,
        grid=(2, steps),
        out_shape=[jax.ShapeDtypeStruct(shape, F32) for shape in shapes]
        + [jax.ShapeDtypeStruct((rows, width), BF16)]
        + [jax.ShapeDtypeStruct(shape, F32) for shape in small_shapes],
        in_specs=in_specs,
        out_specs=out_specs,
        compiler_params=params(),
        name="unpack",
    )(*([fc2_a, fc2_b, fc1_a, fc1_b, fc1_a, qkv_b] + [early_a, early_a, last_a] + [qkv_b] * 3 + [last_a, prior, token_grad, expert]))


def on_device(
    tokens, slot_kind, frame_lead, norm1_gain, w_qkv, w_out, norm2_gain, w_fc1, b_fc1, w_fc2,
    lead_table, final_gain, head_w, head_b, lead_prior, gate_cot,
):
    rows, width = tokens.shape[0], tokens.shape[3]
    hidden = w_fc1.shape[2]
    n, devices = lax.axis_size("blk"), lax.axis_size("blk") * lax.axis_size("dp")
    chips = lax.axis_size("dp") // 2
    pad = lambda count: -(-count // (16 * devices)) * 16 * devices
    fc_rows, fc1_rows = pad(hidden), pad(hidden + width)
    rows_b, rows_early, rows_last = pad(4 * width), pad((width // LANES - 1) * width), pad(width + SMALL_ROWS)
    flat = lambda x: x.reshape(n * rows, width)
    split = lambda x: x.reshape(n, rows, width)

    h, n1, q, k, v, aux = project(
        n, 0, tokens.reshape(rows, width), gate_cot.reshape(EXPERTS, 1, rows), slot_kind, frame_lead.reshape(1, 2),
        lead_table, norm1_gain, w_qkv,
    )
    k, v = flat(k), flat(v)
    e, ob, li = attend(q, k, v, aux)
    h2, n2, a, gp, h3, n1b, qb, kb, vb = middle(
        n, 1, h, ob, w_out, norm2_gain, w_fc1, b_fc1, w_fc2, norm1_gain, w_qkv
    )
    kb, vb = flat(kb), flat(vb)
    eb, obb, lib = attend(qb, kb, vb, aux)
    g_fc2_b, g_fc1_b, small_b, dh2, do, dl, expert, head, out_b = turn(
        h3, obb, lib, aux, w_out, norm2_gain, w_fc1, b_fc1, w_fc2,
        final_gain, head_w.T, head_b[None], lead_prior.T, fc_rows,
    )
    dq, dk, dv, _, fc2, fc1 = attend_back(
        n, chips, 2, qb, kb, vb, eb, do, dl,
        [
            Task(True, fc_rows, (0, 1, 2, 3), (3.5, 12.0, 17.8, 23.6), g_fc2_b),
            Task(False, fc_rows, (3,), (29.4,)),
            Task(True, fc_rows, (0, 1, 2, 3), (4.9, 14.7, 20.7, 26.7), g_fc1_b, begin=2.2),
        ],
    )
    norm_b, small_a, g_fc1_a, dh2, do, dl, g_fc2_b, g_fc1_b, qkv_part, fc2 = between(
        n, chips, 3, (fc_rows, fc_rows, rows_b, fc_rows, fc1_rows), dq, split(dk), split(dv), n1b, h3, dh2, w_qkv, norm1_gain,
        gp, h2, ob, li, n2, a, w_out, norm2_gain, w_fc1, w_fc2, out_b, fc2, fc1,
    )
    dq, dk, dv, dk_done, dv_done, early, fc1, _, fc2, _, g_qkv_b = attend_back(
        n, chips, 4, q, k, v, e, do, dl,
        [
            Task(True, fc1_rows, (0, 1, 2, 3), (4.9, 14.7, 21.8, 27.8), g_fc1_a),
            Task(True, fc_rows, (2, 3), (8.0, 13.1), fc2),
            Task(False, fc_rows, (3, 2, 1), (19.6, 24.5, 29.4)),
            Task(True, rows_b, (3,), (6.0,), qkv_part),
            Task(False, rows_b, (3, 2, 1, 0), (11.9, 16.9, 24.5, 29.4)),
        ],
        Early(n1, rows_early, (13.1, 22.9, 25.6, 29.4)),
    )
    part = lambda x: x.reshape(n, rows, LANES)
    token_grad, expert, g_fc2_a, g_fc1_a, g_early, g_last = last(
        n, chips, 5, rows_last, rows_early, fc_rows, fc1_rows, dq, part(dk), part(dv), dk_done, dv_done, n1, h, dh2, w_qkv,
        norm1_gain, aux, expert, norm_b, small_a, small_b, head, fc2, fc1, early,
    )
    fc2, fc1, out, qkv, token_grad, expert, lead_average, norm1, norm2, bias, table, final, head, head_bias = unpack(
        g_fc2_a, g_fc2_b, g_fc1_a, g_fc1_b, g_early, g_last, g_qkv_b, lead_prior.T, token_grad, expert, hidden
    )
    return (
        expert.reshape(EXPERTS, rows, 1, 1),
        lead_average.T,
        token_grad.reshape(rows, 1, 1, width),
        norm1,
        qkv,
        out,
        norm2,
        fc1,
        bias,
        fc2,
        table,
        final,
        head.T,
        head_bias.reshape(-1),
    )


def solution(mesh):
    return jax.shard_map(
        on_device,
        mesh=mesh,
        in_specs=(P("blk", "dp", None, None), P("dp", None), P("dp", None, None))
        + (P(),) * 12
        + (P(None, "blk", "dp", None),),
        out_specs=(P(None, "blk", "dp", None), P(), P("blk", "dp", None, None)) + (P(),) * 11,
        check_vma=False,
    )
```

```python
import functools
import math

import jax
import jax.numpy as jnp
from jax import lax
from jax.experimental import pallas as pl
from jax.experimental.pallas import tpu as pltpu
from jax.sharding import PartitionSpec as P

HEAD_DIM = 64
LEADS = 40
LAYERS = 2
EXPERTS = 3
LANES = 128
norm_eps = 1e-06
gelu_in = math.sqrt(2.0 / math.pi)
gelu_cubic = 0.044715
MESH = pl.DeviceIdType.MESH
F32 = jnp.float32
BF16 = jnp.bfloat16
VMEM = pl.BlockSpec(memory_space=pltpu.VMEM)
ANY = pl.BlockSpec(memory_space=pl.ANY)

KIND_ROW, LEAD_ROW = 3, 4
ROW_NORM1, ROW_MLP, ROW_HEAD, SMALL_ROWS = 40, 56, 72, 96


class Late:
    def __init__(self, src, buf, sem):
        self.copy, self.buf, self.waiting = pltpu.make_async_copy(src, buf, sem), buf, True
        self.shape = buf.shape
        self.copy.start()

    def ready(self):
        if self.waiting:
            self.copy.wait()
            self.waiting = False
        return self.buf

    def __getitem__(self, at):
        return self.ready()[at]


class Ship:
    def __init__(self, sems):
        self.sems, self.copies = sems, []

    def __call__(self, src, dst):
        self.copies.append(pltpu.make_async_copy(src, dst, self.sems.at[len(self.copies)]))
        self.copies[-1].start()

    def finish(self):
        for copy in self.copies:
            copy.wait()


def run(kernel, name, collective_id, late, ins, in_specs, out_shape, out_specs, scratch):
    late = [item if isinstance(item, tuple) else (item, None) for item in late]
    count = len(late)

    def body(*refs):
        buffers, sems = refs[len(refs) - count - 1 : -1], refs[-1]
        arriving = [
            Late(ref if layer is None else ref.at[layer], buffer, sems.at[i])
            for i, (ref, buffer, (_, layer)) in enumerate(zip(refs[:count], buffers, late))
        ]
        kernel(arriving, *refs[count : len(refs) - count - 1])

    shape = lambda array, layer: array.shape if layer is None else array.shape[1:]
    return pl.pallas_call(
        body,
        out_shape=out_shape,
        in_specs=[ANY] * count + in_specs,
        out_specs=out_specs,
        scratch_shapes=scratch
        + [pltpu.VMEM(shape(array, layer), array.dtype) for array, layer in late]
        + [pltpu.SemaphoreType.DMA((count,))],
        compiler_params=params(collective_id),
        name=name,
    )(*[array for array, _ in late], *ins)


def params(collective_id=None):
    if collective_id is None:
        return pltpu.CompilerParams(vmem_limit_bytes=60 * 2**20)
    return pltpu.CompilerParams(
        vmem_limit_bytes=60 * 2**20, collective_id=collective_id, has_side_effects=True
    )


def dot(a, b, dims=(1, 0)):
    return lax.dot_general(
        a, b, (((dims[0],), (dims[1],)), ((), ())), preferred_element_type=F32
    )


def dot_split(a, b, dims=(1, 0)):
    a_high, b_high = a.astype(BF16), b.astype(BF16)
    a_low, b_low = (a - a_high.astype(F32)).astype(BF16), (b - b_high.astype(F32)).astype(BF16)
    return dot(a_high, b_high, dims) + (dot(a_high, b_low, dims) + dot(a_low, b_high, dims))


def normalize(x):
    centered = x - jnp.mean(x, axis=-1, keepdims=True)
    rstd = lax.rsqrt(jnp.mean(centered * centered, axis=-1, keepdims=True) + norm_eps)
    return centered * rstd, rstd


def normalize_back(dg, xhat, rstd):
    return (
        dg - jnp.mean(dg, axis=-1, keepdims=True) - xhat * jnp.mean(dg * xhat, axis=-1, keepdims=True)
    ) * rstd


def turned(x):
    return x.astype(F32).T.astype(BF16)


def diagonal(shape):
    return lax.broadcasted_iota(jnp.int32, shape, 0) == lax.broadcasted_iota(jnp.int32, shape, 1)


def column_sum(x):
    return jnp.sum(x, axis=0, keepdims=True)


class Place:
    def __init__(self, n):
        self.n = n
        dp, self.b = lax.axis_index("dp"), lax.axis_index("blk")
        self.core, self.e = lax.rem(dp, 2), lax.div(dp, 2)
        half = n // 2
        self.side = lax.div(self.b, half)
        self.moves = self.core != self.side
        far = lax.rem(self.b + half, n)
        self.band = jnp.where(self.moves, far, self.b)
        self.partner = (self.e * 2 + 1 - self.core, far)

    def peer(self, step):
        half = self.n // 2
        band = lax.rem(self.band + step, self.n)
        near = lax.div(band, half) == self.side
        b = jnp.where(near, band, lax.rem(band + half, self.n))
        core = jnp.where(near, self.side, 1 - self.side)
        return (self.e * 2 + core, b)


def signal(sem, device):
    pl.semaphore_signal(sem, inc=1, device_id=device, device_id_type=MESH)


def send(src, dst, ssem, rsem, device):
    return pltpu.make_async_remote_copy(
        src_ref=src, dst_ref=dst, send_sem=ssem, recv_sem=rsem, device_id=device, device_id_type=MESH
    )


def row_step(rows):
    step = 16
    while step * 2 <= 128 and rows % (step * 2) == 0:
        step *= 2
    return step


def add_rows(out, out_at, sources, rows):
    step = row_step(rows)

    def body(i, carry):
        total = 0.0
        for ref, at in sources:
            total = total + ref[pl.ds(pl.multiple_of(at + i * step, 16), step), :].astype(F32)
        out[pl.ds(pl.multiple_of(out_at + i * step, 16), step), :] = total.astype(BF16)
        return carry

    lax.fori_loop(0, rows // step, body, 0)


def sum_sizes(n, chips):
    return [2, n, chips // 4, 4]


def direct_sizes(n, chips):
    return [2, n * chips]


class Axes:
    def __init__(self, n, chips):
        dp, b = lax.axis_index("dp"), lax.axis_index("blk")
        core, e = lax.rem(dp, 2), lax.div(dp, 2)
        inner = chips // 4
        slow, fast = lax.div(e, inner), lax.rem(e, inner)
        self.sizes = sum_sizes(n, chips)
        across = lambda i: (dp, i)
        within = lambda i: ((slow * inner + i) * 2 + core, b)
        along = lambda i: ((i * inner + fast) * 2 + core, b)
        self.index = [core, b, fast, slow]
        self.device = [lambda i: (e * 2 + i, b), across, within, along]
        if n == inner:
            swap = core == 1
            pick_one = lambda f, g: lambda i: tuple(jnp.where(swap, y, x) for x, y in zip(f(i), g(i)))
            self.device[1], self.device[2] = pick_one(across, within), pick_one(within, across)
            self.index[1], self.index[2] = jnp.where(swap, fast, b), jnp.where(swap, b, fast)

    def peers(self, phase):
        size = self.sizes[phase]
        for step in range(1, size):
            i = lax.rem(self.index[phase] + step, size)
            yield step, i, self.device[phase](i)

    def greet(self, bar):
        met = 0
        for phase in range(len(self.sizes)):
            for _, _, device in self.peers(phase):
                signal(bar, device)
                met += 1
        return met


class DirectAxes(Axes):
    def __init__(self, n, chips):
        dp, b = lax.axis_index("dp"), lax.axis_index("blk")
        core, e = lax.rem(dp, 2), lax.div(dp, 2)
        self.sizes = direct_sizes(n, chips)
        self.index = [core, b * chips + e]
        self.device = [lambda i: (e * 2 + i, b), lambda i: (lax.rem(i, chips) * 2 + core, lax.div(i, chips))]


class Region:
    def __init__(self, axes, rows):
        self.axes, self.at, self.rows = axes, [0], [rows]
        for phase in range(len(axes.sizes)):
            self.rows.append(self.rows[-1] // axes.sizes[phase])
            self.at.append(self.at[-1] + axes.index[phase] * self.rows[-1])


class Reduce(Region):
    def __init__(self, axes, total, first, last, src, dst, refs):
        super().__init__(axes, total)
        self.first, self.last, self.src, self.dst = first, last, src, dst
        self.work, *recv, self.ssem, self.rsem, self.lsem = refs
        self.recv = dict(zip(range(first, last + 1), recv))

    def own(self):
        rows = self.rows[self.first + 1]
        at = pl.ds(pl.multiple_of(self.at[self.first + 1] - self.at[self.first], 16), rows)
        return pltpu.make_async_copy(self.src.at[at], self.work, self.lsem.at[0])

    def copies(self, phase):
        rows = self.rows[phase + 1]
        base = self.at[self.first] if phase == self.first else self.at[self.first + 1]
        src = self.src if phase == self.first else self.work
        for step, i, device in self.axes.peers(phase):
            begin = pl.multiple_of(self.at[phase] - base + i * rows, 16)
            at = phase - self.first, step - 1
            yield send(src.at[pl.ds(begin, rows)], self.recv[phase].at[step - 1], self.ssem.at[at], self.rsem.at[at], device)

    def start(self, phase):
        for copy in self.copies(phase):
            copy.start()

    def finish(self, phase):
        if phase == self.first:
            self.own().wait()
        for copy in self.copies(phase):
            copy.wait()
        at = self.at[phase + 1] - self.at[self.first + 1]
        sources = [(self.work, at)] + [(self.recv[phase].at[i], 0) for i in range(self.axes.sizes[phase] - 1)]
        if phase < self.last:
            add_rows(self.work, at, sources, self.rows[phase + 1])
        else:
            add_rows(self.dst, 0, sources, self.rows[phase + 1])

    def finish_start(self, phase):
        self.finish(phase)
        self.start(phase + 1)

    def act(self, phase):
        return functools.partial(self.finish_start if phase < self.last else self.finish, phase)


def rows_after(sizes, total, phases):
    for size in sizes[:phases]:
        total //= size
    return total


def reduce_scratch(sizes, total, first, last, width):
    shapes = [pltpu.VMEM((rows_after(sizes, total, first + 1), width), BF16)]
    for phase in range(first, last + 1):
        shapes.append(pltpu.VMEM((sizes[phase] - 1, rows_after(sizes, total, phase + 1), width), BF16))
    most = max(sizes[first : last + 1]) - 1
    return shapes + [pltpu.SemaphoreType.DMA((last + 1 - first, most))] * 2 + [pltpu.SemaphoreType.DMA((1,))]


class Gather(Region):
    def __init__(self, axes, total, first, last, src, out, refs):
        super().__init__(axes, total)
        self.first, self.last, self.src, self.out, (self.ssem, self.rsem, self.lsem) = first, last, src, out, refs

    def region(self, phase):
        begin = self.at[phase + 1] - self.at[self.last]
        return self.out.at[pl.ds(pl.multiple_of(begin, 16), self.rows[phase + 1])]

    def own(self):
        return pltpu.make_async_copy(self.src, self.region(self.first), self.lsem.at[0])

    def copies(self, phase):
        src = self.src if phase == self.first else self.region(phase)
        for step, _, device in self.axes.peers(phase):
            at = self.first - phase, step - 1
            yield send(src, self.region(phase), self.ssem.at[at], self.rsem.at[at], device)

    def start(self, phase):
        if phase == self.first:
            self.own().start()
        for copy in self.copies(phase):
            copy.start()

    def finish(self, phase):
        if phase == self.first:
            self.own().wait()
        for copy in self.copies(phase):
            copy.wait()

    def finish_start(self, phase):
        self.finish(phase)
        self.start(phase - 1)

    def act(self, phase):
        return functools.partial(self.finish_start if phase > self.last else self.finish, phase)


class Spread(Gather):
    def __init__(self, axes, direct, total, src, out, refs):
        super().__init__(axes, total, 1, 0, src, out, refs)
        self.direct = direct

    def region(self, phase):
        which = 4 if phase == 1 else 1
        return self.out.at[pl.ds(pl.multiple_of(self.at[which], 16), self.rows[which])]

    def copies(self, phase):
        src = self.src if phase == 1 else self.region(0)
        for step, _, device in self.direct.peers(phase):
            at = 1 - phase, step - 1
            yield send(src, self.region(phase), self.ssem.at[at], self.rsem.at[at], device)


def gather_scratch(sizes, first, last):
    most = max(sizes[last : first + 1]) - 1
    return [pltpu.SemaphoreType.DMA((first + 1 - last, most))] * 2 + [pltpu.SemaphoreType.DMA((1,))]


class Keys:
    def __init__(self, place, whole, bufs, ssem, rsem, lsem):
        self.place, self.whole, self.bufs, self.ssem, self.rsem, self.lsem = place, whole, bufs, ssem, rsem, lsem
        self.copies = []

    def start(self, i, at, kv):
        n = self.place.n
        for part, (buf, whole) in enumerate(zip(self.bufs, self.whole)):
            width = buf.shape[1]
            buf[at, :] = kv[:, part * width : (part + 1) * width]
            self.copies.append(pltpu.make_async_copy(buf.at[at], whole.at[0, at], self.lsem.at[part, i]))
            for step in range(1, n):
                to = step - 1, part, i
                self.copies.append(
                    send(buf.at[at], whole.at[step, at], self.ssem.at[to], self.rsem.at[to], self.place.peer(n - step))
                )
            for copy in self.copies[-n:]:
                copy.start()

    def finish(self):
        for copy in self.copies:
            copy.wait()


def keys_scratch(n, rows, width, blocks):
    return [
        pltpu.VMEM((rows, width), BF16),
        pltpu.VMEM((rows, width), BF16),
        pltpu.SemaphoreType.DMA((n - 1, 2, blocks)),
        pltpu.SemaphoreType.DMA((n - 1, 2, blocks)),
        pltpu.SemaphoreType.DMA((2, blocks)),
    ]


def block_of(rows):
    return min(256, rows // 2)


def project_kernel(
    n, late, tok_in, cot, kind, leads, table, gain, h_out, n1_out, q_out, k_all, v_all, aux_out,
    tok, aux_in, ssem, rsem, kbuf, vbuf, ksem, krsem, lsem,
):
    (w,) = late
    place = Place(n)
    rows, width = kbuf.shape
    block = block_of(rows)
    blocks = rows // block
    bar = pltpu.get_barrier_semaphore()
    for step in range(1, n):
        signal(bar, place.peer(step))

    @pl.when(place.moves)
    def _():
        signal(bar, place.partner)

    for i in range(EXPERTS):
        aux_in[i : i + 1, :] = cot[i]
    kind_one = kind[...].astype(F32)
    lead_one = leads[...].astype(F32)
    first_lead = lead_one[:, 0:1]
    second_lead = jnp.where(kind_one == 1.0, lead_one[:, 1:2], first_lead)
    for row, value in ((KIND_ROW, kind_one), (LEAD_ROW, first_lead), (LEAD_ROW + 1, second_lead)):
        aux_in[row : row + 1, :] = jnp.broadcast_to(value, (1, rows))
    aux_in[LEAD_ROW + 2 :, :] = jnp.zeros((8 - LEAD_ROW - 2, rows), F32)

    @pl.when(place.moves)
    def _():
        pl.semaphore_wait(bar, n)

    @pl.when(jnp.logical_not(place.moves))
    def _():
        pl.semaphore_wait(bar, n - 1)

    swaps = [send(aux_in, aux_out, ssem.at[blocks], rsem.at[blocks], place.partner)]
    stays = []
    for i in range(blocks):
        at = pl.ds(i * block, block)
        swaps.append(send(tok_in.at[at], tok.at[at], ssem.at[i], rsem.at[i], place.partner))
        stays.append(pltpu.make_async_copy(tok_in.at[at], tok.at[at], rsem.at[i]))

    @pl.when(place.moves)
    def _():
        for copy in swaps:
            copy.start()
        swaps[0].wait_recv()

    @pl.when(jnp.logical_not(place.moves))
    def _():
        for copy in stays:
            copy.start()
        aux_out[...] = aux_in[...]

    lead_index = lax.broadcasted_iota(jnp.int32, (table.shape[0], 1), 0).astype(F32)
    lead_rows = []
    for half in range(2):
        lead = aux_out[LEAD_ROW + half : LEAD_ROW + half + 1, 0:1]
        lead_rows.append(column_sum(jnp.where(lead_index == lead, table[...], 0.0)))

    keys = Keys(place, (k_all, v_all), (kbuf, vbuf), ksem, krsem, lsem)
    for i in range(blocks):
        at = pl.ds(i * block, block)

        @pl.when(place.moves)
        def _():
            swaps[1 + i].wait_recv()

        @pl.when(jnp.logical_not(place.moves))
        def _():
            stays[i].wait()

        x = tok[at, :].astype(F32) + lead_rows[i * block // (rows // 2)]
        h_out[at, :] = x
        n1 = (normalize(x)[0] * gain[0:1, :]).astype(BF16)
        n1_out[at, :] = n1
        keys.start(i, at, dot(n1, w[:, width:]).astype(BF16))
        q_out[at, :] = (dot(n1, w[:, :width]) * HEAD_DIM**-0.5).astype(BF16)
    keys.finish()

    @pl.when(place.moves)
    def _():
        for copy in swaps:
            copy.wait_send()


def project(n, collective_id, tokens, cot, kind, leads, table, gain, w):
    rows, width = tokens.shape
    blocks = rows // block_of(rows)
    half = jax.ShapeDtypeStruct((rows, width), BF16)
    whole = jax.ShapeDtypeStruct((n, rows, width), BF16)
    return run(
        functools.partial(project_kernel, n),
        "project",
        collective_id,
        [(w, 0)],
        [tokens, cot, kind, leads, table, gain],
        [ANY] + [VMEM] * 5,
        [jax.ShapeDtypeStruct((rows, width), F32), half, half, whole, whole, jax.ShapeDtypeStruct((8, rows), F32)],
        [VMEM, VMEM, VMEM, ANY, ANY, VMEM],
        [pltpu.VMEM((rows, width), BF16), pltpu.VMEM((8, rows), F32)]
        + [pltpu.SemaphoreType.DMA((blocks + 1,))] * 2
        + keys_scratch(n, rows, width, blocks),
    )


def head_lanes(x, head):
    lane = lax.broadcasted_iota(jnp.int32, x.shape, 1)
    return jnp.where(lane // HEAD_DIM == head, x, jnp.zeros_like(x))


def attend_kernel(band, q_ref, k_ref, v_ref, aux_ref, e_ref, ob_ref, li_ref, vte):
    j = pl.program_id(1)
    keys, queries = e_ref.shape[1:]
    chunk = band // 2
    own_half = lax.rem(j, 2)
    coarse = aux_ref[KIND_ROW : KIND_ROW + 1, 0:1]
    coarse_flag = jnp.max(coarse) > 0.5
    seen_half = jnp.where(coarse_flag, own_half, 0)

    @pl.when(j == 0)
    def _():
        values = v_ref[...].astype(F32).T
        key_half = lax.rem(lax.broadcasted_iota(jnp.int32, (1, keys), 1) // chunk, 2)

        def prepare(half):
            seen = jnp.where(key_half == half, 1.0, 1.0 - coarse)
            for head in range(2):
                rows = values[head * HEAD_DIM : (head + 1) * HEAD_DIM, :] * seen
                vte[head, half, :HEAD_DIM, :] = rows.astype(BF16)

            @pl.when(pl.program_id(0) == 0)
            def _():
                for head in range(2):
                    vte[head, half, HEAD_DIM:, :] = jnp.broadcast_to(seen, (HEAD_DIM, keys)).astype(BF16)

        prepare(0)

        @pl.when(coarse_flag)
        def _():
            prepare(1)

    def finish(head, total, norm):
        inverse = 1.0 / norm
        ob_ref[head * HEAD_DIM : (head + 1) * HEAD_DIM, :] = (total * inverse).astype(BF16)
        li_ref[head : head + 1, :] = inverse

    li_ref[...] = jnp.zeros_like(li_ref)
    least, largest = None, None
    for head in range(2):
        e = jnp.exp(dot(k_ref[...], head_lanes(q_ref[...], head), (1, 1))).astype(BF16)
        e_ref[head, :, :] = e
        total = dot(vte[head, seen_half], e)
        norm = total[HEAD_DIM : HEAD_DIM + 1, :]
        finish(head, total[:HEAD_DIM, :], norm)
        least = norm if least is None else jnp.minimum(least, norm)
        largest = norm if largest is None else jnp.maximum(largest, norm)

    @pl.when(coarse_flag)
    def _():
        for c in range(keys // (2 * chunk)):
            at = pl.ds(pl.multiple_of((2 * c + 1 - own_half) * chunk, chunk), chunk)
            for head in range(2):
                e_ref[head, at, :] = jnp.zeros((chunk, queries), BF16)

    fits = jnp.logical_and(least > 1e-20, largest < 1e25)

    @pl.when(jnp.min(fits.astype(F32)) < 0.5)
    def _():
        for head in range(2):
            queries_one = head_lanes(q_ref[...], head)

            def scores(c):
                at = pl.ds(pl.multiple_of(c * chunk, chunk), chunk)
                hidden = jnp.logical_and(coarse > 0.5, lax.rem(c, 2) != own_half)
                return at, hidden, jnp.where(hidden, -1e30, dot(k_ref[at, :], queries_one, (1, 1)))

            def highest_step(c, top):
                return jnp.maximum(top, jnp.max(scores(c)[2], axis=0, keepdims=True))

            top = lax.fori_loop(0, keys // chunk, highest_step, jnp.full((1, queries), -1e30, F32))

            def total_step(c, total):
                at, hidden, s = scores(c)
                e = jnp.where(hidden, 0.0, jnp.exp(s - top)).astype(BF16)
                e_ref[head, at, :] = e
                return total + dot(vte[head, seen_half, :, at], e)

            total = lax.fori_loop(
                0, keys // chunk, total_step, jnp.zeros((LANES, queries), F32)
            )
            finish(head, total[:HEAD_DIM, :], total[HEAD_DIM : HEAD_DIM + 1, :])


def attend(q, k, v, aux):
    rows, width = q.shape
    keys, queries, pairs = k.shape[0], rows // 2, width // LANES
    return pl.pallas_call(
        functools.partial(attend_kernel, rows),
        grid=(pairs, 2),
        out_shape=[
            jax.ShapeDtypeStruct((2 * pairs, keys, rows), BF16),
            jax.ShapeDtypeStruct((width, rows), BF16),
            jax.ShapeDtypeStruct((8 * pairs, rows), F32),
        ],
        in_specs=[
            pl.BlockSpec((queries, LANES), lambda p, j: (j, p)),
            pl.BlockSpec((keys, LANES), lambda p, j: (0, p)),
            pl.BlockSpec((keys, LANES), lambda p, j: (0, p)),
            pl.BlockSpec(aux.shape, lambda p, j: (0, 0)),
        ],
        out_specs=[
            pl.BlockSpec((2, keys, queries), lambda p, j: (p, 0, j)),
            pl.BlockSpec((LANES, queries), lambda p, j: (p, j)),
            pl.BlockSpec((8, queries), lambda p, j: (p, j)),
        ],
        scratch_shapes=[pltpu.VMEM((2, 2, LANES, keys), BF16)],
        compiler_params=params(),
        name="attend",
    )(q, k, v, aux)


POINT_TIMES = (1.1, 2.2, 2.9, 3.5, 4.2, 4.9)
POINTS = len(POINT_TIMES)


def point(time):
    step = min(int(time / POINT_TIMES[-1]), 5)
    rest = time - step * POINT_TIMES[-1]
    return step * POINTS + next((i for i, end in enumerate(POINT_TIMES) if end >= rest - 0.05), POINTS - 1)


class Task:
    def __init__(self, reduces, total, phases, ends, array=None, begin=0.0):
        self.reduces, self.total, self.phases, self.array = reduces, total, phases, array
        self.ends, self.begin = [point(time) for time in ends], point(begin)


class Early:
    def __init__(self, n1, total, points):
        self.n1, self.total, self.points = n1, total, [point(time) for time in points]

    def shapes(self, n, rows, width, sizes):
        done = width - LANES
        outs = [((rows, done), BF16), ((rows, done), BF16), ((rows_after(sizes, self.total, 2), width), BF16)]
        pairs = done // LANES
        scratch = [
            pltpu.VMEM((rows, width), BF16),
            pltpu.VMEM((width, rows), BF16),
            pltpu.VMEM((pairs, rows, LANES), BF16),
            pltpu.VMEM((pairs, 2, n, rows, LANES), BF16),
            pltpu.VMEM((pairs, 2, n - 1, rows, LANES), BF16),
            pltpu.VMEM((self.total, width), BF16),
            pltpu.SemaphoreType.DMA((1,)),
            pltpu.SemaphoreType.DMA((pairs, 2, n - 1)),
            pltpu.SemaphoreType.DMA((pairs, 2, n - 1)),
        ]
        return outs, scratch + reduce_scratch(sizes, self.total, 0, 1, width)

    def bind(self, axes, place, n1_ref, outs, refs):
        self.place = place
        self.done, result = outs[:2], outs[2]
        self.n1_buf, self.n1_turned, self.dq, self.parts, self.recv, self.g, n1_sem, self.ssem, self.rsem = refs[:9]
        self.reduce = Reduce(axes, self.total, 0, 1, self.g, result, refs[9:])
        self.fetch = pltpu.make_async_copy(n1_ref, self.n1_buf, n1_sem.at[0])

    def copies(self, pair):
        for step in range(1, self.place.n):
            for part in range(2):
                at = pair, part, step - 1
                yield send(
                    self.parts.at[pair, part, step], self.recv.at[at], self.ssem.at[at], self.rsem.at[at], self.place.peer(step)
                )

    def start(self, pair, dk, dv):
        for part, total in enumerate((dk, dv)):
            self.parts[pair, part] = total.reshape(self.parts.shape[2:]).astype(BF16)
        for copy in self.copies(pair):
            copy.start()

    def finish(self, pair):
        if pair == 0:
            self.fetch.wait()
            self.n1_turned[...] = turned(self.n1_buf[...])
        for copy in self.copies(pair):
            copy.wait()
        own = [self.dq[pair]]
        for part in range(2):
            total = self.parts[pair, part, 0].astype(F32)
            for step in range(self.place.n - 1):
                total = total + self.recv[pair, part, step].astype(F32)
            own.append(total.astype(BF16))
            self.done[part][:, pair * LANES : (pair + 1) * LANES] = own[-1]
        width = self.n1_buf.shape[1]
        put = dot(self.n1_turned[...], jnp.concatenate(own, axis=1)).astype(BF16)
        self.g[pair * width : (pair + 1) * width, :] = put
        if pair == self.dq.shape[0] - 1:
            end = (pair + 1) * width
            if self.total > end:
                self.g[end:, :] = jnp.zeros((self.total - end, width), BF16)
            self.reduce.own().start()
            self.reduce.start(0)

    def schedule(self):
        pairs = self.dq.shape[0]
        acts = [functools.partial(self.finish, pair) for pair in range(pairs)] + [self.reduce.act(0), self.reduce.act(1)]
        return zip(self.points, acts)


def attend_back_kernel(n, chips, tasks, early, *refs):
    q_ref, k_ref, v_ref, e_ref, do_ref, dl_ref = refs[:6]
    refs = refs[6:]
    if early:
        n1_ref, refs = refs[0], refs[1:]
    given = sum(task.array is not None for task in tasks)
    sources, refs = list(refs[:given]), refs[given:]
    dq_ref, dk_ref, dv_ref = refs[:3]
    refs = refs[3:]
    if early:
        early_outs, refs = refs[:3], refs[3:]
    results, refs = refs[: len(tasks)], refs[len(tasks) :]
    kt, vext, dk_sum, dv_sum, rhs = refs[:5]
    refs = refs[5:]
    t = pl.program_id(0) * pl.num_programs(1) + pl.program_id(1)
    keys, queries = e_ref.shape[1:]

    axes = Axes(n, chips)
    bar = pltpu.get_barrier_semaphore()
    met = sum(size - 1 for size in axes.sizes) + (n - 1 if early else 0)
    schedule = {0: [lambda: pl.semaphore_wait(bar, met)]}
    reduces = []
    begin = 0
    if early:
        place = Place(n)
        early.bind(axes, place, n1_ref, early_outs, refs[:15])
        refs = refs[15:]
        for end, act in early.schedule():
            schedule.setdefault(end, []).append(act)
    for index, (task, result) in enumerate(zip(tasks, results)):
        if task.array is None:
            source, begin = results[index - 1], tasks[index - 1].ends[-1]
        else:
            source, begin = sources.pop(0), task.begin
        first, last = task.phases[0], task.phases[-1]
        count = (4 + len(task.phases)) if task.reduces else 3
        scratch, refs = refs[:count], refs[count:]
        if task.reduces:
            move = Reduce(axes, task.total, first, last, source, result, scratch)
            reduces.append(move)
        else:
            move = Gather(axes, task.total, first, last, source, result, scratch)
        schedule.setdefault(begin, []).append(functools.partial(move.start, first))
        for phase, end in zip(task.phases, task.ends):
            schedule.setdefault(end, []).append(move.act(phase))

    def points(part):
        for place_of in sorted(schedule):
            if place_of % POINTS == part:

                @pl.when(t == place_of // POINTS)
                def _():
                    for act in schedule[place_of]:
                        act()

    @pl.when(t == 0)
    def _():
        axes.greet(bar)
        if early:
            for step in range(1, n):
                signal(bar, place.peer(step))
            early.fetch.start()
        for reduce in reduces:
            reduce.own().start()

    @pl.when(pl.program_id(1) == 0)
    def _():
        kt[...] = k_ref[...].astype(F32).T.astype(BF16)
        vext[:, :LANES] = v_ref[...]
        vext[:, LANES:] = jnp.ones((keys, LANES), BF16)
        dk_sum[...] = jnp.zeros_like(dk_sum)
        dv_sum[...] = jnp.zeros_like(dv_sum)

    do = do_ref[...].astype(F32)
    row_head = lax.broadcasted_iota(jnp.int32, (LANES, 1), 0) // HEAD_DIM
    for head in range(2):
        rhs[head, :LANES, :] = jnp.where(row_head == head, do, 0.0).astype(BF16)
        rhs[head, LANES : LANES + 16, :] = dl_ref[16 * head : 16 * head + 16, :]
        rhs[head, LANES + 16 :, :] = jnp.zeros((LANES - 16, queries), BF16)
    do_rows = jnp.concatenate([rhs[head, :LANES, :].astype(F32).T.astype(BF16) for head in range(2)], axis=0)
    q_rows = jnp.concatenate([head_lanes(q_ref[...], head) for head in range(2)], axis=0)
    ds, dq = [], []
    for head in range(2):
        ds.append((e_ref[head].astype(F32) * dot(vext[...], rhs[head])).astype(BF16))
        dq.append(dot(kt[...], ds[head])[head * HEAD_DIM : (head + 1) * HEAD_DIM])
        points(head)
    halves = [pl.ds(0, keys // 2), pl.ds(keys // 2, keys // 2)]
    for part, at in enumerate(halves):
        dv_sum[at, :] += dot(jnp.concatenate([e_ref[0, at, :], e_ref[1, at, :]], axis=1), do_rows)
        points(2 + part)
    ds = jnp.concatenate(ds, axis=1)
    for part, at in enumerate(halves):
        dk_sum[at, :] += dot(ds[part * (keys // 2) : (part + 1) * (keys // 2)], q_rows)
        if part == 0:
            points(4)
    dq_rows = (jnp.concatenate(dq, axis=0) * HEAD_DIM**-0.5).T.astype(BF16)
    dq_ref[...] = dq_rows
    whole_pair = pl.program_id(1) == pl.num_programs(1) - 1
    if early:
        pair = pl.program_id(0)

        @pl.when(pair < pl.num_programs(0) - 1)
        def _():
            early.dq[pair, pl.ds(pl.multiple_of(pl.program_id(1) * queries, 16), queries), :] = dq_rows

        @pl.when(jnp.logical_and(pair < pl.num_programs(0) - 1, whole_pair))
        def _():
            early.start(pair, dk_sum[...], dv_sum[...])

        whole_pair = jnp.logical_and(pair == pl.num_programs(0) - 1, whole_pair)

    @pl.when(whole_pair)
    def _():
        dk_ref[...] = dk_sum[...].astype(BF16)
        dv_ref[...] = dv_sum[...].astype(BF16)

    points(5)


def attend_back(n, chips, collective_id, q, k, v, e, do, dl, tasks, early=None):
    sizes = sum_sizes(n, chips)
    rows, width = q.shape
    keys, queries, pairs = k.shape[0], rows // 2, width // LANES
    scratch, results = [], []
    for task in tasks:
        first, last = task.phases[0], task.phases[-1]
        if task.reduces:
            scratch += reduce_scratch(sizes, task.total, first, last, width)
            height = rows_after(sizes, task.total, last + 1)
        else:
            scratch += gather_scratch(sizes, first, last)
            height = rows_after(sizes, task.total, last)
        results.append(jax.ShapeDtypeStruct((height, width), BF16))
    key_width, key_spec = width, pl.BlockSpec((keys, LANES), lambda p, j: (0, p))
    early_outs = []
    if early:
        key_width, key_spec = LANES, pl.BlockSpec((keys, LANES), lambda p, j: (0, 0))
        outs, early_scratch = early.shapes(n, rows, width, sizes)
        early_outs = [jax.ShapeDtypeStruct(*out) for out in outs]
        scratch = early_scratch + scratch
    return pl.pallas_call(
        functools.partial(attend_back_kernel, n, chips, tasks, early),
        grid=(pairs, 2),
        out_shape=[
            jax.ShapeDtypeStruct((rows, width), BF16),
            jax.ShapeDtypeStruct((keys, key_width), BF16),
            jax.ShapeDtypeStruct((keys, key_width), BF16),
        ]
        + early_outs
        + results,
        in_specs=[
            pl.BlockSpec((queries, LANES), lambda p, j: (j, p)),
            pl.BlockSpec((keys, LANES), lambda p, j: (0, p)),
            pl.BlockSpec((keys, LANES), lambda p, j: (0, p)),
            pl.BlockSpec((2, keys, queries), lambda p, j: (p, 0, j)),
            pl.BlockSpec((LANES, queries), lambda p, j: (p, j)),
            pl.BlockSpec((32, queries), lambda p, j: (p, j)),
        ]
        + [ANY] * (1 if early else 0)
        + [ANY if task.reduces and task.phases[0] == 0 else VMEM for task in tasks if task.array is not None],
        out_specs=[
            pl.BlockSpec((queries, LANES), lambda p, j: (j, p)),
            key_spec,
            key_spec,
        ]
        + [VMEM] * len(early_outs)
        + [VMEM if task.reduces else ANY for task in tasks],
        scratch_shapes=[
            pltpu.VMEM((LANES, keys), BF16),
            pltpu.VMEM((keys, 2 * LANES), BF16),
            pltpu.VMEM((keys, LANES), F32),
            pltpu.VMEM((keys, LANES), F32),
            pltpu.VMEM((2, 2 * LANES, queries), BF16),
        ]
        + scratch,
        compiler_params=params(collective_id),
        name="attend_back",
    )(q, k, v, e, do, dl, *([early.n1] if early else []), *[task.array for task in tasks if task.array is not None])


def mlp_block(at, h, ob, w_out, gain2, w1, b1, w2, h2_ref, n2_ref, a_ref, gp_ref):
    h2 = h + dot(ob, w_out[...], (0, 0))
    h2_ref[at, :] = h2
    n2 = (normalize(h2)[0] * gain2[...]).astype(BF16)
    n2_ref[at, :] = n2
    u = dot(n2, w1[...]) + b1[...]
    square = u * u
    t = jnp.tanh(gelu_in * u * (1.0 + gelu_cubic * square))
    half = 0.5 + 0.5 * t
    a = (u * half).astype(BF16)
    a_ref[at, :] = a
    slope = half + (0.5 * gelu_in) * u * (1.0 - t * t) * (1.0 + 3.0 * gelu_cubic * square)
    gp_ref[at, :] = slope.astype(BF16)
    return h2 + dot(a, w2[...])


def middle_kernel(
    n, late, gain2, b1, gain1, h2_out, n2_out, a_out, gp_out, h3_out, n1_out, q_out, k_all, v_all,
    h2_ref, n2_ref, a_ref, gp_ref, h3_ref, n1_ref, q_ref, ship_sems, kbuf, vbuf, ksem, krsem, lsem,
):
    h, ob, w_out, w1, w2, w = late
    place = Place(n)
    rows, width = h.shape
    block = rows // 2
    bar = pltpu.get_barrier_semaphore()
    for step in range(1, n):
        signal(bar, place.peer(step))
    keys = Keys(place, (k_all, v_all), (kbuf, vbuf), ksem, krsem, lsem)
    ship = Ship(ship_sems)
    gain2, b1 = gain2.at[pl.ds(0, 1)], b1.at[pl.ds(0, 1)]
    pairs = ((h2_ref, h2_out), (n2_ref, n2_out), (a_ref, a_out), (gp_ref, gp_out), (h3_ref, h3_out), (n1_ref, n1_out), (q_ref, q_out))
    for i in range(rows // block):
        at = pl.ds(i * block, block)
        h3 = mlp_block(at, h[at, :], ob[:, at], w_out, gain2, w1, b1, w2, h2_ref, n2_ref, a_ref, gp_ref)
        h3_ref[at, :] = h3
        n1 = (normalize(h3)[0] * gain1[1:2, :]).astype(BF16)
        n1_ref[at, :] = n1
        kv = dot(n1, w[:, width:]).astype(BF16)
        if i == 0:
            pl.semaphore_wait(bar, n - 1)
        keys.start(i, at, kv)
        q_ref[at, :] = (dot(n1, w[:, :width]) * HEAD_DIM**-0.5).astype(BF16)
        for src, dst in pairs:
            ship(src.at[at], dst.at[at])
    keys.finish()
    ship.finish()


def middle(n, collective_id, h, ob, w_out, gain2, w1, b1, w2, gain1, w):
    rows, width = h.shape
    hidden = w1.shape[2]
    blocks = 2
    shapes = [
        ((rows, width), F32), ((rows, width), BF16), ((rows, hidden), BF16), ((rows, hidden), BF16), ((rows, width), F32),
        ((rows, width), BF16), ((rows, width), BF16),
    ]
    return run(
        functools.partial(middle_kernel, n),
        "middle",
        collective_id,
        [h, ob, (w_out, 0), (w1, 0), (w2, 0), (w, 1)],
        [gain2, b1, gain1],
        [VMEM] * 3,
        [jax.ShapeDtypeStruct(*shape) for shape in shapes] + [jax.ShapeDtypeStruct((n, rows, width), BF16)] * 2,
        [ANY] * 9,
        [pltpu.VMEM(*shape) for shape in shapes]
        + [pltpu.SemaphoreType.DMA((blocks * len(shapes),))]
        + keys_scratch(n, rows, width, blocks),
    )


def mlp_back_block(at, dh, gp, h2, ob, li, w_out, gain2, w1, w2, dz_ref, du_ref, dy_ref, dh2_ref, do_ref, dl_ref):
    dz = dh.astype(BF16)
    dz_ref[at, :] = dz
    du = (dot(dz, w2[...], (1, 1)) * gp.astype(F32)).astype(BF16)
    du_ref[at, :] = du
    bias_sum = column_sum(du.astype(F32))
    dn2 = dot(du, w1[...], (1, 1))
    xhat, rstd = normalize(h2)
    gain_sum = column_sum(dn2 * xhat)
    dh2 = dh + normalize_back(dn2 * gain2[...], xhat, rstd)
    dh2_ref[at, :] = dh2
    dy = dh2.astype(BF16)
    dy_ref[at, :] = dy
    do = dot(w_out[...], dy, (1, 1))
    product = do * ob.astype(F32)
    for head in range(do.shape[0] // HEAD_DIM):
        rows = slice(head * HEAD_DIM, (head + 1) * HEAD_DIM)
        inverse = li[8 * (head // 2) + head % 2 : 8 * (head // 2) + head % 2 + 1, :]
        do_ref[rows, at] = (do[rows] * inverse).astype(BF16)
        rest = -column_sum(product[rows]) * inverse
        terms = []
        for _ in range(3):
            terms.append(rest.astype(BF16).astype(F32))
            rest = rest - terms[-1]
        row = lax.broadcasted_iota(jnp.int32, (16, 1), 0)
        block = jnp.where(row == 0, terms[0], jnp.where(row == 1, terms[1], jnp.where(row == 2, terms[2], 0.0)))
        dl_ref[16 * head : 16 * head + 16, at] = block.astype(BF16)
    return bias_sum, gain_sum


def fc1_sums(g_ref, n2, du):
    width = n2.shape[1]
    n2_turned = turned(n2[...])
    for part in range(du.shape[1] // width):
        at = slice(part * width, (part + 1) * width)
        g_ref[at, :] = dot(n2_turned, du[:, at]).astype(BF16)
    return du.shape[1]


def fill(g_ref, at):
    if g_ref.shape[0] > at:
        g_ref[at:, :] = jnp.zeros((g_ref.shape[0] - at, g_ref.shape[1]), BF16)


def put_rows(small_ref, row, value, width):
    for part in range(value.shape[1] // width):
        small_ref[row + part : row + part + 1, :] = value[:, part * width : (part + 1) * width]


def back_shapes(rows, width):
    return [
        jax.ShapeDtypeStruct((rows, width), F32),
        jax.ShapeDtypeStruct((width, rows), BF16),
        jax.ShapeDtypeStruct((16 * width // HEAD_DIM, rows), BF16),
    ]


def turn_kernel(
    late, li_ref, aux_ref, gain2, b1, fgain, head_w, head_b, prior_ref,
    g2_out, g1_out, small_ref, dh2_out, do_out, dl_out, expert_ref, head_ref, out_ref,
    g2_ref, g1_ref, dh2_ref, do_ref, dl_ref, dz, du, dy, h2_ref, n2_ref, a_ref, gp_ref, wide, tall, ship_sems,
):
    h_ref, ob_ref, w_out, w1, w2 = late
    rows, width = h_ref.shape
    gain2, b1 = gain2.at[pl.ds(1, 1)], b1.at[pl.ds(1, 1)]
    block = rows // 2
    ship = Ship(ship_sems)
    wide[...] = jnp.zeros_like(wide)
    wide[0:EXPERTS, :] = head_w[...]
    hw = wide[...]
    fgain_row = fgain[...].reshape(1, width)
    tall[...] = jnp.ones_like(tall)
    tall[0:EXPERTS, 0:LEADS] = prior_ref[...]
    logp = jnp.log(tall[...])
    tall[...] = jnp.zeros_like(tall)
    tall[0:1, 0:EXPERTS] = head_b[...]
    hb = jnp.sum(jnp.where(diagonal((8, LANES)), tall[0:1, :], 0.0), axis=1, keepdims=True)
    lane = lax.broadcasted_iota(jnp.int32, (8, LANES), 1).astype(F32)
    expert = lax.broadcasted_iota(jnp.int32, (8, 1), 0)
    bias_sum, gain_sum, final_sum, head_sum, hbias_sum, lead_sum = 0.0, 0.0, 0.0, 0.0, 0.0, 0.0
    for i in range(2):
        at = pl.ds(i * block, block)
        h3 = mlp_block(at, h_ref[at, :], ob_ref[:, at], w_out, gain2, w1, b1, w2, h2_ref, n2_ref, a_ref, gp_ref)
        xhat, rstd = normalize(h3)
        nf = xhat * fgain_row
        own_lead = lane == aux_ref[LEAD_ROW + i : LEAD_ROW + i + 1, 0:1]
        prior = jnp.sum(jnp.where(own_lead, logp, 0.0), axis=1, keepdims=True)
        logits = dot_split(hw, nf, (1, 1)) + hb - prior
        logits = jnp.where(expert < EXPERTS, logits, -1e30)
        power = jnp.exp(logits - jnp.max(logits, axis=0, keepdims=True))
        weights = power / jnp.sum(power, axis=0, keepdims=True)
        expert_ref[:, at] = weights
        counted = jnp.where(expert == EXPERTS, 1.0, weights)
        lead_sum = lead_sum + jnp.where(own_lead, jnp.sum(counted, axis=1, keepdims=True), 0.0)
        cot = jnp.where(expert < EXPERTS, aux_ref[:, at], 0.0)
        dlogits = weights * (cot - jnp.sum(weights * cot, axis=0, keepdims=True))
        head_sum = head_sum + dot_split(dlogits, nf)
        hbias_sum = hbias_sum + jnp.sum(dlogits, axis=1, keepdims=True)
        dnf = dot_split(dlogits, hw, (0, 0))
        final_sum = final_sum + column_sum(dnf * xhat)
        dh = normalize_back(dnf * fgain_row, xhat, rstd)
        sums = mlp_back_block(
            at, dh, gp_ref[at, :], h2_ref[at, :], ob_ref[:, at], li_ref[:, at], w_out, gain2, w1, w2,
            dz, du, dy, dh2_ref, do_ref, dl_ref,
        )
        bias_sum, gain_sum = bias_sum + sums[0], gain_sum + sums[1]
        ship(dh2_ref.at[at], dh2_out.at[at])
        ship(do_ref.at[:, at], do_out.at[:, at])
        ship(dl_ref.at[:, at], dl_out.at[:, at])
    small_ref[...] = jnp.zeros_like(small_ref)
    put_rows(small_ref, 0, gain_sum, width)
    put_rows(small_ref, 1, final_sum, width)
    put_rows(small_ref, 4, bias_sum, width)
    head_ref[0:8, :] = head_sum
    head_ref[8:16, :] = jnp.zeros((8, width), F32)
    head_ref[8:16, 0:LANES] = lead_sum
    head_ref[16:24, :] = jnp.broadcast_to(hbias_sum, (8, width))
    g2_ref[: a_ref.shape[1], :] = dot(a_ref[...], dz[...], (0, 0)).astype(BF16)
    fill(g2_ref, a_ref.shape[1])
    ship(g2_ref, g2_out)
    fill(g1_ref, fc1_sums(g1_ref, n2_ref, du))
    ship(g1_ref, g1_out)
    out_ref[...] = dot(ob_ref[...], dy[...]).astype(BF16)
    ship.finish()


def turn(h, ob, li, aux, w_out, gain2, w1, b1, w2, fgain, head_w, head_b, prior, grad_rows):
    rows, width = h.shape
    hidden = w1.shape[2]
    grads = [jax.ShapeDtypeStruct((grad_rows, width), BF16)] * 2
    shapes = back_shapes(rows, width)
    return run(
        turn_kernel,
        "turn",
        None,
        [h, ob, (w_out, 1), (w1, 1), (w2, 1)],
        [li, aux, gain2, b1, fgain, head_w, head_b, prior],
        [VMEM] * 8,
        grads
        + [jax.ShapeDtypeStruct((8, width), F32)]
        + shapes
        + [
            jax.ShapeDtypeStruct((8, rows), F32),
            jax.ShapeDtypeStruct((24, width), F32),
            jax.ShapeDtypeStruct((width, width), BF16),
        ],
        [ANY, ANY, VMEM, ANY, ANY, ANY, VMEM, VMEM, VMEM],
        [pltpu.VMEM(shape.shape, shape.dtype) for shape in grads + shapes]
        + [
            pltpu.VMEM((rows, width), BF16),
            pltpu.VMEM((rows, hidden), BF16),
            pltpu.VMEM((rows, width), BF16),
            pltpu.VMEM((rows, width), F32),
            pltpu.VMEM((rows, width), BF16),
            pltpu.VMEM((rows, hidden), BF16),
            pltpu.VMEM((rows, hidden), BF16),
            pltpu.VMEM((8, width), F32),
            pltpu.VMEM((8, LANES), F32),
            pltpu.SemaphoreType.DMA((8,)),
        ],
    )


class KeyGrads:
    def __init__(self, place, parts, own, recv, dkv, ssem, rsem):
        self.place, self.parts, self.own, self.recv, self.dkv, self.ssem, self.rsem = place, parts, own, recv, dkv, ssem, rsem

    def copies(self):
        for step in range(1, self.place.n):
            for part, src in enumerate(self.parts):
                at = step - 1, part
                yield send(src.at[step], self.recv.at[at], self.ssem.at[at], self.rsem.at[at], self.place.peer(step))

    def start(self):
        for copy in self.copies():
            copy.start()

    def finish(self):
        for copy in self.copies():
            copy.wait()
        width = self.dkv.shape[1] // 2
        for part, own in enumerate(self.own):
            total = own[...].astype(F32)
            for step in range(self.place.n - 1):
                total = total + self.recv[step, part].astype(F32)
            self.dkv[:, part * width : (part + 1) * width] = total.astype(BF16)


def key_scratch(n, rows, width):
    return [
        pltpu.VMEM((n - 1, 2, rows, width), BF16),
        pltpu.VMEM((rows, 2 * width), BF16),
        pltpu.SemaphoreType.DMA((n - 1, 2)),
        pltpu.SemaphoreType.DMA((n - 1, 2)),
    ]


def project_back_block(at, dn1_q, dkv, w, gain_row, h, dh2):
    width = h.shape[1]
    dn1 = dn1_q + dot(dkv[at, :], w[:, width:], (1, 1))
    xhat, rstd = normalize(h[at, :])
    return dh2[at, :] + normalize_back(dn1 * gain_row, xhat, rstd), column_sum(dn1 * xhat)


def key_weight_sums(g_ref, n1_turned, dkv):
    width = n1_turned.shape[0]
    for part in range(2):
        at = slice(part * width, (part + 1) * width)
        g_ref[(part + 1) * width : (part + 2) * width, :] = dot(n1_turned, dkv[:, at]).astype(BF16)


def between_kernel(
    n, chips, late, dk, dv, gain1, li_ref, gain2,
    norm_ref, small_ref, g1_out, dh2_out, do_out, dl_out, fc2_out, fc1_out, qkv_next, fc2_next_ref,
    gq_ref, g2_ref, g1_ref, dh2_ref, do_ref, dl_ref, dz, du, dy, ship_sems, krecv, dkv, ksem, krsem, *refs,
):
    n1, dq, fc2_src, fc1_src, dk_own, dv_own, w, h3, dh2_in, out_b, a, w2, gp, w1, h2_ref, w_out, ob_ref, n2_ref = late
    place, axes = Place(n), Axes(n, chips)
    rows, width = dq.shape
    hidden = a.shape[1]
    block = rows // 2
    bar = pltpu.get_barrier_semaphore()
    met = axes.greet(bar)
    for step in range(1, n):
        signal(bar, place.peer(step))
    ship = Ship(ship_sems)
    refs = list(refs)
    take = lambda count: [refs.pop(0) for _ in range(count)]
    fc2 = Gather(axes, fc2_out.shape[0], 2, 0, fc2_src.buf, fc2_out, take(3))
    fc1 = Gather(axes, fc1_out.shape[0], 3, 0, fc1_src.buf, fc1_out, take(3))
    qkv = Reduce(axes, gq_ref.shape[0], 0, 2, gq_ref, qkv_next, take(7))
    fc2_next = Reduce(axes, g2_ref.shape[0], 0, 1, g2_ref, fc2_next_ref, take(6))
    keys = KeyGrads(place, (dk, dv), (dk_own, dv_own), krecv, dkv, ksem, krsem)

    n1_turned = turned(n1[...])
    gq_ref[:width, :] = dot(n1_turned, dq[...]).astype(BF16)
    fc2_src.ready()
    fc1_src.ready()
    pl.semaphore_wait(bar, met + n - 1)
    keys.start()
    fc2.start(2)
    fc1.start(3)
    dn1_q = [dot(dq[pl.ds(i * block, block), :], w[:, :width], (1, 1)) for i in range(2)]
    keys.finish()
    gain_sum = 0.0
    dh = []
    for i in range(2):
        at = pl.ds(i * block, block)
        dh_one, part = project_back_block(at, dn1_q[i], dkv, w, gain1[1:2, :], h3, dh2_in)
        dh.append(dh_one)
        dz[at, :] = dh_one.astype(BF16)
        gain_sum = gain_sum + part
    norm_ref[...] = jnp.broadcast_to(gain_sum, norm_ref.shape)
    fc2.finish_start(2)
    key_weight_sums(gq_ref, n1_turned, dkv)
    gq_ref[3 * width : 4 * width, :] = out_b[...]
    fill(gq_ref, 4 * width)
    qkv.own().start()
    qkv.start(0)
    g2_ref[:hidden, :] = dot(a[...], dz[...], (0, 0)).astype(BF16)
    fill(g2_ref, hidden)
    fc2_next.own().start()
    fc2_next.start(0)
    fc1.finish_start(3)
    bias_sum, gain_sum = 0.0, 0.0
    parts = min(4, rows // LANES)
    quarter = rows // parts
    acts = [
        [qkv.act(0), fc2_next.act(0)],
        [fc1.act(2)],
        [fc2.act(1), qkv.act(1)],
        [],
    ]
    dh = jnp.concatenate(dh, axis=0)
    for i in range(parts):
        at = pl.ds(i * quarter, quarter)
        dh_one = dh[i * quarter : (i + 1) * quarter]
        sums = mlp_back_block(
            at, dh_one, gp[at, :], h2_ref[at, :], ob_ref[:, at], li_ref[:, at], w_out, gain2.at[pl.ds(0, 1)], w1, w2,
            dz, du, dy, dh2_ref, do_ref, dl_ref,
        )
        bias_sum, gain_sum = bias_sum + sums[0], gain_sum + sums[1]
        for group in acts[i * 4 // parts : (i + 1) * 4 // parts]:
            for act in group:
                act()
        ship(dh2_ref.at[at], dh2_out.at[at])
        ship(do_ref.at[:, at], do_out.at[:, at])
        ship(dl_ref.at[:, at], dl_out.at[:, at])
    small_ref[...] = jnp.zeros_like(small_ref)
    put_rows(small_ref, 0, gain_sum, width)
    put_rows(small_ref, 4, bias_sum, width)
    at = fc1_sums(g1_ref, n2_ref, du)
    g1_ref[at : at + width, :] = dot(ob_ref[...], dy[...]).astype(BF16)
    fill(g1_ref, at + width)
    ship(g1_ref, g1_out)
    fc1.finish_start(1)
    fc2.finish(0)
    fc2_next.finish(1)
    qkv.finish(2)
    fc1.finish(0)
    ship.finish()


def between(
    n, chips, collective_id, totals, dq, dk, dv, n1, h3, dh2, w, gain1, gp, h2, ob, li, n2, a, w_out, gain2, w1, w2, out_b, fc2, fc1
):
    rows, width = dq.shape
    hidden = a.shape[1]
    sizes = sum_sizes(n, chips)
    half = lambda height: jax.ShapeDtypeStruct((height, width), BF16)
    kept = [half(totals[4])] + back_shapes(rows, width)
    return run(
        functools.partial(between_kernel, n, chips),
        "between",
        collective_id,
        [n1, dq, fc2, fc1, (dk, 0), (dv, 0), (w, 1), h3, dh2, out_b, a, (w2, 0), gp, (w1, 0), h2, (w_out, 0), ob, n2],
        [dk, dv, gain1, li, gain2],
        [ANY, ANY, VMEM, VMEM, VMEM],
        [jax.ShapeDtypeStruct((8, width), F32)] * 2
        + kept
        + [
            half(totals[0]),
            half(totals[1]),
            half(rows_after(sizes, totals[2], 3)),
            half(rows_after(sizes, totals[3], 2)),
        ],
        [VMEM, VMEM] + [ANY] * 6 + [VMEM, VMEM],
        [pltpu.VMEM((totals[2], width), BF16), pltpu.VMEM((totals[3], width), BF16)]
        + [pltpu.VMEM(shape.shape, shape.dtype) for shape in kept]
        + [
            pltpu.VMEM((rows, width), BF16),
            pltpu.VMEM((rows, hidden), BF16),
            pltpu.VMEM((rows, width), BF16),
            pltpu.SemaphoreType.DMA((13,)),
        ]
        + key_scratch(n, rows, width)
        + gather_scratch(sizes, 2, 0)
        + gather_scratch(sizes, 3, 0)
        + reduce_scratch(sizes, totals[2], 0, 2, width)
        + reduce_scratch(sizes, totals[3], 0, 1, width),
    )


def last_axes(n, chips):
    return DirectAxes if n * chips <= 16 else Axes


def last_kernel(
    n, chips, late, dk, dv, gain, aux, expert, norm_b, small_a, small_b, head,
    tg_out, ex_out, fc2_out, fc1_out, early_ref, sum_ref,
    tg, g_ref, own_shard, early_shard, krecv, dkv, ksem, krsem, ssem, rsem, *refs,
):
    n1, dq, fc2_src, fc1_src, early, dk_own, dv_own, w, dk_done, dv_done, h, dh2 = late
    place, axes = Place(n), Axes(n, chips)
    direct = last_axes(n, chips)(n, chips)
    rows, width = dq.shape
    block = rows // 2
    bar = pltpu.get_barrier_semaphore()
    met = axes.greet(bar) + direct.greet(bar) + n - 1
    for step in range(1, n):
        signal(bar, place.peer(step))

    @pl.when(place.moves)
    def _():
        signal(bar, place.partner)

    refs = list(refs)
    take = lambda count: [refs.pop(0) for _ in range(count)]
    top = len(direct.sizes) - 1
    fc2 = Gather(axes, fc2_out.shape[0], 1, 0, fc2_src.buf, fc2_out, take(3))
    fc1 = Gather(axes, fc1_out.shape[0], 3, 0, fc1_src.buf, fc1_out, take(3))
    early_reduce = Reduce(axes, early_ref.shape[0], 2, 3, early.buf, early_shard, take(6))
    if last_axes(n, chips) is DirectAxes:
        early_gather = Spread(axes, direct, early_ref.shape[0], early_shard, early_ref, take(3))
    else:
        early_gather = Gather(axes, early_ref.shape[0], 3, 0, early_shard, early_ref, take(3))
    reduce = Reduce(direct, g_ref.shape[0], 0, top, g_ref, own_shard, take(5 + top))
    gather = Gather(direct, g_ref.shape[0], top, 0, own_shard, sum_ref, take(3))
    keys = KeyGrads(place, (dk, dv), (dk_own, dv_own), krecv, dkv, ksem, krsem)
    n1_turned = turned(n1[...])
    for array in (fc2_src, fc1_src, early):
        array.ready()

    @pl.when(place.moves)
    def _():
        pl.semaphore_wait(bar, met + 1)

    @pl.when(jnp.logical_not(place.moves))
    def _():
        pl.semaphore_wait(bar, met)

    swaps = [send(expert, ex_out, ssem.at[2], rsem.at[2], place.partner)]
    for i in range(2):
        at = pl.ds(i * block, block)
        swaps.append(send(tg.at[at], tg_out.at[at], ssem.at[i], rsem.at[i], place.partner))

    def swap(index):
        @pl.when(place.moves)
        def _():
            swaps[index].start()

    keys.start()
    swap(0)
    early_reduce.own().start()
    early_reduce.start(2)
    fc1.start(3)
    fc2.start(1)
    done = dk_done.shape[1]
    dn1 = []
    for i in range(2):
        at = pl.ds(i * block, block)
        part = dot(dq[at, :], w[:, :width], (1, 1)) + dot(dk_done[at, :], w[:, width : width + done], (1, 1))
        dn1.append(part + dot(dv_done[at, :], w[:, 2 * width : 2 * width + done], (1, 1)))
    keys.finish()
    early_reduce.finish_start(2)
    fc1.finish_start(3)
    gain_sum = 0.0
    half_sums = []
    for i in range(2):
        at = pl.ds(i * block, block)
        part = dot(dkv[at, :LANES], w[:, width + done : 2 * width], (1, 1))
        part = dn1[i] + part + dot(dkv[at, LANES:], w[:, 2 * width + done :], (1, 1))
        xhat, rstd = normalize(h[at, :])
        gain_sum = gain_sum + column_sum(part * xhat)
        dh = dh2[at, :] + normalize_back(part * gain[0:1, :], xhat, rstd)
        half_sums.append(column_sum(dh))
        tg[at, :] = dh.astype(BF16)
        swap(1 + i)
    lead_index = lax.broadcasted_iota(jnp.int32, (LEADS, 1), 0).astype(F32)
    table = 0.0
    for half in range(2):
        lead = aux[LEAD_ROW + half : LEAD_ROW + half + 1, 0:1]
        table = table + jnp.where(lead_index == lead, half_sums[half], 0.0)
    early_reduce.finish(3)
    early_gather.start(early_gather.first)
    g_ref[:width, :] = dot(n1_turned, jnp.concatenate([dq[:, done:], dkv[...]], axis=1)).astype(BF16)
    at = width
    for piece in (table, jnp.broadcast_to(gain_sum, (8, width)), norm_b[...], small_a[...], small_b[...], head[...]):
        g_ref[at : at + piece.shape[0], :] = piece.astype(BF16)
        at += piece.shape[0]
    g_ref[at:, :] = jnp.zeros((g_ref.shape[0] - at, width), BF16)
    reduce.own().start()
    reduce.start(0)

    @pl.when(jnp.logical_not(place.moves))
    def _():
        tg_out[...] = tg[...]
        ex_out[...] = expert[...]

    def turn_round():
        reduce.finish(top)
        gather.start(top)

    chains = [
        [reduce.act(phase) for phase in range(top)] + [turn_round] + [gather.act(phase) for phase in range(top, -1, -1)],
        [fc1.act(phase) for phase in range(2, -1, -1)],
        [fc2.act(1), fc2.act(0)],
        [early_gather.act(phase) for phase in range(early_gather.first, -1, -1)],
    ]
    for turn_index in range(max(len(chain) for chain in chains)):
        for chain in chains:
            if turn_index < len(chain):
                chain[turn_index]()

    @pl.when(place.moves)
    def _():
        for copy in swaps:
            copy.wait()


def last(
    n, chips, collective_id, rows_last, rows_early, fc2_rows, fc1_rows, dq, dk, dv, dk_done, dv_done, n1, h, dh2, w, gain, aux,
    expert, norm_b, small_a, small_b, head, fc2, fc1, early,
):
    rows, width = dq.shape
    devices = 2 * n * chips
    sizes = sum_sizes(n, chips)
    direct = direct_sizes(n, chips) if last_axes(n, chips) is DirectAxes else sizes
    half = lambda height: jax.ShapeDtypeStruct((height, width), BF16)
    return run(
        functools.partial(last_kernel, n, chips),
        "last",
        collective_id,
        [n1, dq, fc2, fc1, early, (dk, 0), (dv, 0), (w, 0), dk_done, dv_done, h, dh2],
        [dk, dv, gain, aux, expert, norm_b, small_a, small_b, head],
        [ANY, ANY] + [VMEM] * 7,
        [half(rows), jax.ShapeDtypeStruct((8, rows), F32)] + [half(height) for height in (fc2_rows, fc1_rows, rows_early, rows_last)],
        [VMEM, VMEM, ANY, ANY, ANY, ANY],
        [
            pltpu.VMEM((rows, width), BF16),
            pltpu.VMEM((rows_last, width), BF16),
            pltpu.VMEM((rows_last // devices, width), BF16),
            pltpu.VMEM((rows_early // devices, width), BF16),
        ]
        + key_scratch(n, rows, LANES)
        + [pltpu.SemaphoreType.DMA((3,))] * 2
        + gather_scratch(sizes, 1, 0)
        + gather_scratch(sizes, 3, 0)
        + reduce_scratch(sizes, rows_early, 2, 3, width)
        + gather_scratch(direct, len(direct) - 1, 0)
        + reduce_scratch(direct, rows_last, 0, len(direct) - 1, width)
        + gather_scratch(direct, len(direct) - 1, 0),
    )


def unpack_kernel(
    fc2_a, fc2_b, fc1_a, fc1_b, out_a, out_b, first_a, second_a, third_a, q_b, k_b, v_b, small, prior, tg_in, expert_in,
    fc2, fc1, out, qkv, tg, expert, lead_average, norm1, norm2, bias, table, final, head, head_bias,
):
    layer, step = pl.program_id(0), pl.program_id(1)

    def layer_part(own, sources):
        @pl.when(layer == own)
        def _():
            for source, target, at in sources:
                target[0, :, at] = source[...].astype(F32)
            for source_rows, at in turned:
                fc1[0, :, at] = (fc1_a, fc1_b)[own][source_rows, :].astype(F32)

    width = table.shape[1]
    everything = slice(0, width)
    turned = [(slice(i * width, (i + 1) * width), slice(i * width, (i + 1) * width)) for i in range(fc1.shape[2] // width)]
    layer_part(0, [(fc2_a, fc2, everything), (out_a, out, everything)])
    layer_part(1, [(fc2_b, fc2, everything), (out_b, out, everything)])
    thirds = [slice(i * width, (i + 1) * width) for i in range(3)]

    @pl.when(layer == 0)
    def _():
        for pair, source in enumerate((first_a, second_a, third_a)):
            for part in range(3):
                at = part * width + pair * LANES
                qkv[0, :, at : at + LANES] = source[:, part * LANES : (part + 1) * LANES].astype(F32)


    @pl.when(layer == 1)
    def _():
        for source, at in zip((q_b, k_b, v_b), thirds):
            qkv[0, :, at] = source[...].astype(F32)

    tg[...] = tg_in[...]

    @pl.when(jnp.logical_and(layer == 0, step == 0))
    def _():
        rows = small[...].astype(F32)
        for i in range(EXPERTS):
            expert[i] = expert_in[i : i + 1, :]
        table[...] = rows[:LEADS]
        for own in range(2):
            norm1[own : own + 1, :] = rows[ROW_NORM1 + 8 * own : ROW_NORM1 + 8 * own + 1]
            base = ROW_MLP + 8 * own
            norm2[own : own + 1, :] = rows[base : base + 1]
            for part in range(bias.shape[1] // width):
                bias[own : own + 1, part * width : (part + 1) * width] = rows[base + 4 + part : base + 5 + part]
        final[...] = rows[ROW_MLP + 9].reshape(final.shape)
        head[...] = rows[ROW_HEAD : ROW_HEAD + EXPERTS]
        totals = rows[ROW_HEAD + 8 : ROW_HEAD + 16, 0:LEADS]
        means = totals[0:EXPERTS] / jnp.maximum(totals[EXPERTS : EXPERTS + 1], 1.0)
        lead_average[...] = 0.5 * prior[...] + 0.5 * means
        column = rows[ROW_HEAD + 16 : ROW_HEAD + 24, 0:LANES]
        head_bias[...] = column_sum(jnp.where(diagonal((8, LANES)), column, 0.0))[:, 0:EXPERTS]


def unpack(fc2_a, fc2_b, fc1_a, fc1_b, early_a, last_a, qkv_b, prior, token_grad, expert, hidden):
    rows, width = token_grad.shape
    steps = 2
    slab, tall = width // steps, hidden // steps

    def at(own, block, first):
        start = first // block
        if own == 0:
            return pl.BlockSpec((block, width), lambda l, j: (start + jnp.where(l == 0, j, steps - 1), 0))
        return pl.BlockSpec((block, width), lambda l, j: (start + jnp.where(l == 1, j, 0), 0))

    fixed = lambda shape: pl.BlockSpec(shape, lambda l, j: (0,) * len(shape))
    moving = pl.BlockSpec((rows // (2 * steps), width), lambda l, j: (l * steps + j, 0))
    in_specs = [at(own, tall, 0) for _ in range(2) for own in range(2)]
    in_specs += [at(0, slab, hidden), at(1, slab, 3 * width)]
    in_specs += [at(0, slab, 0), at(0, slab, width), at(0, slab, 0)]
    in_specs += [at(1, slab, part * width) for part in range(3)]
    in_specs += [pl.BlockSpec((SMALL_ROWS, width), lambda l, j: (width // SMALL_ROWS, 0)), fixed(prior.shape), moving]
    in_specs += [fixed(expert.shape)]
    small_shapes = [
        (EXPERTS, 1, rows), prior.shape, (2, width), (2, width), (2, hidden), (LEADS, width), (width,),
        (EXPERTS, width), (1, EXPERTS),
    ]
    shapes = [(2, hidden, width), (2, width, hidden), (2, width, width), (2, width, 3 * width)]
    out_specs = [
        pl.BlockSpec((1, tall, width), lambda l, j: (l, j, 0)),
        pl.BlockSpec((1, width, tall), lambda l, j: (l, 0, j)),
        pl.BlockSpec((1, slab, width), lambda l, j: (l, j, 0)),
        pl.BlockSpec((1, slab, 3 * width), lambda l, j: (l, j, 0)),
        moving,
    ] + [fixed(shape) for shape in small_shapes]
    return pl.pallas_call(
        unpack_kernel,
        grid=(2, steps),
        out_shape=[jax.ShapeDtypeStruct(shape, F32) for shape in shapes]
        + [jax.ShapeDtypeStruct((rows, width), BF16)]
        + [jax.ShapeDtypeStruct(shape, F32) for shape in small_shapes],
        in_specs=in_specs,
        out_specs=out_specs,
        compiler_params=params(),
        name="unpack",
    )(*([fc2_a, fc2_b, fc1_a, fc1_b, fc1_a, qkv_b] + [early_a, early_a, last_a] + [qkv_b] * 3 + [last_a, prior, token_grad, expert]))


def on_device(
    tokens, slot_kind, frame_lead, norm1_gain, w_qkv, w_out, norm2_gain, w_fc1, b_fc1, w_fc2,
    lead_table, final_gain, head_w, head_b, lead_prior, gate_cot,
):
    rows, width = tokens.shape[0], tokens.shape[3]
    hidden = w_fc1.shape[2]
    n, devices = lax.axis_size("blk"), lax.axis_size("blk") * lax.axis_size("dp")
    chips = lax.axis_size("dp") // 2
    pad = lambda count: -(-count // (16 * devices)) * 16 * devices
    fc_rows, fc1_rows = pad(hidden), pad(hidden + width)
    rows_b, rows_early, rows_last = pad(4 * width), pad((width // LANES - 1) * width), pad(width + SMALL_ROWS)
    flat = lambda x: x.reshape(n * rows, width)
    split = lambda x: x.reshape(n, rows, width)

    h, n1, q, k, v, aux = project(
        n, 0, tokens.reshape(rows, width), gate_cot.reshape(EXPERTS, 1, rows), slot_kind, frame_lead.reshape(1, 2),
        lead_table, norm1_gain, w_qkv,
    )
    k, v = flat(k), flat(v)
    e, ob, li = attend(q, k, v, aux)
    h2, n2, a, gp, h3, n1b, qb, kb, vb = middle(
        n, 1, h, ob, w_out, norm2_gain, w_fc1, b_fc1, w_fc2, norm1_gain, w_qkv
    )
    kb, vb = flat(kb), flat(vb)
    eb, obb, lib = attend(qb, kb, vb, aux)
    g_fc2_b, g_fc1_b, small_b, dh2, do, dl, expert, head, out_b = turn(
        h3, obb, lib, aux, w_out, norm2_gain, w_fc1, b_fc1, w_fc2,
        final_gain, head_w.T, head_b[None], lead_prior.T, fc_rows,
    )
    dq, dk, dv, _, fc2, fc1 = attend_back(
        n, chips, 2, qb, kb, vb, eb, do, dl,
        [
            Task(True, fc_rows, (0, 1, 2, 3), (3.5, 12.0, 17.8, 23.6), g_fc2_b),
            Task(False, fc_rows, (3,), (29.4,)),
            Task(True, fc_rows, (0, 1, 2, 3), (4.9, 14.7, 20.7, 26.7), g_fc1_b, begin=2.2),
        ],
    )
    norm_b, small_a, g_fc1_a, dh2, do, dl, g_fc2_b, g_fc1_b, qkv_part, fc2 = between(
        n, chips, 3, (fc_rows, fc_rows, rows_b, fc_rows, fc1_rows), dq, split(dk), split(dv), n1b, h3, dh2, w_qkv, norm1_gain,
        gp, h2, ob, li, n2, a, w_out, norm2_gain, w_fc1, w_fc2, out_b, fc2, fc1,
    )
    dq, dk, dv, dk_done, dv_done, early, fc1, _, fc2, _, g_qkv_b = attend_back(
        n, chips, 4, q, k, v, e, do, dl,
        [
            Task(True, fc1_rows, (0, 1, 2, 3), (4.9, 14.7, 21.8, 27.8), g_fc1_a),
            Task(True, fc_rows, (2, 3), (8.0, 13.1), fc2),
            Task(False, fc_rows, (3, 2), (20.5, 27.8)),
            Task(True, rows_b, (3,), (6.0,), qkv_part),
            Task(False, rows_b, (3, 2, 1, 0), (11.9, 16.9, 24.5, 29.4)),
        ],
        Early(n1, rows_early, (13.1, 22.9, 25.6, 29.4)),
    )
    part = lambda x: x.reshape(n, rows, LANES)
    token_grad, expert, g_fc2_a, g_fc1_a, g_early, g_last = last(
        n, chips, 5, rows_last, rows_early, fc_rows, fc1_rows, dq, part(dk), part(dv), dk_done, dv_done, n1, h, dh2, w_qkv,
        norm1_gain, aux, expert, norm_b, small_a, small_b, head, fc2, fc1, early,
    )
    fc2, fc1, out, qkv, token_grad, expert, lead_average, norm1, norm2, bias, table, final, head, head_bias = unpack(
        g_fc2_a, g_fc2_b, g_fc1_a, g_fc1_b, g_early, g_last, g_qkv_b, lead_prior.T, token_grad, expert, hidden
    )
    return (
        expert.reshape(EXPERTS, rows, 1, 1),
        lead_average.T,
        token_grad.reshape(rows, 1, 1, width),
        norm1,
        qkv,
        out,
        norm2,
        fc1,
        bias,
        fc2,
        table,
        final,
        head.T,
        head_bias.reshape(-1),
    )


def solution(mesh):
    return jax.shard_map(
        on_device,
        mesh=mesh,
        in_specs=(P("blk", "dp", None, None), P("dp", None), P("dp", None, None))
        + (P(),) * 12
        + (P(None, "blk", "dp", None),),
        out_specs=(P(None, "blk", "dp", None), P(), P("blk", "dp", None, None)) + (P(),) * 11,
        check_vma=False,
    )
```

```python
import functools
import math

import jax
import jax.numpy as jnp
from jax import lax
from jax.experimental import pallas as pl
from jax.experimental.pallas import tpu as pltpu
from jax.sharding import PartitionSpec as P

HEAD_DIM = 64
LEADS = 40
LAYERS = 2
EXPERTS = 3
LANES = 128
norm_eps = 1e-06
gelu_in = math.sqrt(2.0 / math.pi)
gelu_cubic = 0.044715
MESH = pl.DeviceIdType.MESH
F32 = jnp.float32
BF16 = jnp.bfloat16
VMEM = pl.BlockSpec(memory_space=pltpu.VMEM)
ANY = pl.BlockSpec(memory_space=pl.ANY)

KIND_ROW, LEAD_ROW = 3, 4
ROW_NORM1, ROW_MLP, ROW_HEAD, SMALL_ROWS = 40, 56, 72, 96


class Late:
    def __init__(self, src, buf, sem):
        self.copy, self.buf, self.waiting = pltpu.make_async_copy(src, buf, sem), buf, True
        self.shape = buf.shape
        self.copy.start()

    def ready(self):
        if self.waiting:
            self.copy.wait()
            self.waiting = False
        return self.buf

    def __getitem__(self, at):
        return self.ready()[at]


class Ship:
    def __init__(self, sems):
        self.sems, self.copies = sems, []

    def __call__(self, src, dst):
        self.copies.append(pltpu.make_async_copy(src, dst, self.sems.at[len(self.copies)]))
        self.copies[-1].start()

    def finish(self):
        for copy in self.copies:
            copy.wait()


def run(kernel, name, collective_id, late, ins, in_specs, out_shape, out_specs, scratch):
    late = [item if isinstance(item, tuple) else (item, None) for item in late]
    count = len(late)

    def body(*refs):
        buffers, sems = refs[len(refs) - count - 1 : -1], refs[-1]
        arriving = [
            Late(ref if layer is None else ref.at[layer], buffer, sems.at[i])
            for i, (ref, buffer, (_, layer)) in enumerate(zip(refs[:count], buffers, late))
        ]
        kernel(arriving, *refs[count : len(refs) - count - 1])

    shape = lambda array, layer: array.shape if layer is None else array.shape[1:]
    return pl.pallas_call(
        body,
        out_shape=out_shape,
        in_specs=[ANY] * count + in_specs,
        out_specs=out_specs,
        scratch_shapes=scratch
        + [pltpu.VMEM(shape(array, layer), array.dtype) for array, layer in late]
        + [pltpu.SemaphoreType.DMA((count,))],
        compiler_params=params(collective_id),
        name=name,
    )(*[array for array, _ in late], *ins)


def params(collective_id=None):
    if collective_id is None:
        return pltpu.CompilerParams(vmem_limit_bytes=60 * 2**20)
    return pltpu.CompilerParams(
        vmem_limit_bytes=60 * 2**20, collective_id=collective_id, has_side_effects=True
    )


def dot(a, b, dims=(1, 0)):
    return lax.dot_general(
        a, b, (((dims[0],), (dims[1],)), ((), ())), preferred_element_type=F32
    )


def dot_split(a, b, dims=(1, 0)):
    a_high, b_high = a.astype(BF16), b.astype(BF16)
    a_low, b_low = (a - a_high.astype(F32)).astype(BF16), (b - b_high.astype(F32)).astype(BF16)
    return dot(a_high, b_high, dims) + (dot(a_high, b_low, dims) + dot(a_low, b_high, dims))


def normalize(x):
    centered = x - jnp.mean(x, axis=-1, keepdims=True)
    rstd = lax.rsqrt(jnp.mean(centered * centered, axis=-1, keepdims=True) + norm_eps)
    return centered * rstd, rstd


def normalize_back(dg, xhat, rstd):
    return (
        dg - jnp.mean(dg, axis=-1, keepdims=True) - xhat * jnp.mean(dg * xhat, axis=-1, keepdims=True)
    ) * rstd


def turned(x):
    return x.astype(F32).T.astype(BF16)


def diagonal(shape):
    return lax.broadcasted_iota(jnp.int32, shape, 0) == lax.broadcasted_iota(jnp.int32, shape, 1)


def column_sum(x):
    return jnp.sum(x, axis=0, keepdims=True)


class Place:
    def __init__(self, n):
        self.n = n
        dp, self.b = lax.axis_index("dp"), lax.axis_index("blk")
        self.core, self.e = lax.rem(dp, 2), lax.div(dp, 2)
        half = n // 2
        self.side = lax.div(self.b, half)
        self.moves = self.core != self.side
        far = lax.rem(self.b + half, n)
        self.band = jnp.where(self.moves, far, self.b)
        self.partner = (self.e * 2 + 1 - self.core, far)

    def peer(self, step):
        half = self.n // 2
        band = lax.rem(self.band + step, self.n)
        near = lax.div(band, half) == self.side
        b = jnp.where(near, band, lax.rem(band + half, self.n))
        core = jnp.where(near, self.side, 1 - self.side)
        return (self.e * 2 + core, b)


def signal(sem, device):
    pl.semaphore_signal(sem, inc=1, device_id=device, device_id_type=MESH)


def send(src, dst, ssem, rsem, device):
    return pltpu.make_async_remote_copy(
        src_ref=src, dst_ref=dst, send_sem=ssem, recv_sem=rsem, device_id=device, device_id_type=MESH
    )


def row_step(rows):
    step = 16
    while step * 2 <= 128 and rows % (step * 2) == 0:
        step *= 2
    return step


def add_rows(out, out_at, sources, rows):
    step = row_step(rows)

    def body(i, carry):
        total = 0.0
        for ref, at in sources:
            total = total + ref[pl.ds(pl.multiple_of(at + i * step, 16), step), :].astype(F32)
        out[pl.ds(pl.multiple_of(out_at + i * step, 16), step), :] = total.astype(BF16)
        return carry

    lax.fori_loop(0, rows // step, body, 0)


def sum_sizes(n, chips):
    return [2, n, chips // 4, 4]


def direct_sizes(n, chips):
    return [2, n * chips]


class Axes:
    def __init__(self, n, chips):
        dp, b = lax.axis_index("dp"), lax.axis_index("blk")
        core, e = lax.rem(dp, 2), lax.div(dp, 2)
        inner = chips // 4
        slow, fast = lax.div(e, inner), lax.rem(e, inner)
        self.sizes = sum_sizes(n, chips)
        across = lambda i: (dp, i)
        within = lambda i: ((slow * inner + i) * 2 + core, b)
        along = lambda i: ((i * inner + fast) * 2 + core, b)
        self.index = [core, b, fast, slow]
        self.device = [lambda i: (e * 2 + i, b), across, within, along]
        if n == inner:
            swap = core == 1
            pick_one = lambda f, g: lambda i: tuple(jnp.where(swap, y, x) for x, y in zip(f(i), g(i)))
            self.device[1], self.device[2] = pick_one(across, within), pick_one(within, across)
            self.index[1], self.index[2] = jnp.where(swap, fast, b), jnp.where(swap, b, fast)

    def peers(self, phase):
        size = self.sizes[phase]
        for step in range(1, size):
            i = lax.rem(self.index[phase] + step, size)
            yield step, i, self.device[phase](i)

    def greet(self, bar):
        met = 0
        for phase in range(len(self.sizes)):
            for _, _, device in self.peers(phase):
                signal(bar, device)
                met += 1
        return met


class DirectAxes(Axes):
    def __init__(self, n, chips):
        dp, b = lax.axis_index("dp"), lax.axis_index("blk")
        core, e = lax.rem(dp, 2), lax.div(dp, 2)
        self.sizes = direct_sizes(n, chips)
        self.index = [core, b * chips + e]
        self.device = [lambda i: (e * 2 + i, b), lambda i: (lax.rem(i, chips) * 2 + core, lax.div(i, chips))]


class Region:
    def __init__(self, axes, rows):
        self.axes, self.at, self.rows = axes, [0], [rows]
        for phase in range(len(axes.sizes)):
            self.rows.append(self.rows[-1] // axes.sizes[phase])
            self.at.append(self.at[-1] + axes.index[phase] * self.rows[-1])


class Reduce(Region):
    def __init__(self, axes, total, first, last, src, dst, refs):
        super().__init__(axes, total)
        self.first, self.last, self.src, self.dst = first, last, src, dst
        self.work, *recv, self.ssem, self.rsem, self.lsem = refs
        self.recv = dict(zip(range(first, last + 1), recv))

    def own(self):
        rows = self.rows[self.first + 1]
        at = pl.ds(pl.multiple_of(self.at[self.first + 1] - self.at[self.first], 16), rows)
        return pltpu.make_async_copy(self.src.at[at], self.work, self.lsem.at[0])

    def copies(self, phase):
        rows = self.rows[phase + 1]
        base = self.at[self.first] if phase == self.first else self.at[self.first + 1]
        src = self.src if phase == self.first else self.work
        for step, i, device in self.axes.peers(phase):
            begin = pl.multiple_of(self.at[phase] - base + i * rows, 16)
            at = phase - self.first, step - 1
            yield send(src.at[pl.ds(begin, rows)], self.recv[phase].at[step - 1], self.ssem.at[at], self.rsem.at[at], device)

    def start(self, phase):
        for copy in self.copies(phase):
            copy.start()

    def finish(self, phase):
        if phase == self.first:
            self.own().wait()
        for copy in self.copies(phase):
            copy.wait()
        at = self.at[phase + 1] - self.at[self.first + 1]
        sources = [(self.work, at)] + [(self.recv[phase].at[i], 0) for i in range(self.axes.sizes[phase] - 1)]
        if phase < self.last:
            add_rows(self.work, at, sources, self.rows[phase + 1])
        else:
            add_rows(self.dst, 0, sources, self.rows[phase + 1])

    def finish_start(self, phase):
        self.finish(phase)
        self.start(phase + 1)

    def act(self, phase):
        return functools.partial(self.finish_start if phase < self.last else self.finish, phase)


def rows_after(sizes, total, phases):
    for size in sizes[:phases]:
        total //= size
    return total


def reduce_scratch(sizes, total, first, last, width):
    shapes = [pltpu.VMEM((rows_after(sizes, total, first + 1), width), BF16)]
    for phase in range(first, last + 1):
        shapes.append(pltpu.VMEM((sizes[phase] - 1, rows_after(sizes, total, phase + 1), width), BF16))
    most = max(sizes[first : last + 1]) - 1
    return shapes + [pltpu.SemaphoreType.DMA((last + 1 - first, most))] * 2 + [pltpu.SemaphoreType.DMA((1,))]


class Gather(Region):
    def __init__(self, axes, total, first, last, src, out, refs):
        super().__init__(axes, total)
        self.first, self.last, self.src, self.out, (self.ssem, self.rsem, self.lsem) = first, last, src, out, refs

    def region(self, phase):
        begin = self.at[phase + 1] - self.at[self.last]
        return self.out.at[pl.ds(pl.multiple_of(begin, 16), self.rows[phase + 1])]

    def own(self):
        return pltpu.make_async_copy(self.src, self.region(self.first), self.lsem.at[0])

    def copies(self, phase):
        src = self.src if phase == self.first else self.region(phase)
        for step, _, device in self.axes.peers(phase):
            at = self.first - phase, step - 1
            yield send(src, self.region(phase), self.ssem.at[at], self.rsem.at[at], device)

    def start(self, phase):
        if phase == self.first:
            self.own().start()
        for copy in self.copies(phase):
            copy.start()

    def finish(self, phase):
        if phase == self.first:
            self.own().wait()
        for copy in self.copies(phase):
            copy.wait()

    def finish_start(self, phase):
        self.finish(phase)
        self.start(phase - 1)

    def act(self, phase):
        return functools.partial(self.finish_start if phase > self.last else self.finish, phase)


class Spread(Gather):
    def __init__(self, axes, direct, total, src, out, refs):
        super().__init__(axes, total, 1, 0, src, out, refs)
        self.direct = direct

    def region(self, phase):
        which = 4 if phase == 1 else 1
        return self.out.at[pl.ds(pl.multiple_of(self.at[which], 16), self.rows[which])]

    def copies(self, phase):
        src = self.src if phase == 1 else self.region(0)
        for step, _, device in self.direct.peers(phase):
            at = 1 - phase, step - 1
            yield send(src, self.region(phase), self.ssem.at[at], self.rsem.at[at], device)


def gather_scratch(sizes, first, last):
    most = max(sizes[last : first + 1]) - 1
    return [pltpu.SemaphoreType.DMA((first + 1 - last, most))] * 2 + [pltpu.SemaphoreType.DMA((1,))]


class Keys:
    def __init__(self, place, whole, bufs, ssem, rsem, lsem):
        self.place, self.whole, self.bufs, self.ssem, self.rsem, self.lsem = place, whole, bufs, ssem, rsem, lsem
        self.copies = []

    def start(self, i, at, kv):
        n = self.place.n
        for part, (buf, whole) in enumerate(zip(self.bufs, self.whole)):
            width = buf.shape[1]
            buf[at, :] = kv[:, part * width : (part + 1) * width]
            self.copies.append(pltpu.make_async_copy(buf.at[at], whole.at[0, at], self.lsem.at[part, i]))
            for step in range(1, n):
                to = step - 1, part, i
                self.copies.append(
                    send(buf.at[at], whole.at[step, at], self.ssem.at[to], self.rsem.at[to], self.place.peer(n - step))
                )
            for copy in self.copies[-n:]:
                copy.start()

    def finish(self):
        for copy in self.copies:
            copy.wait()


def keys_scratch(n, rows, width, blocks):
    return [
        pltpu.VMEM((rows, width), BF16),
        pltpu.VMEM((rows, width), BF16),
        pltpu.SemaphoreType.DMA((n - 1, 2, blocks)),
        pltpu.SemaphoreType.DMA((n - 1, 2, blocks)),
        pltpu.SemaphoreType.DMA((2, blocks)),
    ]


def block_of(rows):
    return min(256, rows // 2)


def project_kernel(
    n, late, tok_in, cot, kind, leads, table, gain, h_out, n1_out, q_out, k_all, v_all, aux_out,
    tok, aux_in, ssem, rsem, kbuf, vbuf, ksem, krsem, lsem,
):
    (w,) = late
    place = Place(n)
    rows, width = kbuf.shape
    block = block_of(rows)
    blocks = rows // block
    bar = pltpu.get_barrier_semaphore()
    for step in range(1, n):
        signal(bar, place.peer(step))

    @pl.when(place.moves)
    def _():
        signal(bar, place.partner)

    for i in range(EXPERTS):
        aux_in[i : i + 1, :] = cot[i]
    kind_one = kind[...].astype(F32)
    lead_one = leads[...].astype(F32)
    first_lead = lead_one[:, 0:1]
    second_lead = jnp.where(kind_one == 1.0, lead_one[:, 1:2], first_lead)
    for row, value in ((KIND_ROW, kind_one), (LEAD_ROW, first_lead), (LEAD_ROW + 1, second_lead)):
        aux_in[row : row + 1, :] = jnp.broadcast_to(value, (1, rows))
    aux_in[LEAD_ROW + 2 :, :] = jnp.zeros((8 - LEAD_ROW - 2, rows), F32)

    @pl.when(place.moves)
    def _():
        pl.semaphore_wait(bar, n)

    @pl.when(jnp.logical_not(place.moves))
    def _():
        pl.semaphore_wait(bar, n - 1)

    swaps = [send(aux_in, aux_out, ssem.at[blocks], rsem.at[blocks], place.partner)]
    stays = []
    for i in range(blocks):
        at = pl.ds(i * block, block)
        swaps.append(send(tok_in.at[at], tok.at[at], ssem.at[i], rsem.at[i], place.partner))
        stays.append(pltpu.make_async_copy(tok_in.at[at], tok.at[at], rsem.at[i]))

    @pl.when(place.moves)
    def _():
        for copy in swaps:
            copy.start()
        swaps[0].wait_recv()

    @pl.when(jnp.logical_not(place.moves))
    def _():
        for copy in stays:
            copy.start()
        aux_out[...] = aux_in[...]

    lead_index = lax.broadcasted_iota(jnp.int32, (table.shape[0], 1), 0).astype(F32)
    lead_rows = []
    for half in range(2):
        lead = aux_out[LEAD_ROW + half : LEAD_ROW + half + 1, 0:1]
        lead_rows.append(column_sum(jnp.where(lead_index == lead, table[...], 0.0)))

    keys = Keys(place, (k_all, v_all), (kbuf, vbuf), ksem, krsem, lsem)
    for i in range(blocks):
        at = pl.ds(i * block, block)

        @pl.when(place.moves)
        def _():
            swaps[1 + i].wait_recv()

        @pl.when(jnp.logical_not(place.moves))
        def _():
            stays[i].wait()

        x = tok[at, :].astype(F32) + lead_rows[i * block // (rows // 2)]
        h_out[at, :] = x
        n1 = (normalize(x)[0] * gain[0:1, :]).astype(BF16)
        n1_out[at, :] = n1
        keys.start(i, at, dot(n1, w[:, width:]).astype(BF16))
        q_out[at, :] = (dot(n1, w[:, :width]) * HEAD_DIM**-0.5).astype(BF16)
    keys.finish()

    @pl.when(place.moves)
    def _():
        for copy in swaps:
            copy.wait_send()


def project(n, collective_id, tokens, cot, kind, leads, table, gain, w):
    rows, width = tokens.shape
    blocks = rows // block_of(rows)
    half = jax.ShapeDtypeStruct((rows, width), BF16)
    whole = jax.ShapeDtypeStruct((n, rows, width), BF16)
    return run(
        functools.partial(project_kernel, n),
        "project",
        collective_id,
        [(w, 0)],
        [tokens, cot, kind, leads, table, gain],
        [ANY] + [VMEM] * 5,
        [jax.ShapeDtypeStruct((rows, width), F32), half, half, whole, whole, jax.ShapeDtypeStruct((8, rows), F32)],
        [VMEM, VMEM, VMEM, ANY, ANY, VMEM],
        [pltpu.VMEM((rows, width), BF16), pltpu.VMEM((8, rows), F32)]
        + [pltpu.SemaphoreType.DMA((blocks + 1,))] * 2
        + keys_scratch(n, rows, width, blocks),
    )


def head_lanes(x, head):
    lane = lax.broadcasted_iota(jnp.int32, x.shape, 1)
    return jnp.where(lane // HEAD_DIM == head, x, jnp.zeros_like(x))


def attend_kernel(band, q_ref, k_ref, v_ref, aux_ref, e_ref, ob_ref, li_ref, vte):
    j = pl.program_id(1)
    keys, queries = e_ref.shape[1:]
    chunk = band // 2
    own_half = lax.rem(j, 2)
    coarse = aux_ref[KIND_ROW : KIND_ROW + 1, 0:1]
    coarse_flag = jnp.max(coarse) > 0.5
    seen_half = jnp.where(coarse_flag, own_half, 0)

    @pl.when(j == 0)
    def _():
        values = v_ref[...].astype(F32).T
        key_half = lax.rem(lax.broadcasted_iota(jnp.int32, (1, keys), 1) // chunk, 2)

        def prepare(half):
            seen = jnp.where(key_half == half, 1.0, 1.0 - coarse)
            for head in range(2):
                rows = values[head * HEAD_DIM : (head + 1) * HEAD_DIM, :] * seen
                vte[head, half, :HEAD_DIM, :] = rows.astype(BF16)

            @pl.when(pl.program_id(0) == 0)
            def _():
                for head in range(2):
                    vte[head, half, HEAD_DIM:, :] = jnp.broadcast_to(seen, (HEAD_DIM, keys)).astype(BF16)

        prepare(0)

        @pl.when(coarse_flag)
        def _():
            prepare(1)

    def finish(head, total, norm):
        inverse = 1.0 / norm
        ob_ref[head * HEAD_DIM : (head + 1) * HEAD_DIM, :] = (total * inverse).astype(BF16)
        li_ref[head : head + 1, :] = inverse

    li_ref[...] = jnp.zeros_like(li_ref)
    least, largest = None, None
    for head in range(2):
        e = jnp.exp(dot(k_ref[...], head_lanes(q_ref[...], head), (1, 1))).astype(BF16)
        e_ref[head, :, :] = e
        total = dot(vte[head, seen_half], e)
        norm = total[HEAD_DIM : HEAD_DIM + 1, :]
        finish(head, total[:HEAD_DIM, :], norm)
        least = norm if least is None else jnp.minimum(least, norm)
        largest = norm if largest is None else jnp.maximum(largest, norm)

    @pl.when(coarse_flag)
    def _():
        for c in range(keys // (2 * chunk)):
            at = pl.ds(pl.multiple_of((2 * c + 1 - own_half) * chunk, chunk), chunk)
            for head in range(2):
                e_ref[head, at, :] = jnp.zeros((chunk, queries), BF16)

    fits = jnp.logical_and(least > 1e-20, largest < 1e25)

    @pl.when(jnp.min(fits.astype(F32)) < 0.5)
    def _():
        for head in range(2):
            queries_one = head_lanes(q_ref[...], head)

            def scores(c):
                at = pl.ds(pl.multiple_of(c * chunk, chunk), chunk)
                hidden = jnp.logical_and(coarse > 0.5, lax.rem(c, 2) != own_half)
                return at, hidden, jnp.where(hidden, -1e30, dot(k_ref[at, :], queries_one, (1, 1)))

            def highest_step(c, top):
                return jnp.maximum(top, jnp.max(scores(c)[2], axis=0, keepdims=True))

            top = lax.fori_loop(0, keys // chunk, highest_step, jnp.full((1, queries), -1e30, F32))

            def total_step(c, total):
                at, hidden, s = scores(c)
                e = jnp.where(hidden, 0.0, jnp.exp(s - top)).astype(BF16)
                e_ref[head, at, :] = e
                return total + dot(vte[head, seen_half, :, at], e)

            total = lax.fori_loop(
                0, keys // chunk, total_step, jnp.zeros((LANES, queries), F32)
            )
            finish(head, total[:HEAD_DIM, :], total[HEAD_DIM : HEAD_DIM + 1, :])


def attend(q, k, v, aux):
    rows, width = q.shape
    keys, queries, pairs = k.shape[0], rows // 2, width // LANES
    return pl.pallas_call(
        functools.partial(attend_kernel, rows),
        grid=(pairs, 2),
        out_shape=[
            jax.ShapeDtypeStruct((2 * pairs, keys, rows), BF16),
            jax.ShapeDtypeStruct((width, rows), BF16),
            jax.ShapeDtypeStruct((8 * pairs, rows), F32),
        ],
        in_specs=[
            pl.BlockSpec((queries, LANES), lambda p, j: (j, p)),
            pl.BlockSpec((keys, LANES), lambda p, j: (0, p)),
            pl.BlockSpec((keys, LANES), lambda p, j: (0, p)),
            pl.BlockSpec(aux.shape, lambda p, j: (0, 0)),
        ],
        out_specs=[
            pl.BlockSpec((2, keys, queries), lambda p, j: (p, 0, j)),
            pl.BlockSpec((LANES, queries), lambda p, j: (p, j)),
            pl.BlockSpec((8, queries), lambda p, j: (p, j)),
        ],
        scratch_shapes=[pltpu.VMEM((2, 2, LANES, keys), BF16)],
        compiler_params=params(),
        name="attend",
    )(q, k, v, aux)


POINT_TIMES = (1.1, 2.2, 2.9, 3.5, 4.2, 4.9)
POINTS = len(POINT_TIMES)


def point(time):
    step = min(int(time / POINT_TIMES[-1]), 5)
    rest = time - step * POINT_TIMES[-1]
    return step * POINTS + next((i for i, end in enumerate(POINT_TIMES) if end >= rest - 0.05), POINTS - 1)


class Task:
    def __init__(self, reduces, total, phases, ends, array=None, begin=0.0):
        self.reduces, self.total, self.phases, self.array = reduces, total, phases, array
        self.ends, self.begin = [point(time) for time in ends], point(begin)


class Early:
    def __init__(self, n1, total, points):
        self.n1, self.total, self.points = n1, total, [point(time) for time in points]

    def shapes(self, n, rows, width, sizes):
        done = width - LANES
        outs = [((rows, done), BF16), ((rows, done), BF16), ((rows_after(sizes, self.total, 2), width), BF16)]
        pairs = done // LANES
        scratch = [
            pltpu.VMEM((rows, width), BF16),
            pltpu.VMEM((width, rows), BF16),
            pltpu.VMEM((pairs, rows, LANES), BF16),
            pltpu.VMEM((pairs, 2, n, rows, LANES), BF16),
            pltpu.VMEM((pairs, 2, n - 1, rows, LANES), BF16),
            pltpu.VMEM((self.total, width), BF16),
            pltpu.SemaphoreType.DMA((1,)),
            pltpu.SemaphoreType.DMA((pairs, 2, n - 1)),
            pltpu.SemaphoreType.DMA((pairs, 2, n - 1)),
        ]
        return outs, scratch + reduce_scratch(sizes, self.total, 0, 1, width)

    def bind(self, axes, place, n1_ref, outs, refs):
        self.place = place
        self.done, result = outs[:2], outs[2]
        self.n1_buf, self.n1_turned, self.dq, self.parts, self.recv, self.g, n1_sem, self.ssem, self.rsem = refs[:9]
        self.reduce = Reduce(axes, self.total, 0, 1, self.g, result, refs[9:])
        self.fetch = pltpu.make_async_copy(n1_ref, self.n1_buf, n1_sem.at[0])

    def copies(self, pair):
        for step in range(1, self.place.n):
            for part in range(2):
                at = pair, part, step - 1
                yield send(
                    self.parts.at[pair, part, step], self.recv.at[at], self.ssem.at[at], self.rsem.at[at], self.place.peer(step)
                )

    def start(self, pair, dk, dv):
        for part, total in enumerate((dk, dv)):
            self.parts[pair, part] = total.reshape(self.parts.shape[2:]).astype(BF16)
        for copy in self.copies(pair):
            copy.start()

    def finish(self, pair):
        if pair == 0:
            self.fetch.wait()
            self.n1_turned[...] = turned(self.n1_buf[...])
        for copy in self.copies(pair):
            copy.wait()
        own = [self.dq[pair]]
        for part in range(2):
            total = self.parts[pair, part, 0].astype(F32)
            for step in range(self.place.n - 1):
                total = total + self.recv[pair, part, step].astype(F32)
            own.append(total.astype(BF16))
            self.done[part][:, pair * LANES : (pair + 1) * LANES] = own[-1]
        width = self.n1_buf.shape[1]
        put = dot(self.n1_turned[...], jnp.concatenate(own, axis=1)).astype(BF16)
        self.g[pair * width : (pair + 1) * width, :] = put
        if pair == self.dq.shape[0] - 1:
            end = (pair + 1) * width
            if self.total > end:
                self.g[end:, :] = jnp.zeros((self.total - end, width), BF16)
            self.reduce.own().start()
            self.reduce.start(0)

    def schedule(self):
        pairs = self.dq.shape[0]
        acts = [functools.partial(self.finish, pair) for pair in range(pairs)] + [self.reduce.act(0), self.reduce.act(1)]
        return zip(self.points, acts)


def attend_back_kernel(n, chips, tasks, early, *refs):
    q_ref, k_ref, v_ref, e_ref, do_ref, dl_ref = refs[:6]
    refs = refs[6:]
    if early:
        n1_ref, refs = refs[0], refs[1:]
    given = sum(task.array is not None for task in tasks)
    sources, refs = list(refs[:given]), refs[given:]
    dq_ref, dk_ref, dv_ref = refs[:3]
    refs = refs[3:]
    if early:
        early_outs, refs = refs[:3], refs[3:]
    results, refs = refs[: len(tasks)], refs[len(tasks) :]
    kt, vext, dk_sum, dv_sum, rhs = refs[:5]
    refs = refs[5:]
    t = pl.program_id(0) * pl.num_programs(1) + pl.program_id(1)
    keys, queries = e_ref.shape[1:]

    axes = Axes(n, chips)
    bar = pltpu.get_barrier_semaphore()
    met = sum(size - 1 for size in axes.sizes) + (n - 1 if early else 0)
    schedule = {0: [lambda: pl.semaphore_wait(bar, met)]}
    reduces = []
    begin = 0
    if early:
        place = Place(n)
        early.bind(axes, place, n1_ref, early_outs, refs[:15])
        refs = refs[15:]
        for end, act in early.schedule():
            schedule.setdefault(end, []).append(act)
    for index, (task, result) in enumerate(zip(tasks, results)):
        if task.array is None:
            source, begin = results[index - 1], tasks[index - 1].ends[-1]
        else:
            source, begin = sources.pop(0), task.begin
        first, last = task.phases[0], task.phases[-1]
        count = (4 + len(task.phases)) if task.reduces else 3
        scratch, refs = refs[:count], refs[count:]
        if task.reduces:
            move = Reduce(axes, task.total, first, last, source, result, scratch)
            reduces.append(move)
        else:
            move = Gather(axes, task.total, first, last, source, result, scratch)
        schedule.setdefault(begin, []).append(functools.partial(move.start, first))
        for phase, end in zip(task.phases, task.ends):
            schedule.setdefault(end, []).append(move.act(phase))

    def points(part):
        for place_of in sorted(schedule):
            if place_of % POINTS == part:

                @pl.when(t == place_of // POINTS)
                def _():
                    for act in schedule[place_of]:
                        act()

    @pl.when(t == 0)
    def _():
        axes.greet(bar)
        if early:
            for step in range(1, n):
                signal(bar, place.peer(step))
            early.fetch.start()
        for reduce in reduces:
            reduce.own().start()

    @pl.when(pl.program_id(1) == 0)
    def _():
        kt[...] = k_ref[...].astype(F32).T.astype(BF16)
        vext[:, :LANES] = v_ref[...]
        vext[:, LANES:] = jnp.ones((keys, LANES), BF16)
        dk_sum[...] = jnp.zeros_like(dk_sum)
        dv_sum[...] = jnp.zeros_like(dv_sum)

    do = do_ref[...].astype(F32)
    row_head = lax.broadcasted_iota(jnp.int32, (LANES, 1), 0) // HEAD_DIM
    for head in range(2):
        rhs[head, :LANES, :] = jnp.where(row_head == head, do, 0.0).astype(BF16)
        rhs[head, LANES : LANES + 16, :] = dl_ref[16 * head : 16 * head + 16, :]
        rhs[head, LANES + 16 :, :] = jnp.zeros((LANES - 16, queries), BF16)
    do_rows = jnp.concatenate([rhs[head, :LANES, :].astype(F32).T.astype(BF16) for head in range(2)], axis=0)
    q_rows = jnp.concatenate([head_lanes(q_ref[...], head) for head in range(2)], axis=0)
    ds, dq = [], []
    for head in range(2):
        ds.append((e_ref[head].astype(F32) * dot(vext[...], rhs[head])).astype(BF16))
        dq.append(dot(kt[...], ds[head])[head * HEAD_DIM : (head + 1) * HEAD_DIM])
        points(head)
    halves = [pl.ds(0, keys // 2), pl.ds(keys // 2, keys // 2)]
    for part, at in enumerate(halves):
        dv_sum[at, :] += dot(jnp.concatenate([e_ref[0, at, :], e_ref[1, at, :]], axis=1), do_rows)
        points(2 + part)
    ds = jnp.concatenate(ds, axis=1)
    for part, at in enumerate(halves):
        dk_sum[at, :] += dot(ds[part * (keys // 2) : (part + 1) * (keys // 2)], q_rows)
        if part == 0:
            points(4)
    dq_rows = (jnp.concatenate(dq, axis=0) * HEAD_DIM**-0.5).T.astype(BF16)
    dq_ref[...] = dq_rows
    whole_pair = pl.program_id(1) == pl.num_programs(1) - 1
    if early:
        pair = pl.program_id(0)

        @pl.when(pair < pl.num_programs(0) - 1)
        def _():
            early.dq[pair, pl.ds(pl.multiple_of(pl.program_id(1) * queries, 16), queries), :] = dq_rows

        @pl.when(jnp.logical_and(pair < pl.num_programs(0) - 1, whole_pair))
        def _():
            early.start(pair, dk_sum[...], dv_sum[...])

        whole_pair = jnp.logical_and(pair == pl.num_programs(0) - 1, whole_pair)

    @pl.when(whole_pair)
    def _():
        dk_ref[...] = dk_sum[...].astype(BF16)
        dv_ref[...] = dv_sum[...].astype(BF16)

    points(5)


def attend_back(n, chips, collective_id, q, k, v, e, do, dl, tasks, early=None):
    sizes = sum_sizes(n, chips)
    rows, width = q.shape
    keys, queries, pairs = k.shape[0], rows // 2, width // LANES
    scratch, results = [], []
    for task in tasks:
        first, last = task.phases[0], task.phases[-1]
        if task.reduces:
            scratch += reduce_scratch(sizes, task.total, first, last, width)
            height = rows_after(sizes, task.total, last + 1)
        else:
            scratch += gather_scratch(sizes, first, last)
            height = rows_after(sizes, task.total, last)
        results.append(jax.ShapeDtypeStruct((height, width), BF16))
    key_width, key_spec = width, pl.BlockSpec((keys, LANES), lambda p, j: (0, p))
    early_outs = []
    if early:
        key_width, key_spec = LANES, pl.BlockSpec((keys, LANES), lambda p, j: (0, 0))
        outs, early_scratch = early.shapes(n, rows, width, sizes)
        early_outs = [jax.ShapeDtypeStruct(*out) for out in outs]
        scratch = early_scratch + scratch
    return pl.pallas_call(
        functools.partial(attend_back_kernel, n, chips, tasks, early),
        grid=(pairs, 2),
        out_shape=[
            jax.ShapeDtypeStruct((rows, width), BF16),
            jax.ShapeDtypeStruct((keys, key_width), BF16),
            jax.ShapeDtypeStruct((keys, key_width), BF16),
        ]
        + early_outs
        + results,
        in_specs=[
            pl.BlockSpec((queries, LANES), lambda p, j: (j, p)),
            pl.BlockSpec((keys, LANES), lambda p, j: (0, p)),
            pl.BlockSpec((keys, LANES), lambda p, j: (0, p)),
            pl.BlockSpec((2, keys, queries), lambda p, j: (p, 0, j)),
            pl.BlockSpec((LANES, queries), lambda p, j: (p, j)),
            pl.BlockSpec((32, queries), lambda p, j: (p, j)),
        ]
        + [ANY] * (1 if early else 0)
        + [ANY if task.reduces and task.phases[0] == 0 else VMEM for task in tasks if task.array is not None],
        out_specs=[
            pl.BlockSpec((queries, LANES), lambda p, j: (j, p)),
            key_spec,
            key_spec,
        ]
        + [VMEM] * len(early_outs)
        + [VMEM if task.reduces else ANY for task in tasks],
        scratch_shapes=[
            pltpu.VMEM((LANES, keys), BF16),
            pltpu.VMEM((keys, 2 * LANES), BF16),
            pltpu.VMEM((keys, LANES), F32),
            pltpu.VMEM((keys, LANES), F32),
            pltpu.VMEM((2, 2 * LANES, queries), BF16),
        ]
        + scratch,
        compiler_params=params(collective_id),
        name="attend_back",
    )(q, k, v, e, do, dl, *([early.n1] if early else []), *[task.array for task in tasks if task.array is not None])


def mlp_block(at, h, ob, w_out, gain2, w1, b1, w2, h2_ref, n2_ref, a_ref, gp_ref):
    h2 = h + dot(ob, w_out[...], (0, 0))
    h2_ref[at, :] = h2
    n2 = (normalize(h2)[0] * gain2[...]).astype(BF16)
    n2_ref[at, :] = n2
    u = dot(n2, w1[...]) + b1[...]
    square = u * u
    t = jnp.tanh(gelu_in * u * (1.0 + gelu_cubic * square))
    half = 0.5 + 0.5 * t
    a = (u * half).astype(BF16)
    a_ref[at, :] = a
    slope = half + (0.5 * gelu_in) * u * (1.0 - t * t) * (1.0 + 3.0 * gelu_cubic * square)
    gp_ref[at, :] = slope.astype(BF16)
    return h2 + dot(a, w2[...])


def middle_kernel(
    n, late, gain2, b1, gain1, h2_out, n2_out, a_out, gp_out, h3_out, n1_out, q_out, k_all, v_all,
    h2_ref, n2_ref, a_ref, gp_ref, h3_ref, n1_ref, q_ref, ship_sems, kbuf, vbuf, ksem, krsem, lsem,
):
    h, ob, w_out, w1, w2, w = late
    place = Place(n)
    rows, width = h.shape
    block = rows // 2
    bar = pltpu.get_barrier_semaphore()
    for step in range(1, n):
        signal(bar, place.peer(step))
    keys = Keys(place, (k_all, v_all), (kbuf, vbuf), ksem, krsem, lsem)
    ship = Ship(ship_sems)
    gain2, b1 = gain2.at[pl.ds(0, 1)], b1.at[pl.ds(0, 1)]
    pairs = ((h2_ref, h2_out), (n2_ref, n2_out), (a_ref, a_out), (gp_ref, gp_out), (h3_ref, h3_out), (n1_ref, n1_out), (q_ref, q_out))
    for i in range(rows // block):
        at = pl.ds(i * block, block)
        h3 = mlp_block(at, h[at, :], ob[:, at], w_out, gain2, w1, b1, w2, h2_ref, n2_ref, a_ref, gp_ref)
        h3_ref[at, :] = h3
        n1 = (normalize(h3)[0] * gain1[1:2, :]).astype(BF16)
        n1_ref[at, :] = n1
        kv = dot(n1, w[:, width:]).astype(BF16)
        if i == 0:
            pl.semaphore_wait(bar, n - 1)
        keys.start(i, at, kv)
        q_ref[at, :] = (dot(n1, w[:, :width]) * HEAD_DIM**-0.5).astype(BF16)
        for src, dst in pairs:
            ship(src.at[at], dst.at[at])
    keys.finish()
    ship.finish()


def middle(n, collective_id, h, ob, w_out, gain2, w1, b1, w2, gain1, w):
    rows, width = h.shape
    hidden = w1.shape[2]
    blocks = 2
    shapes = [
        ((rows, width), F32), ((rows, width), BF16), ((rows, hidden), BF16), ((rows, hidden), BF16), ((rows, width), F32),
        ((rows, width), BF16), ((rows, width), BF16),
    ]
    return run(
        functools.partial(middle_kernel, n),
        "middle",
        collective_id,
        [h, ob, (w_out, 0), (w1, 0), (w2, 0), (w, 1)],
        [gain2, b1, gain1],
        [VMEM] * 3,
        [jax.ShapeDtypeStruct(*shape) for shape in shapes] + [jax.ShapeDtypeStruct((n, rows, width), BF16)] * 2,
        [ANY] * 9,
        [pltpu.VMEM(*shape) for shape in shapes]
        + [pltpu.SemaphoreType.DMA((blocks * len(shapes),))]
        + keys_scratch(n, rows, width, blocks),
    )


def mlp_back_block(at, dh, gp, h2, ob, li, w_out, gain2, w1, w2, dz_ref, du_ref, dy_ref, dh2_ref, do_ref, dl_ref):
    dz = dh.astype(BF16)
    dz_ref[at, :] = dz
    du = (dot(dz, w2[...], (1, 1)) * gp.astype(F32)).astype(BF16)
    du_ref[at, :] = du
    bias_sum = column_sum(du.astype(F32))
    dn2 = dot(du, w1[...], (1, 1))
    xhat, rstd = normalize(h2)
    gain_sum = column_sum(dn2 * xhat)
    dh2 = dh + normalize_back(dn2 * gain2[...], xhat, rstd)
    dh2_ref[at, :] = dh2
    dy = dh2.astype(BF16)
    dy_ref[at, :] = dy
    do = dot(w_out[...], dy, (1, 1))
    product = do * ob.astype(F32)
    for head in range(do.shape[0] // HEAD_DIM):
        rows = slice(head * HEAD_DIM, (head + 1) * HEAD_DIM)
        inverse = li[8 * (head // 2) + head % 2 : 8 * (head // 2) + head % 2 + 1, :]
        do_ref[rows, at] = (do[rows] * inverse).astype(BF16)
        rest = -column_sum(product[rows]) * inverse
        terms = []
        for _ in range(3):
            terms.append(rest.astype(BF16).astype(F32))
            rest = rest - terms[-1]
        row = lax.broadcasted_iota(jnp.int32, (16, 1), 0)
        block = jnp.where(row == 0, terms[0], jnp.where(row == 1, terms[1], jnp.where(row == 2, terms[2], 0.0)))
        dl_ref[16 * head : 16 * head + 16, at] = block.astype(BF16)
    return bias_sum, gain_sum


def fc1_sums(g_ref, n2, du):
    width = n2.shape[1]
    n2_turned = turned(n2[...])
    for part in range(du.shape[1] // width):
        at = slice(part * width, (part + 1) * width)
        g_ref[at, :] = dot(n2_turned, du[:, at]).astype(BF16)
    return du.shape[1]


def fill(g_ref, at):
    if g_ref.shape[0] > at:
        g_ref[at:, :] = jnp.zeros((g_ref.shape[0] - at, g_ref.shape[1]), BF16)


def put_rows(small_ref, row, value, width):
    for part in range(value.shape[1] // width):
        small_ref[row + part : row + part + 1, :] = value[:, part * width : (part + 1) * width]


def back_shapes(rows, width):
    return [
        jax.ShapeDtypeStruct((rows, width), F32),
        jax.ShapeDtypeStruct((width, rows), BF16),
        jax.ShapeDtypeStruct((16 * width // HEAD_DIM, rows), BF16),
    ]


def turn_kernel(
    late, li_ref, aux_ref, gain2, b1, fgain, head_w, head_b, prior_ref,
    g2_out, g1_out, small_ref, dh2_out, do_out, dl_out, expert_ref, head_ref, out_ref,
    g2_ref, g1_ref, dh2_ref, do_ref, dl_ref, dz, du, dy, h2_ref, n2_ref, a_ref, gp_ref, wide, tall, ship_sems,
):
    h_ref, ob_ref, w_out, w1, w2 = late
    rows, width = h_ref.shape
    gain2, b1 = gain2.at[pl.ds(1, 1)], b1.at[pl.ds(1, 1)]
    block = rows // 2
    ship = Ship(ship_sems)
    wide[...] = jnp.zeros_like(wide)
    wide[0:EXPERTS, :] = head_w[...]
    hw = wide[...]
    fgain_row = fgain[...].reshape(1, width)
    tall[...] = jnp.ones_like(tall)
    tall[0:EXPERTS, 0:LEADS] = prior_ref[...]
    logp = jnp.log(tall[...])
    tall[...] = jnp.zeros_like(tall)
    tall[0:1, 0:EXPERTS] = head_b[...]
    hb = jnp.sum(jnp.where(diagonal((8, LANES)), tall[0:1, :], 0.0), axis=1, keepdims=True)
    lane = lax.broadcasted_iota(jnp.int32, (8, LANES), 1).astype(F32)
    expert = lax.broadcasted_iota(jnp.int32, (8, 1), 0)
    bias_sum, gain_sum, final_sum, head_sum, hbias_sum, lead_sum = 0.0, 0.0, 0.0, 0.0, 0.0, 0.0
    for i in range(2):
        at = pl.ds(i * block, block)
        h3 = mlp_block(at, h_ref[at, :], ob_ref[:, at], w_out, gain2, w1, b1, w2, h2_ref, n2_ref, a_ref, gp_ref)
        xhat, rstd = normalize(h3)
        nf = xhat * fgain_row
        own_lead = lane == aux_ref[LEAD_ROW + i : LEAD_ROW + i + 1, 0:1]
        prior = jnp.sum(jnp.where(own_lead, logp, 0.0), axis=1, keepdims=True)
        logits = dot_split(hw, nf, (1, 1)) + hb - prior
        logits = jnp.where(expert < EXPERTS, logits, -1e30)
        power = jnp.exp(logits - jnp.max(logits, axis=0, keepdims=True))
        weights = power / jnp.sum(power, axis=0, keepdims=True)
        expert_ref[:, at] = weights
        counted = jnp.where(expert == EXPERTS, 1.0, weights)
        lead_sum = lead_sum + jnp.where(own_lead, jnp.sum(counted, axis=1, keepdims=True), 0.0)
        cot = jnp.where(expert < EXPERTS, aux_ref[:, at], 0.0)
        dlogits = weights * (cot - jnp.sum(weights * cot, axis=0, keepdims=True))
        head_sum = head_sum + dot_split(dlogits, nf)
        hbias_sum = hbias_sum + jnp.sum(dlogits, axis=1, keepdims=True)
        dnf = dot_split(dlogits, hw, (0, 0))
        final_sum = final_sum + column_sum(dnf * xhat)
        dh = normalize_back(dnf * fgain_row, xhat, rstd)
        sums = mlp_back_block(
            at, dh, gp_ref[at, :], h2_ref[at, :], ob_ref[:, at], li_ref[:, at], w_out, gain2, w1, w2,
            dz, du, dy, dh2_ref, do_ref, dl_ref,
        )
        bias_sum, gain_sum = bias_sum + sums[0], gain_sum + sums[1]
        ship(dh2_ref.at[at], dh2_out.at[at])
        ship(do_ref.at[:, at], do_out.at[:, at])
        ship(dl_ref.at[:, at], dl_out.at[:, at])
    small_ref[...] = jnp.zeros_like(small_ref)
    put_rows(small_ref, 0, gain_sum, width)
    put_rows(small_ref, 1, final_sum, width)
    put_rows(small_ref, 4, bias_sum, width)
    head_ref[0:8, :] = head_sum
    head_ref[8:16, :] = jnp.zeros((8, width), F32)
    head_ref[8:16, 0:LANES] = lead_sum
    head_ref[16:24, :] = jnp.broadcast_to(hbias_sum, (8, width))
    g2_ref[: a_ref.shape[1], :] = dot(a_ref[...], dz[...], (0, 0)).astype(BF16)
    fill(g2_ref, a_ref.shape[1])
    ship(g2_ref, g2_out)
    fill(g1_ref, fc1_sums(g1_ref, n2_ref, du))
    ship(g1_ref, g1_out)
    out_ref[...] = dot(ob_ref[...], dy[...]).astype(BF16)
    ship.finish()


def turn(h, ob, li, aux, w_out, gain2, w1, b1, w2, fgain, head_w, head_b, prior, grad_rows):
    rows, width = h.shape
    hidden = w1.shape[2]
    grads = [jax.ShapeDtypeStruct((grad_rows, width), BF16)] * 2
    shapes = back_shapes(rows, width)
    return run(
        turn_kernel,
        "turn",
        None,
        [h, ob, (w_out, 1), (w1, 1), (w2, 1)],
        [li, aux, gain2, b1, fgain, head_w, head_b, prior],
        [VMEM] * 8,
        grads
        + [jax.ShapeDtypeStruct((8, width), F32)]
        + shapes
        + [
            jax.ShapeDtypeStruct((8, rows), F32),
            jax.ShapeDtypeStruct((24, width), F32),
            jax.ShapeDtypeStruct((width, width), BF16),
        ],
        [ANY, ANY, VMEM, ANY, ANY, ANY, VMEM, VMEM, VMEM],
        [pltpu.VMEM(shape.shape, shape.dtype) for shape in grads + shapes]
        + [
            pltpu.VMEM((rows, width), BF16),
            pltpu.VMEM((rows, hidden), BF16),
            pltpu.VMEM((rows, width), BF16),
            pltpu.VMEM((rows, width), F32),
            pltpu.VMEM((rows, width), BF16),
            pltpu.VMEM((rows, hidden), BF16),
            pltpu.VMEM((rows, hidden), BF16),
            pltpu.VMEM((8, width), F32),
            pltpu.VMEM((8, LANES), F32),
            pltpu.SemaphoreType.DMA((8,)),
        ],
    )


class KeyGrads:
    def __init__(self, place, parts, own, recv, dkv, ssem, rsem):
        self.place, self.parts, self.own, self.recv, self.dkv, self.ssem, self.rsem = place, parts, own, recv, dkv, ssem, rsem

    def copies(self):
        for step in range(1, self.place.n):
            for part, src in enumerate(self.parts):
                at = step - 1, part
                yield send(src.at[step], self.recv.at[at], self.ssem.at[at], self.rsem.at[at], self.place.peer(step))

    def start(self):
        for copy in self.copies():
            copy.start()

    def finish(self):
        for copy in self.copies():
            copy.wait()
        width = self.dkv.shape[1] // 2
        for part, own in enumerate(self.own):
            total = own[...].astype(F32)
            for step in range(self.place.n - 1):
                total = total + self.recv[step, part].astype(F32)
            self.dkv[:, part * width : (part + 1) * width] = total.astype(BF16)


def key_scratch(n, rows, width):
    return [
        pltpu.VMEM((n - 1, 2, rows, width), BF16),
        pltpu.VMEM((rows, 2 * width), BF16),
        pltpu.SemaphoreType.DMA((n - 1, 2)),
        pltpu.SemaphoreType.DMA((n - 1, 2)),
    ]


def project_back_block(at, dn1_q, dkv, w, gain_row, h, dh2):
    width = h.shape[1]
    dn1 = dn1_q + dot(dkv[at, :], w[:, width:], (1, 1))
    xhat, rstd = normalize(h[at, :])
    return dh2[at, :] + normalize_back(dn1 * gain_row, xhat, rstd), column_sum(dn1 * xhat)


def key_weight_sums(g_ref, n1_turned, dkv):
    width = n1_turned.shape[0]
    for part in range(2):
        at = slice(part * width, (part + 1) * width)
        g_ref[(part + 1) * width : (part + 2) * width, :] = dot(n1_turned, dkv[:, at]).astype(BF16)


def between_kernel(
    n, chips, late, dk, dv, gain1, li_ref, gain2,
    norm_ref, small_ref, g1_out, dh2_out, do_out, dl_out, fc2_out, fc1_out, qkv_next, fc2_next_ref,
    gq_ref, g2_ref, g1_ref, dh2_ref, do_ref, dl_ref, dz, du, dy, ship_sems, krecv, dkv, ksem, krsem, *refs,
):
    n1, dq, fc2_src, fc1_src, dk_own, dv_own, w, h3, dh2_in, out_b, a, w2, gp, w1, h2_ref, w_out, ob_ref, n2_ref = late
    place, axes = Place(n), Axes(n, chips)
    rows, width = dq.shape
    hidden = a.shape[1]
    block = rows // 2
    bar = pltpu.get_barrier_semaphore()
    met = axes.greet(bar)
    for step in range(1, n):
        signal(bar, place.peer(step))
    ship = Ship(ship_sems)
    refs = list(refs)
    take = lambda count: [refs.pop(0) for _ in range(count)]
    fc2 = Gather(axes, fc2_out.shape[0], 2, 0, fc2_src.buf, fc2_out, take(3))
    fc1 = Gather(axes, fc1_out.shape[0], 3, 0, fc1_src.buf, fc1_out, take(3))
    qkv = Reduce(axes, gq_ref.shape[0], 0, 2, gq_ref, qkv_next, take(7))
    fc2_next = Reduce(axes, g2_ref.shape[0], 0, 1, g2_ref, fc2_next_ref, take(6))
    keys = KeyGrads(place, (dk, dv), (dk_own, dv_own), krecv, dkv, ksem, krsem)

    n1_turned = turned(n1[...])
    gq_ref[:width, :] = dot(n1_turned, dq[...]).astype(BF16)
    fc2_src.ready()
    fc1_src.ready()
    pl.semaphore_wait(bar, met + n - 1)
    keys.start()
    fc2.start(2)
    fc1.start(3)
    dn1_q = [dot(dq[pl.ds(i * block, block), :], w[:, :width], (1, 1)) for i in range(2)]
    keys.finish()
    gain_sum = 0.0
    dh = []
    for i in range(2):
        at = pl.ds(i * block, block)
        dh_one, part = project_back_block(at, dn1_q[i], dkv, w, gain1[1:2, :], h3, dh2_in)
        dh.append(dh_one)
        dz[at, :] = dh_one.astype(BF16)
        gain_sum = gain_sum + part
    norm_ref[...] = jnp.broadcast_to(gain_sum, norm_ref.shape)
    fc2.finish_start(2)
    key_weight_sums(gq_ref, n1_turned, dkv)
    gq_ref[3 * width : 4 * width, :] = out_b[...]
    fill(gq_ref, 4 * width)
    qkv.own().start()
    qkv.start(0)
    g2_ref[:hidden, :] = dot(a[...], dz[...], (0, 0)).astype(BF16)
    fill(g2_ref, hidden)
    fc2_next.own().start()
    fc2_next.start(0)
    fc1.finish_start(3)
    bias_sum, gain_sum = 0.0, 0.0
    parts = min(4, rows // LANES)
    quarter = rows // parts
    acts = [
        [qkv.act(0), fc2_next.act(0)],
        [fc1.act(2)],
        [fc2.act(1), qkv.act(1)],
        [],
    ]
    dh = jnp.concatenate(dh, axis=0)
    for i in range(parts):
        at = pl.ds(i * quarter, quarter)
        dh_one = dh[i * quarter : (i + 1) * quarter]
        sums = mlp_back_block(
            at, dh_one, gp[at, :], h2_ref[at, :], ob_ref[:, at], li_ref[:, at], w_out, gain2.at[pl.ds(0, 1)], w1, w2,
            dz, du, dy, dh2_ref, do_ref, dl_ref,
        )
        bias_sum, gain_sum = bias_sum + sums[0], gain_sum + sums[1]
        for group in acts[i * 4 // parts : (i + 1) * 4 // parts]:
            for act in group:
                act()
        ship(dh2_ref.at[at], dh2_out.at[at])
        ship(do_ref.at[:, at], do_out.at[:, at])
        ship(dl_ref.at[:, at], dl_out.at[:, at])
    small_ref[...] = jnp.zeros_like(small_ref)
    put_rows(small_ref, 0, gain_sum, width)
    put_rows(small_ref, 4, bias_sum, width)
    at = fc1_sums(g1_ref, n2_ref, du)
    g1_ref[at : at + width, :] = dot(ob_ref[...], dy[...]).astype(BF16)
    fill(g1_ref, at + width)
    ship(g1_ref, g1_out)
    fc1.finish_start(1)
    fc2.finish(0)
    fc2_next.finish(1)
    qkv.finish(2)
    fc1.finish(0)
    ship.finish()


def between(
    n, chips, collective_id, totals, dq, dk, dv, n1, h3, dh2, w, gain1, gp, h2, ob, li, n2, a, w_out, gain2, w1, w2, out_b, fc2, fc1
):
    rows, width = dq.shape
    hidden = a.shape[1]
    sizes = sum_sizes(n, chips)
    half = lambda height: jax.ShapeDtypeStruct((height, width), BF16)
    kept = [half(totals[4])] + back_shapes(rows, width)
    return run(
        functools.partial(between_kernel, n, chips),
        "between",
        collective_id,
        [n1, dq, fc2, fc1, (dk, 0), (dv, 0), (w, 1), h3, dh2, out_b, a, (w2, 0), gp, (w1, 0), h2, (w_out, 0), ob, n2],
        [dk, dv, gain1, li, gain2],
        [ANY, ANY, VMEM, VMEM, VMEM],
        [jax.ShapeDtypeStruct((8, width), F32)] * 2
        + kept
        + [
            half(totals[0]),
            half(totals[1]),
            half(rows_after(sizes, totals[2], 3)),
            half(rows_after(sizes, totals[3], 2)),
        ],
        [VMEM, VMEM] + [ANY] * 6 + [VMEM, VMEM],
        [pltpu.VMEM((totals[2], width), BF16), pltpu.VMEM((totals[3], width), BF16)]
        + [pltpu.VMEM(shape.shape, shape.dtype) for shape in kept]
        + [
            pltpu.VMEM((rows, width), BF16),
            pltpu.VMEM((rows, hidden), BF16),
            pltpu.VMEM((rows, width), BF16),
            pltpu.SemaphoreType.DMA((13,)),
        ]
        + key_scratch(n, rows, width)
        + gather_scratch(sizes, 2, 0)
        + gather_scratch(sizes, 3, 0)
        + reduce_scratch(sizes, totals[2], 0, 2, width)
        + reduce_scratch(sizes, totals[3], 0, 1, width),
    )


def last_axes(n, chips):
    return DirectAxes if n * chips <= 16 else Axes


def last_kernel(
    n, chips, late, dk, dv, gain, aux, expert, norm_b, small_a, small_b, head,
    tg_out, ex_out, fc2_out, fc1_out, early_ref, sum_ref,
    tg, g_ref, own_shard, early_shard, krecv, dkv, ksem, krsem, ssem, rsem, *refs,
):
    n1, dq, fc2_src, fc1_src, early, dk_own, dv_own, w, dk_done, dv_done, h, dh2 = late
    place, axes = Place(n), Axes(n, chips)
    direct = last_axes(n, chips)(n, chips)
    rows, width = dq.shape
    block = rows // 2
    bar = pltpu.get_barrier_semaphore()
    met = axes.greet(bar) + direct.greet(bar) + n - 1
    for step in range(1, n):
        signal(bar, place.peer(step))

    @pl.when(place.moves)
    def _():
        signal(bar, place.partner)

    refs = list(refs)
    take = lambda count: [refs.pop(0) for _ in range(count)]
    top = len(direct.sizes) - 1
    fc2 = Gather(axes, fc2_out.shape[0], 1, 0, fc2_src.buf, fc2_out, take(3))
    fc1 = Gather(axes, fc1_out.shape[0], 3, 0, fc1_src.buf, fc1_out, take(3))
    early_reduce = Reduce(axes, early_ref.shape[0], 2, 3, early.buf, early_shard, take(6))
    if last_axes(n, chips) is DirectAxes:
        early_gather = Spread(axes, direct, early_ref.shape[0], early_shard, early_ref, take(3))
    else:
        early_gather = Gather(axes, early_ref.shape[0], 3, 0, early_shard, early_ref, take(3))
    reduce = Reduce(direct, g_ref.shape[0], 0, top, g_ref, own_shard, take(5 + top))
    gather = Gather(direct, g_ref.shape[0], top, 0, own_shard, sum_ref, take(3))
    keys = KeyGrads(place, (dk, dv), (dk_own, dv_own), krecv, dkv, ksem, krsem)
    n1_turned = turned(n1[...])
    for array in (fc2_src, fc1_src, early):
        array.ready()

    @pl.when(place.moves)
    def _():
        pl.semaphore_wait(bar, met + 1)

    @pl.when(jnp.logical_not(place.moves))
    def _():
        pl.semaphore_wait(bar, met)

    swaps = [send(expert, ex_out, ssem.at[2], rsem.at[2], place.partner)]
    for i in range(2):
        at = pl.ds(i * block, block)
        swaps.append(send(tg.at[at], tg_out.at[at], ssem.at[i], rsem.at[i], place.partner))

    def swap(index):
        @pl.when(place.moves)
        def _():
            swaps[index].start()

    keys.start()
    swap(0)
    early_reduce.own().start()
    early_reduce.start(2)
    fc1.start(3)
    fc2.start(1)
    done = dk_done.shape[1]
    dn1 = []
    for i in range(2):
        at = pl.ds(i * block, block)
        part = dot(dq[at, :], w[:, :width], (1, 1)) + dot(dk_done[at, :], w[:, width : width + done], (1, 1))
        dn1.append(part + dot(dv_done[at, :], w[:, 2 * width : 2 * width + done], (1, 1)))
    keys.finish()
    early_reduce.finish_start(2)
    fc1.finish_start(3)
    gain_sum = 0.0
    half_sums = []
    for i in range(2):
        at = pl.ds(i * block, block)
        part = dot(dkv[at, :LANES], w[:, width + done : 2 * width], (1, 1))
        part = dn1[i] + part + dot(dkv[at, LANES:], w[:, 2 * width + done :], (1, 1))
        xhat, rstd = normalize(h[at, :])
        gain_sum = gain_sum + column_sum(part * xhat)
        dh = dh2[at, :] + normalize_back(part * gain[0:1, :], xhat, rstd)
        half_sums.append(column_sum(dh))
        tg[at, :] = dh.astype(BF16)
        swap(1 + i)
    lead_index = lax.broadcasted_iota(jnp.int32, (LEADS, 1), 0).astype(F32)
    table = 0.0
    for half in range(2):
        lead = aux[LEAD_ROW + half : LEAD_ROW + half + 1, 0:1]
        table = table + jnp.where(lead_index == lead, half_sums[half], 0.0)
    early_reduce.finish(3)
    early_gather.start(early_gather.first)
    g_ref[:width, :] = dot(n1_turned, jnp.concatenate([dq[:, done:], dkv[...]], axis=1)).astype(BF16)
    at = width
    for piece in (table, jnp.broadcast_to(gain_sum, (8, width)), norm_b[...], small_a[...], small_b[...], head[...]):
        g_ref[at : at + piece.shape[0], :] = piece.astype(BF16)
        at += piece.shape[0]
    g_ref[at:, :] = jnp.zeros((g_ref.shape[0] - at, width), BF16)
    reduce.own().start()
    reduce.start(0)

    @pl.when(jnp.logical_not(place.moves))
    def _():
        tg_out[...] = tg[...]
        ex_out[...] = expert[...]

    def turn_round():
        reduce.finish(top)
        gather.start(top)

    chains = [
        [reduce.act(phase) for phase in range(top)] + [turn_round] + [gather.act(phase) for phase in range(top, -1, -1)],
        [fc1.act(phase) for phase in range(2, -1, -1)],
        [fc2.act(1), fc2.act(0)],
        [early_gather.act(phase) for phase in range(early_gather.first, -1, -1)],
    ]
    for turn_index in range(max(len(chain) for chain in chains)):
        for chain in chains:
            if turn_index < len(chain):
                chain[turn_index]()

    @pl.when(place.moves)
    def _():
        for copy in swaps:
            copy.wait()


def last(
    n, chips, collective_id, rows_last, rows_early, fc2_rows, fc1_rows, dq, dk, dv, dk_done, dv_done, n1, h, dh2, w, gain, aux,
    expert, norm_b, small_a, small_b, head, fc2, fc1, early,
):
    rows, width = dq.shape
    devices = 2 * n * chips
    sizes = sum_sizes(n, chips)
    direct = direct_sizes(n, chips) if last_axes(n, chips) is DirectAxes else sizes
    half = lambda height: jax.ShapeDtypeStruct((height, width), BF16)
    return run(
        functools.partial(last_kernel, n, chips),
        "last",
        collective_id,
        [n1, dq, fc2, fc1, early, (dk, 0), (dv, 0), (w, 0), dk_done, dv_done, h, dh2],
        [dk, dv, gain, aux, expert, norm_b, small_a, small_b, head],
        [ANY, ANY] + [VMEM] * 7,
        [half(rows), jax.ShapeDtypeStruct((8, rows), F32)] + [half(height) for height in (fc2_rows, fc1_rows, rows_early, rows_last)],
        [VMEM, VMEM, ANY, ANY, ANY, ANY],
        [
            pltpu.VMEM((rows, width), BF16),
            pltpu.VMEM((rows_last, width), BF16),
            pltpu.VMEM((rows_last // devices, width), BF16),
            pltpu.VMEM((rows_early // devices, width), BF16),
        ]
        + key_scratch(n, rows, LANES)
        + [pltpu.SemaphoreType.DMA((3,))] * 2
        + gather_scratch(sizes, 1, 0)
        + gather_scratch(sizes, 3, 0)
        + reduce_scratch(sizes, rows_early, 2, 3, width)
        + gather_scratch(direct, len(direct) - 1, 0)
        + reduce_scratch(direct, rows_last, 0, len(direct) - 1, width)
        + gather_scratch(direct, len(direct) - 1, 0),
    )


def unpack_kernel(
    fc2_a, fc2_b, fc1_a, fc1_b, out_a, out_b, first_a, second_a, third_a, q_b, k_b, v_b, small, prior, tg_in, expert_in,
    fc2, fc1, out, qkv, tg, expert, lead_average, norm1, norm2, bias, table, final, head, head_bias,
):
    layer, step = pl.program_id(0), pl.program_id(1)

    def layer_part(own, sources):
        @pl.when(layer == own)
        def _():
            for source, target, at in sources:
                target[0, :, at] = source[...].astype(F32)
            for source_rows, at in turned:
                fc1[0, :, at] = (fc1_a, fc1_b)[own][source_rows, :].astype(F32)

    width = table.shape[1]
    everything = slice(0, width)
    turned = [(slice(i * width, (i + 1) * width), slice(i * width, (i + 1) * width)) for i in range(fc1.shape[2] // width)]
    layer_part(0, [(fc2_a, fc2, everything), (out_a, out, everything)])
    layer_part(1, [(fc2_b, fc2, everything), (out_b, out, everything)])
    thirds = [slice(i * width, (i + 1) * width) for i in range(3)]

    @pl.when(layer == 0)
    def _():
        for pair, source in enumerate((first_a, second_a, third_a)):
            for part in range(3):
                at = part * width + pair * LANES
                qkv[0, :, at : at + LANES] = source[:, part * LANES : (part + 1) * LANES].astype(F32)


    @pl.when(layer == 1)
    def _():
        for source, at in zip((q_b, k_b, v_b), thirds):
            qkv[0, :, at] = source[...].astype(F32)

    tg[...] = tg_in[...]

    @pl.when(jnp.logical_and(layer == 0, step == 0))
    def _():
        rows = small[...].astype(F32)
        for i in range(EXPERTS):
            expert[i] = expert_in[i : i + 1, :]
        table[...] = rows[:LEADS]
        for own in range(2):
            norm1[own : own + 1, :] = rows[ROW_NORM1 + 8 * own : ROW_NORM1 + 8 * own + 1]
            base = ROW_MLP + 8 * own
            norm2[own : own + 1, :] = rows[base : base + 1]
            for part in range(bias.shape[1] // width):
                bias[own : own + 1, part * width : (part + 1) * width] = rows[base + 4 + part : base + 5 + part]
        final[...] = rows[ROW_MLP + 9].reshape(final.shape)
        head[...] = rows[ROW_HEAD : ROW_HEAD + EXPERTS]
        totals = rows[ROW_HEAD + 8 : ROW_HEAD + 16, 0:LEADS]
        means = totals[0:EXPERTS] / jnp.maximum(totals[EXPERTS : EXPERTS + 1], 1.0)
        lead_average[...] = 0.5 * prior[...] + 0.5 * means
        column = rows[ROW_HEAD + 16 : ROW_HEAD + 24, 0:LANES]
        head_bias[...] = column_sum(jnp.where(diagonal((8, LANES)), column, 0.0))[:, 0:EXPERTS]


def unpack(fc2_a, fc2_b, fc1_a, fc1_b, early_a, last_a, qkv_b, prior, token_grad, expert, hidden):
    rows, width = token_grad.shape
    steps = 2
    slab, tall = width // steps, hidden // steps

    def at(own, block, first):
        start = first // block
        if own == 0:
            return pl.BlockSpec((block, width), lambda l, j: (start + jnp.where(l == 0, j, steps - 1), 0))
        return pl.BlockSpec((block, width), lambda l, j: (start + jnp.where(l == 1, j, 0), 0))

    fixed = lambda shape: pl.BlockSpec(shape, lambda l, j: (0,) * len(shape))
    moving = pl.BlockSpec((rows // (2 * steps), width), lambda l, j: (l * steps + j, 0))
    in_specs = [at(own, tall, 0) for _ in range(2) for own in range(2)]
    in_specs += [at(0, slab, hidden), at(1, slab, 3 * width)]
    in_specs += [at(0, slab, 0), at(0, slab, width), at(0, slab, 0)]
    in_specs += [at(1, slab, part * width) for part in range(3)]
    in_specs += [pl.BlockSpec((SMALL_ROWS, width), lambda l, j: (width // SMALL_ROWS, 0)), fixed(prior.shape), moving]
    in_specs += [fixed(expert.shape)]
    small_shapes = [
        (EXPERTS, 1, rows), prior.shape, (2, width), (2, width), (2, hidden), (LEADS, width), (width,),
        (EXPERTS, width), (1, EXPERTS),
    ]
    shapes = [(2, hidden, width), (2, width, hidden), (2, width, width), (2, width, 3 * width)]
    out_specs = [
        pl.BlockSpec((1, tall, width), lambda l, j: (l, j, 0)),
        pl.BlockSpec((1, width, tall), lambda l, j: (l, 0, j)),
        pl.BlockSpec((1, slab, width), lambda l, j: (l, j, 0)),
        pl.BlockSpec((1, slab, 3 * width), lambda l, j: (l, j, 0)),
        moving,
    ] + [fixed(shape) for shape in small_shapes]
    return pl.pallas_call(
        unpack_kernel,
        grid=(2, steps),
        out_shape=[jax.ShapeDtypeStruct(shape, F32) for shape in shapes]
        + [jax.ShapeDtypeStruct((rows, width), BF16)]
        + [jax.ShapeDtypeStruct(shape, F32) for shape in small_shapes],
        in_specs=in_specs,
        out_specs=out_specs,
        compiler_params=params(),
        name="unpack",
    )(*([fc2_a, fc2_b, fc1_a, fc1_b, fc1_a, qkv_b] + [early_a, early_a, last_a] + [qkv_b] * 3 + [last_a, prior, token_grad, expert]))


def on_device(
    tokens, slot_kind, frame_lead, norm1_gain, w_qkv, w_out, norm2_gain, w_fc1, b_fc1, w_fc2,
    lead_table, final_gain, head_w, head_b, lead_prior, gate_cot,
):
    rows, width = tokens.shape[0], tokens.shape[3]
    hidden = w_fc1.shape[2]
    n, devices = lax.axis_size("blk"), lax.axis_size("blk") * lax.axis_size("dp")
    chips = lax.axis_size("dp") // 2
    pad = lambda count: -(-count // (16 * devices)) * 16 * devices
    fc_rows, fc1_rows = pad(hidden), pad(hidden + width)
    rows_b, rows_early, rows_last = pad(4 * width), pad((width // LANES - 1) * width), pad(width + SMALL_ROWS)
    flat = lambda x: x.reshape(n * rows, width)
    split = lambda x: x.reshape(n, rows, width)

    h, n1, q, k, v, aux = project(
        n, 0, tokens.reshape(rows, width), gate_cot.reshape(EXPERTS, 1, rows), slot_kind, frame_lead.reshape(1, 2),
        lead_table, norm1_gain, w_qkv,
    )
    k, v = flat(k), flat(v)
    e, ob, li = attend(q, k, v, aux)
    h2, n2, a, gp, h3, n1b, qb, kb, vb = middle(
        n, 1, h, ob, w_out, norm2_gain, w_fc1, b_fc1, w_fc2, norm1_gain, w_qkv
    )
    kb, vb = flat(kb), flat(vb)
    eb, obb, lib = attend(qb, kb, vb, aux)
    g_fc2_b, g_fc1_b, small_b, dh2, do, dl, expert, head, out_b = turn(
        h3, obb, lib, aux, w_out, norm2_gain, w_fc1, b_fc1, w_fc2,
        final_gain, head_w.T, head_b[None], lead_prior.T, fc_rows,
    )
    dq, dk, dv, _, fc2, fc1 = attend_back(
        n, chips, 2, qb, kb, vb, eb, do, dl,
        [
            Task(True, fc_rows, (0, 1, 2, 3), (3.5, 12.0, 17.8, 23.6), g_fc2_b),
            Task(False, fc_rows, (3,), (29.4,)),
            Task(True, fc_rows, (0, 1, 2, 3), (4.9, 14.7, 20.7, 26.7), g_fc1_b, begin=2.2),
        ],
    )
    norm_b, small_a, g_fc1_a, dh2, do, dl, g_fc2_b, g_fc1_b, qkv_part, fc2 = between(
        n, chips, 3, (fc_rows, fc_rows, rows_b, fc_rows, fc1_rows), dq, split(dk), split(dv), n1b, h3, dh2, w_qkv, norm1_gain,
        gp, h2, ob, li, n2, a, w_out, norm2_gain, w_fc1, w_fc2, out_b, fc2, fc1,
    )
    dq, dk, dv, dk_done, dv_done, early, fc1, _, fc2, _, g_qkv_b = attend_back(
        n, chips, 4, q, k, v, e, do, dl,
        [
            Task(True, fc1_rows, (0, 1, 2, 3), (4.9, 14.7, 21.8, 29.4), g_fc1_a),
            Task(True, fc_rows, (2, 3), (8.0, 13.1), fc2),
            Task(False, fc_rows, (3, 2), (20.5, 29.4)),
            Task(True, rows_b, (3,), (6.0,), qkv_part),
            Task(False, rows_b, (3, 2, 1, 0), (12.6, 18.3, 25.6, 29.4)),
        ],
        Early(n1, rows_early, (13.1, 22.9, 25.6, 29.4)),
    )
    part = lambda x: x.reshape(n, rows, LANES)
    token_grad, expert, g_fc2_a, g_fc1_a, g_early, g_last = last(
        n, chips, 5, rows_last, rows_early, fc_rows, fc1_rows, dq, part(dk), part(dv), dk_done, dv_done, n1, h, dh2, w_qkv,
        norm1_gain, aux, expert, norm_b, small_a, small_b, head, fc2, fc1, early,
    )
    fc2, fc1, out, qkv, token_grad, expert, lead_average, norm1, norm2, bias, table, final, head, head_bias = unpack(
        g_fc2_a, g_fc2_b, g_fc1_a, g_fc1_b, g_early, g_last, g_qkv_b, lead_prior.T, token_grad, expert, hidden
    )
    return (
        expert.reshape(EXPERTS, rows, 1, 1),
        lead_average.T,
        token_grad.reshape(rows, 1, 1, width),
        norm1,
        qkv,
        out,
        norm2,
        fc1,
        bias,
        fc2,
        table,
        final,
        head.T,
        head_bias.reshape(-1),
    )


def solution(mesh):
    return jax.shard_map(
        on_device,
        mesh=mesh,
        in_specs=(P("blk", "dp", None, None), P("dp", None), P("dp", None, None))
        + (P(),) * 12
        + (P(None, "blk", "dp", None),),
        out_specs=(P(None, "blk", "dp", None), P(), P("blk", "dp", None, None)) + (P(),) * 11,
        check_vma=False,
    )
```
